32 devices in a mesh: dp: 4 (over y, core), fsdp: 8 (over z, x).
Axes of the slice: x: 2, y: 2, z: 4, core: 2. Of those that a mesh axis runs over, the one named last changes fastest.
Arguments:
- acts: bfloat16 [4096, 8192], P(('dp', 'fsdp')), may hold values from -3 to 3
- out_grads: bfloat16 [4096, 8192], P(('dp', 'fsdp')), may hold values from -6 to 6
- token_counts: int32 [4], replicated, may hold values from 512 to 1024, as said below
- k_factor: float32 [32, 256, 512], P('fsdp'), may hold values from -0.1875 to 2.44
- c_factor: float32 [32, 256, 512], P('fsdp'), may hold values from -0.1875 to 2.44
- k_moment: float32 [32, 256, 512], P('fsdp'), may hold values from -0.046875 to 0.946875
- c_moment: float32 [32, 256, 512], P('fsdp'), may hold values from -0.046875 to 0.946875
- grad_weight: bfloat16 [8192, 8192], P('dp', 'fsdp'), may hold values from -6 to 6
Outputs:
- k_factor_new: float32 [32, 256, 512], P('fsdp')
- c_factor_new: float32 [32, 256, 512], P('fsdp')
- k_moment_new: float32 [32, 256, 512], P('fsdp')
- c_moment_new: float32 [32, 256, 512], P('fsdp')
- precond: bfloat16 [8192, 8192], P('dp', 'fsdp')
The draws below stay inside these ranges and needn't reach their ends.
Inputs may be any that keep to these rules, and one draw needn't show every extreme that they name: `token_counts`: some data group has all 1024 slots valid and some other has exactly 512.
All inputs are finite; a program needn't handle non-finite values.
Results may differ from the reference program's by a relative error of at most 0.0081.
Values may be sent and summed in bfloat16 or wider, within the bound.
No kernel may reach another device: no remote copies, remote signals or barrier semaphores. Data moves between devices by JAX's collectives and lax.ppermute only.
A program may use at most 128 MiB of HBM per device.

```python
import math
import jax
import jax.numpy as jnp
from jax import lax

D = 8192
BS = 256
NB = 32
GROUP_TOK = 1024
TOKENS = 4096
N_DP = 4


def clipped_normal(key, shape):
    return jnp.clip(jax.random.normal(key, shape, jnp.float32), -4.0, 4.0)


def factor_draw(key):
    keys = jax.random.split(key, 4)
    shape = (NB, BS, BS)
    noise = clipped_normal(keys[0], shape)
    side = clipped_normal(keys[1], shape)
    scales = jnp.exp(jax.random.uniform(keys[2], (NB, 1, 1), jnp.float32, math.log(0.5), math.log(1.5)))
    rough = jnp.exp(jax.random.uniform(keys[3], (NB, 1, BS), jnp.float32, math.log(0.6), math.log(1.4)))
    identity = jnp.eye(BS, dtype=jnp.float32)
    blocks = scales * (identity * rough + noise * (0.5 / math.sqrt(BS)))
    border = side * (0.35 / math.sqrt(BS))
    return jnp.concatenate([blocks, border], axis=-1)


def moment_draw(key):
    keys = jax.random.split(key, 3)
    shape = (NB, BS, BS)
    noise = clipped_normal(keys[0], shape)
    side = clipped_normal(keys[1], shape)
    level = jax.random.uniform(keys[2], (NB, 1, BS), jnp.float32, 0.1, 0.9)
    identity = jnp.eye(BS, dtype=jnp.float32)
    blocks = identity * level + noise * (3.0 / BS)
    border = side * (2.0 / BS)
    return jnp.concatenate([blocks, border], axis=-1)


def draw_token_counts(key, part):
    keys = jax.random.split(jax.random.fold_in(key, 71), 2)
    counts = jax.random.randint(keys[0], (N_DP,), GROUP_TOK // 2, GROUP_TOK + 1)
    order = jax.random.permutation(keys[1], N_DP)
    counts = jnp.where(order == 0, GROUP_TOK, counts)
    counts = jnp.where(order == 1, GROUP_TOK // 2, counts)
    return counts.astype(jnp.int32)


def draw_k_factor(key, part):
    return factor_draw(jax.random.fold_in(key, 17))


def draw_c_factor(key, part):
    return factor_draw(jax.random.fold_in(key, 29))


def draw_k_moment(key, part):
    return moment_draw(jax.random.fold_in(key, 41))


def draw_c_moment(key, part):
    return moment_draw(jax.random.fold_in(key, 53))


def level_of(key, extent, cuts, low, top_value):
    gain, own = 1.0, jax.random.fold_in(key, 6)
    for axis_at, shards_of in cuts:
        steps = jnp.exp(jax.random.uniform(jax.random.fold_in(own, axis_at), (shards_of,), jnp.float32, low / len(cuts), top_value / len(cuts)))
        gain = gain * jnp.repeat(steps, extent[axis_at] // shards_of).reshape([-1 if axis == axis_at else 1 for axis in range(len(extent))])
    return gain


def gaussian(rng, dims, deviation, limit, cuts=(), kind=jnp.bfloat16):
    result = jax.random.normal(rng, dims, jnp.float32) * deviation
    if len(cuts) > 0:
        result = level_of(rng, dims, cuts, -0.22, 0.18) * result
    return jnp.clip(result, min=-limit, max=limit).astype(kind)


def setup_inputs(seed: int = 0) -> dict:
    seeds = jax.random.split(jax.random.key(seed), 9)
    acts = gaussian(seeds[0], (TOKENS, D), 0.5, 3.0, ((0, 32),))
    out_grads = gaussian(seeds[1], (TOKENS, D), 1.0, 6.0, ((0, 32),))
    token_counts = draw_token_counts(jax.random.fold_in(seeds[8], 71), 0)
    k_factor = draw_k_factor(jax.random.fold_in(seeds[8], 71), 0)
    c_factor = draw_c_factor(jax.random.fold_in(seeds[8], 71), 0)
    k_moment = draw_k_moment(jax.random.fold_in(seeds[8], 71), 0)
    c_moment = draw_c_moment(jax.random.fold_in(seeds[8], 71), 0)
    grad_weight = gaussian(seeds[7], (D, D), 1.0, 6.0, ((0, 4), (1, 8)))
    return dict(acts=acts, out_grads=out_grads, token_counts=token_counts, k_factor=k_factor, c_factor=c_factor, k_moment=k_moment, c_moment=c_moment, grad_weight=grad_weight)


damping = 0.1
momentum_rate = 0.5
step_rate = 0.2
highest = lax.Precision.HIGHEST


def statistics(masked, factor, border_keep, token_total):
    diag_half = factor[:, :, :BS].astype(jnp.bfloat16)
    side_half = (factor[:, :, BS:] * border_keep).astype(jnp.bfloat16)
    lead_columns = masked[:, :BS]
    lead_image = jnp.dot(lead_columns, diag_half[0], preferred_element_type=jnp.float32).astype(jnp.bfloat16)

    def one_block(block_index):
        columns = lax.dynamic_slice_in_dim(masked, block_index * BS, BS, 1)
        image_sum = jnp.dot(columns, diag_half[block_index], preferred_element_type=jnp.float32)
        image_sum = image_sum + jnp.dot(lead_columns, side_half[block_index], preferred_element_type=jnp.float32)
        image_block = image_sum.astype(jnp.bfloat16)
        own_sum = jnp.dot(image_block.T, image_block, preferred_element_type=jnp.float32) / token_total
        cross_sum = jnp.dot(lead_image.T, image_block, preferred_element_type=jnp.float32) / token_total
        return own_sum, cross_sum

    return lax.map(one_block, jnp.arange(NB, dtype=jnp.int32))


def gram_trace(factor, border_keep):
    diag_part = factor[:, :, :BS]
    side_part = factor[:, :, BS:] * border_keep
    return jnp.sum(diag_part * diag_part) + jnp.sum(side_part * side_part)


def advance(factor, moment, own_sum, cross_sum, lead_block, border_keep, other_h, other_g, width):
    diag_part = factor[:, :, :BS]
    side_part = factor[:, :, BS:] * border_keep
    gram_diag = jnp.einsum("nki,nkj->nij", diag_part, diag_part, precision=highest)
    gram_diag = gram_diag + jnp.einsum("nki,nkj->nij", side_part, side_part, precision=highest)
    gram_side = jnp.einsum("ki,nkj->nij", lead_block, side_part, precision=highest)
    identity = jnp.eye(BS, dtype=jnp.float32)
    fresh_diag = (other_h * own_sum + damping * other_g * gram_diag - width * identity) / (2.0 * width)
    fresh_side = (other_h * cross_sum + damping * other_g * gram_side) * border_keep / (2.0 * width)
    moment_diag = momentum_rate * moment[:, :, :BS] + fresh_diag
    moment_side = (momentum_rate * moment[:, :, BS:] + fresh_side) * border_keep
    new_diag = diag_part - step_rate * jnp.einsum("nik,nkj->nij", diag_part, moment_diag, precision=highest)
    side_change = jnp.einsum("ik,nkj->nij", lead_block, moment_side, precision=highest)
    side_change = side_change + jnp.einsum("nik,nkj->nij", side_part, moment_diag, precision=highest)
    new_side = (side_part - step_rate * side_change) * border_keep
    return jnp.concatenate([new_diag, new_side], axis=-1), jnp.concatenate([moment_diag, moment_side], axis=-1)


def precondition(grad_weight, k_new, c_new):
    k_diag = k_new[:, :, :BS].astype(jnp.bfloat16)
    k_side = k_new[:, :, BS:].astype(jnp.bfloat16)
    c_diag = c_new[:, :, :BS].astype(jnp.bfloat16)
    c_side = c_new[:, :, BS:].astype(jnp.bfloat16)
    block_range = jnp.arange(NB, dtype=jnp.int32)
    lead_columns = grad_weight[:, :BS]

    def first_block(block_index):
        columns = lax.dynamic_slice_in_dim(grad_weight, block_index * BS, BS, 1)
        total_sum = jnp.dot(columns, k_diag[block_index], preferred_element_type=jnp.float32)
        total_sum = total_sum + jnp.dot(lead_columns, k_side[block_index], preferred_element_type=jnp.float32)
        return total_sum.astype(jnp.bfloat16)

    first_product = lax.map(first_block, block_range)

    def second_block(block_index):
        return jnp.dot(first_product[block_index], k_diag[block_index].T, preferred_element_type=jnp.float32)

    own_second = lax.map(second_block, block_range)

    def add_lead(carry, block_index):
        return carry + jnp.dot(first_product[block_index], k_side[block_index].T, preferred_element_type=jnp.float32), None

    lead_term, unused = lax.scan(add_lead, jnp.zeros((D, BS), jnp.float32), block_range)
    second_product = own_second.at[0].add(lead_term).astype(jnp.bfloat16)
    by_rows = second_product.transpose(1, 0, 2).reshape(D, D).reshape(NB, BS, D)
    lead_rows = by_rows[0]

    def third_block(block_index):
        total_sum = jnp.dot(c_diag[block_index].T, by_rows[block_index], preferred_element_type=jnp.float32)
        total_sum = total_sum + jnp.dot(c_side[block_index].T, lead_rows, preferred_element_type=jnp.float32)
        return total_sum.astype(jnp.bfloat16)

    third_product = lax.map(third_block, block_range)

    def fourth_block(block_index):
        return jnp.dot(c_diag[block_index], third_product[block_index], preferred_element_type=jnp.float32)

    own_fourth = lax.map(fourth_block, block_range)

    def add_row(carry, block_index):
        return carry + jnp.dot(c_side[block_index], third_product[block_index], preferred_element_type=jnp.float32), None

    row_term, unused_rows = lax.scan(add_row, jnp.zeros((BS, D), jnp.float32), block_range)
    return own_fourth.at[0].add(row_term).astype(jnp.bfloat16).reshape(D, D)


def reference(acts, out_grads, token_counts, k_factor, c_factor, k_moment, c_moment, grad_weight):
    row_ids = jnp.arange(acts.shape[0], dtype=jnp.int32)
    group_of = row_ids // GROUP_TOK
    slot_of = row_ids % GROUP_TOK
    row_keep = (slot_of < token_counts[group_of]).astype(jnp.bfloat16)[:, None]
    masked_acts = acts * row_keep
    masked_grads = out_grads * row_keep
    token_total = jnp.sum(token_counts).astype(jnp.float32)
    border_keep = (jnp.arange(NB, dtype=jnp.int32) > 0).astype(jnp.float32)[:, None, None]
    own_k, cross_k = statistics(masked_acts, k_factor, border_keep, token_total)
    own_c, cross_c = statistics(masked_grads, c_factor, border_keep, token_total)
    trace_hk = jnp.sum(jnp.trace(own_k, axis1=1, axis2=2))
    trace_hc = jnp.sum(jnp.trace(own_c, axis1=1, axis2=2))
    trace_gk = gram_trace(k_factor, border_keep)
    trace_gc = gram_trace(c_factor, border_keep)
    width = float(D)
    k_factor_new, k_moment_new = advance(k_factor, k_moment, own_k, cross_k, k_factor[0, :, :BS], border_keep, trace_hc, trace_gc, width)
    c_factor_new, c_moment_new = advance(c_factor, c_moment, own_c, cross_c, c_factor[0, :, :BS], border_keep, trace_hk, trace_gk, width)
    precond = precondition(grad_weight, k_factor_new, c_factor_new)
    return (k_factor_new, c_factor_new, k_moment_new, c_moment_new, precond)
```

```python
import functools

import jax
import jax.numpy as jnp
from jax import lax
from jax.experimental import pallas as pl
from jax.experimental.pallas import tpu as pltpu
from jax.sharding import PartitionSpec as P

damping = 0.1
momentum_rate = 0.5
step_rate = 0.2
highest = lax.Precision.HIGHEST
both = ("dp", "fsdp")
f32 = jnp.float32
bf16 = jnp.bfloat16
vmem_cap = 48 * 1024 * 1024


def params(*semantics):
    return pltpu.CompilerParams(dimension_semantics=semantics, vmem_limit_bytes=vmem_cap)


def dot(a, b, dims=((1,), (0,)), precision=None):
    return lax.dot_general(a, b, (dims, ((), ())), precision=precision, preferred_element_type=f32)


nn = ((1,), (0,))
tn = ((0,), (0,))
nt = ((1,), (1,))


def pack_body(zs, xs, ds, bs, tile, lim_ref, a_ref, o_ref):
    rows = pl.program_id(0) * tile + lax.broadcasted_iota(jnp.int32, (tile, bs), 0)
    keep = jnp.where(rows < lim_ref[0], 1.0, 0.0).astype(bf16)
    lead = a_ref[:, :bs] * keep
    for d in range(ds):
        for x in range(xs):
            for z in range(zs):
                n = (z * xs + x) * ds + d
                o_ref[d * xs + x, z] = a_ref[:, n * bs : (n + 1) * bs] * keep
            o_ref[d * xs + x, zs] = lead


def pack(limit, tokens, zs, xs, ds, bs):
    count, width = tokens.shape
    tile = 32
    return pl.pallas_call(
        functools.partial(pack_body, zs, xs, ds, bs, tile),
        grid=(count // tile,),
        in_specs=[
            pl.BlockSpec(memory_space=pltpu.SMEM),
            pl.BlockSpec((tile, width), lambda i: (i, 0)),
        ],
        out_specs=pl.BlockSpec((ds * xs, zs + 1, tile, bs), lambda i: (0, 0, i, 0)),
        out_shape=jax.ShapeDtypeStruct((ds * xs, zs + 1, count, bs), bf16),
        compiler_params=params("arbitrary"),
        name="pack_tokens",
    )(limit, tokens)


def moments_body(ids_ref, x_ref, l_ref, o_ref):
    groups, _, count, bs = x_ref.shape
    cols = x_ref[:, 0].reshape(groups * count, bs)
    lead = l_ref[:, 0].reshape(groups * count, bs)
    o_ref[0, 0] = dot(cols, cols, tn).astype(bf16)
    o_ref[0, 1] = dot(lead, cols, tn).astype(bf16)
    o_ref[0, 2] = dot(lead, lead, tn).astype(bf16)


def raw_moments(ids, owned):
    groups, slots, count, bs = owned.shape
    zs = slots - 1
    return pl.pallas_call(
        moments_body,
        grid_spec=pltpu.PrefetchScalarGridSpec(
            num_scalar_prefetch=1,
            grid=(zs,),
            in_specs=[
                pl.BlockSpec((groups, 1, count, bs), lambda k, ids: (0, ids[0] ^ k, 0, 0)),
                pl.BlockSpec((groups, 1, count, bs), lambda k, ids: (0, zs, 0, 0)),
            ],
            out_specs=pl.BlockSpec((1, 3, bs, bs), lambda k, ids: (k, 0, 0, 0)),
        ),
        out_shape=jax.ShapeDtypeStruct((zs, 3, bs, bs), bf16),
        compiler_params=params("arbitrary"),
        name="raw_moments",
    )(ids, owned, owned)


def image_stats_body(count, ids_ref, sc_ref, *refs):
    parts = refs[:count]
    fac_ref, lead_ref, h_ref, hb_ref, tr_ref = refs[count:]
    bs = lead_ref.shape[0]
    keep = sc_ref[1]
    total = parts[0][...].astype(f32)
    for part in parts[1:]:
        total = total + part[...].astype(f32)
    fac = fac_ref[0]
    diag = fac[:, :bs]
    side = fac[:, bs:] * keep
    gram = jnp.sum(diag * diag) + jnp.sum(side * side)
    bn = diag.astype(bf16).astype(f32)
    pn = side.astype(bf16).astype(f32)
    b0 = lead_ref[...].astype(f32)
    mm = functools.partial(dot, precision=highest)
    t1 = mm(total[0], bn) + mm(total[1], pn, tn)
    t0 = mm(total[1], bn) + mm(total[2], pn)
    own = (mm(bn, t1, tn) + mm(pn, t0, tn)) * sc_ref[0]
    cross = mm(b0, t0, tn) * sc_ref[0]
    h_ref[0] = own
    h_ref[1] = cross
    hb_ref[0] = own.astype(bf16)
    hb_ref[1] = cross.astype(bf16)
    row = lax.broadcasted_iota(jnp.int32, (bs, bs), 0)
    col = lax.broadcasted_iota(jnp.int32, (bs, bs), 1)
    trace = jnp.sum(jnp.where(row == col, own, 0.0))
    top = lax.broadcasted_iota(jnp.int32, (8, 128), 0)
    tr_ref[...] = jnp.where(top == 0, trace, gram)


def image_stats(ids, scalars, parts, factor, lead):
    bs = lead.shape[0]
    whole = lambda shape: pl.BlockSpec(shape, lambda i, ids: (0,) * len(shape))
    return pl.pallas_call(
        functools.partial(image_stats_body, len(parts)),
        grid_spec=pltpu.PrefetchScalarGridSpec(
            num_scalar_prefetch=1,
            grid=(1,),
            in_specs=[pl.BlockSpec(memory_space=pltpu.SMEM)]
            + [whole((3, bs, bs)) for _ in parts]
            + [pl.BlockSpec((1, bs, 2 * bs), lambda i, ids: (ids[1], 0, 0)), whole((bs, bs))],
            out_specs=[whole((2, bs, bs)), whole((2, bs, bs)), whole((8, 128))],
        ),
        out_shape=[
            jax.ShapeDtypeStruct((2, bs, bs), f32),
            jax.ShapeDtypeStruct((2, bs, bs), bf16),
            jax.ShapeDtypeStruct((8, 128), f32),
        ],
        compiler_params=params("arbitrary"),
        name="image_stats",
    )(ids, scalars, *parts, factor, lead)


def advance_block(width, own, cross, fac, mom, b0, other_h, other_g, keep):
    bs = fac.shape[0]
    diag = fac[:, :bs]
    side = fac[:, bs:] * keep
    db = diag.astype(bf16)
    sb = side.astype(bf16)
    gram_d = dot(db, db, tn) + dot(sb, sb, tn)
    gram_s = dot(b0, sb, tn)
    row = lax.broadcasted_iota(jnp.int32, (bs, bs), 0)
    col = lax.broadcasted_iota(jnp.int32, (bs, bs), 1)
    ident = jnp.where(row == col, width, 0.0)
    scale = 1.0 / (2.0 * width)
    md = momentum_rate * mom[:, :bs] + (other_h * own + damping * other_g * gram_d - ident) * scale
    ms = momentum_rate * mom[:, bs:] + (other_h * cross + damping * other_g * gram_s) * scale
    ms = ms * keep
    mdb = md.astype(bf16)
    new_d = diag - step_rate * dot(db, mdb)
    new_s = side - step_rate * (dot(b0, ms.astype(bf16)) + dot(sb, mdb)) * keep
    return md, ms, new_d, new_s


def order_of(ids, m):
    return ids[1] ^ ((m & 1) * 2 + (m >> 1))


def advance_body(width, ids_ref, sc_ref, h_ref, fac_ref, mom_ref, lead_ref, fn_ref, mn_ref, fb_ref):
    blocks = lead_ref.shape[0]
    bs = lead_ref.shape[0]
    j = order_of(ids_ref, pl.program_id(0))
    keep = jnp.where(ids_ref[2] + j > 0, 1.0, 0.0)
    md, ms, new_d, new_s = advance_block(
        width,
        h_ref[0, 0].astype(f32),
        h_ref[0, 1].astype(f32),
        fac_ref[0],
        mom_ref[0],
        lead_ref[...],
        sc_ref[0],
        sc_ref[1],
        keep,
    )
    fn_ref[0, :, :bs] = new_d
    fn_ref[0, :, bs:] = new_s
    mn_ref[0, :, :bs] = md
    mn_ref[0, :, bs:] = ms
    fb_ref[0, :, :bs] = new_d.astype(bf16)
    fb_ref[0, :, bs:] = new_s.astype(bf16)


def advance_all(width, ids, scalars, stats, factor, moment, lead):
    blocks, bs, wide = factor.shape
    spec = pl.BlockSpec((1, bs, wide), lambda m, ids: (order_of(ids, m), 0, 0))
    return pl.pallas_call(
        functools.partial(advance_body, width),
        grid_spec=pltpu.PrefetchScalarGridSpec(
            num_scalar_prefetch=1,
            grid=(blocks,),
            in_specs=[
                pl.BlockSpec(memory_space=pltpu.SMEM),
                pl.BlockSpec((1, 2, bs, bs), lambda m, ids: (m, 0, 0, 0)),
                spec,
                spec,
                pl.BlockSpec((bs, bs), lambda m, ids: (0, 0)),
            ],
            out_specs=[spec, spec, spec],
        ),
        out_shape=[
            jax.ShapeDtypeStruct(factor.shape, f32),
            jax.ShapeDtypeStruct(factor.shape, f32),
            jax.ShapeDtypeStruct(factor.shape, bf16),
        ],
        compiler_params=params("arbitrary"),
        name="advance_all",
    )(ids, scalars, stats, factor, moment, lead)


def advance_one_body(width, ids_ref, sc_ref, h_ref, fac_ref, mom_ref, lead_ref, fb_ref):
    bs = lead_ref.shape[0]
    keep = jnp.where(ids_ref[2] + ids_ref[1] > 0, 1.0, 0.0)
    _, _, new_d, new_s = advance_block(
        width, h_ref[0], h_ref[1], fac_ref[0], mom_ref[0], lead_ref[...], sc_ref[0], sc_ref[1], keep
    )
    fb_ref[:, :bs] = new_d.astype(bf16)
    fb_ref[:, bs:] = new_s.astype(bf16)


def advance_one(width, ids, scalars, stats, factor, moment, lead):
    blocks, bs, wide = factor.shape
    spec = pl.BlockSpec((1, bs, wide), lambda i, ids: (ids[1], 0, 0))
    return pl.pallas_call(
        functools.partial(advance_one_body, width),
        grid_spec=pltpu.PrefetchScalarGridSpec(
            num_scalar_prefetch=1,
            grid=(1,),
            in_specs=[
                pl.BlockSpec(memory_space=pltpu.SMEM),
                pl.BlockSpec((2, bs, bs), lambda i, ids: (0, 0, 0)),
                spec,
                spec,
                pl.BlockSpec((bs, bs), lambda i, ids: (0, 0)),
            ],
            out_specs=pl.BlockSpec((bs, wide), lambda i, ids: (0, 0)),
        ),
        out_shape=jax.ShapeDtypeStruct((bs, wide), bf16),
        compiler_params=params("arbitrary"),
        name="advance_one",
    )(ids, scalars, stats, factor, moment, lead)


def columns_body(ids_ref, g_ref, l_ref, k_ref, s_ref, t_ref):
    blocks, bs, _ = k_ref.shape
    lead = l_ref[...]
    term = None
    for n in range(blocks):
        kd = k_ref[n, :, :bs]
        ks = k_ref[n, :, bs:]
        first = (dot(g_ref[:, n * bs : (n + 1) * bs], kd) + dot(lead, ks)).astype(bf16)
        second = dot(first, kd, nt)
        s_ref[:, n * bs : (n + 1) * bs] = second.astype(bf16)
        part = dot(first, ks, nt)
        if n == 0:
            part = part + second * jnp.where(ids_ref[2] == 0, 1.0, 0.0)
        term = part if term is None else term + part
    t_ref[...] = term.astype(bf16)


def columns(ids, grad, lead, kb):
    rows, wide = grad.shape
    blocks, bs, _ = kb.shape
    tile = 512
    return pl.pallas_call(
        columns_body,
        grid_spec=pltpu.PrefetchScalarGridSpec(
            num_scalar_prefetch=1,
            grid=(rows // tile,),
            in_specs=[
                pl.BlockSpec((tile, wide), lambda i, ids: (i, 0)),
                pl.BlockSpec((tile, bs), lambda i, ids: (i, 0)),
                pl.BlockSpec(kb.shape, lambda i, ids: (0, 0, 0)),
            ],
            out_specs=[
                pl.BlockSpec((tile, wide), lambda i, ids: (i, 0)),
                pl.BlockSpec((tile, bs), lambda i, ids: (i, 0)),
            ],
        ),
        out_shape=[
            jax.ShapeDtypeStruct((rows, wide), bf16),
            jax.ShapeDtypeStruct((rows, bs), bf16),
        ],
        compiler_params=params("arbitrary"),
        name="column_products",
    )(ids, grad, lead, kb)


def row_of(ids, k):
    q = ids[3] ^ k
    return (q & 1) * ids[4] + (q >> 1)


def rows_body(ids_ref, s_ref, l_ref, c_ref, p_ref, u_ref, acc_ref):
    k = pl.program_id(0)
    bs = l_ref.shape[0]
    cd = c_ref[0, :, :bs]
    cs = c_ref[0, :, bs:]
    third = (dot(cd, s_ref[...], tn) + dot(cs, l_ref[...], tn)).astype(bf16)
    fourth = dot(cd, third)
    p_ref[...] = fourth.astype(bf16)
    is_first = (ids_ref[5] == 0) & (row_of(ids_ref, k) == 0)
    term = dot(cs, third) + fourth * jnp.where(is_first, 1.0, 0.0)

    @pl.when(k == 0)
    def _():
        acc_ref[...] = term

    @pl.when(k > 0)
    def _():
        acc_ref[...] = acc_ref[...] + term

    @pl.when(k == pl.num_programs(0) - 1)
    def _():
        u_ref[...] = acc_ref[...].astype(bf16)


def rows(ids, second, lead, cb):
    count, wide = second.shape
    blocks, bs, _ = cb.shape
    spec = pl.BlockSpec((bs, wide), lambda k, ids: (row_of(ids, k), 0))
    whole = pl.BlockSpec((bs, wide), lambda k, ids: (0, 0))
    return pl.pallas_call(
        rows_body,
        grid_spec=pltpu.PrefetchScalarGridSpec(
            num_scalar_prefetch=1,
            grid=(blocks,),
            in_specs=[spec, whole, pl.BlockSpec((1, bs, 2 * bs), lambda k, ids: (k, 0, 0))],
            out_specs=[spec, whole],
            scratch_shapes=[pltpu.VMEM((bs, wide), f32)],
        ),
        out_shape=[
            jax.ShapeDtypeStruct((count, wide), bf16),
            jax.ShapeDtypeStruct((bs, wide), bf16),
        ],
        compiler_params=params("arbitrary"),
        name="row_products",
    )(ids, second, lead, cb)


def planned(acts, out_grads, token_counts, k_factor, c_factor, k_moment, c_moment, grad_weight):
    tok_dev, width = acts.shape
    ds, bs, _ = k_factor.shape
    shards = lax.axis_size("fsdp")
    xs = 2
    zs = shards // xs
    d = lax.axis_index("dp")
    s = lax.axis_index("fsdp")
    x = s % xs
    z = s // xs
    flat = lambda dd, ss: dd * shards + ss
    plane = [[flat(dd, zz * xs + xx) for dd in range(ds) for xx in range(xs)] for zz in range(zs)]
    ids = jnp.stack([z, d, s * ds, s, jnp.int32(ds), d]).astype(jnp.int32)
    token_total = jnp.sum(token_counts).astype(f32)
    valid = jnp.sum(jnp.where(lax.iota(jnp.int32, ds) == d, token_counts, 0))
    limit = (valid - s * tok_dev).reshape(1).astype(jnp.int32)
    keep = jnp.where(s * ds + d > 0, 1.0, 0.0)
    stat_scalars = jnp.stack([1.0 / token_total, keep]).astype(f32)

    def to_all_shards(value):
        over_x = lax.ppermute(value, "fsdp", [(0, 1)])
        value = jnp.where(s == 0, value, over_x)
        got = [
            lax.ppermute(value, "fsdp", [(xx, zz * xs + xx) for xx in range(xs)])
            for zz in range(1, zs)
        ]
        out = got[0]
        for g in got[1:]:
            out = out + g
        return jnp.where(z == 0, value, out)

    leads = jnp.stack([k_factor[0, :, :bs], c_factor[0, :, :bs]]).astype(bf16)
    leads = to_all_shards(leads)
    lead_k, lead_c = leads[0], leads[1]

    def grad_lead_all():
        value = grad_weight[:, :bs]
        half = value.shape[0] // xs
        over_x = lax.ppermute(value[half:], "fsdp", [(0, 1)])
        mine = jnp.where(s == 0, value[:half], over_x)
        got = [
            lax.ppermute(mine, "fsdp", [(xx, zz * xs + xx) for xx in range(xs)])
            for zz in range(1, zs)
        ]
        out = got[0]
        for g in got[1:]:
            out = out + g
        mine = jnp.where(z == 0, mine, out)
        other = lax.ppermute(mine, "fsdp", [(i, i ^ 1) for i in range(shards)])
        low = jnp.where(x == 0, mine, other)
        high = jnp.where(x == 0, other, mine)
        return jnp.concatenate([low, high], axis=0)

    grad_lead = grad_lead_all()

    def side(tokens, factor, lead):
        packed = pack(limit, tokens, zs, xs, ds, bs)
        owned = lax.all_to_all(packed, both, 0, 0, tiled=True, axis_index_groups=plane)
        raw = raw_moments(ids, owned)
        parts = [raw[0]]
        for k in range(1, zs):
            pairs = [(zz * xs + xx, (zz ^ k) * xs + xx) for zz in range(zs) for xx in range(xs)]
            parts.append(lax.ppermute(raw[k], "fsdp", pairs))
        return image_stats(ids, stat_scalars, parts, factor, lead)

    def totals(traces):
        spread = jnp.broadcast_to(traces[None], (ds * shards,) + traces.shape)
        got = lax.all_to_all(spread, both, 0, 0, tiled=True)
        summed = jnp.sum(got, axis=0)
        return summed[:2, 0]

    def over_dp(value):
        pair = jnp.stack([value, lax.ppermute(value, "dp", [(i, i ^ 2) for i in range(ds)])])
        other = lax.ppermute(pair, "dp", [(i, i ^ 1) for i in range(ds)])
        return jnp.concatenate([pair, other], axis=0)

    scale_width = float(width)
    stat_k, stat_kb, trace_k = side(acts, k_factor, lead_k)
    total_k = totals(trace_k)
    all_k = over_dp(stat_kb)
    stat_c, stat_cb, trace_c = side(out_grads, c_factor, lead_c)

    c_block = advance_one(scale_width, ids, total_k, stat_c, c_factor, c_moment, lead_c)
    fetched = []
    for k in range(shards):
        pairs = [
            (flat(dd, zz * xs + xx), flat(zz, (dd * xs + xx) ^ k))
            for dd in range(ds)
            for zz in range(zs)
            for xx in range(xs)
        ]
        fetched.append(lax.ppermute(c_block, both, pairs))
    c_rows = jnp.stack(fetched)

    total_c = totals(trace_c)
    k_factor_new, k_moment_new, kb = advance_all(
        scale_width, ids, total_c, all_k, k_factor, k_moment, lead_k
    )
    second, term = columns(ids, grad_weight, grad_lead, kb)
    count = grad_weight.shape[0]
    by_shard = term.reshape(shards, count // shards, bs)
    got = lax.all_to_all(by_shard, "fsdp", 0, 0, tiled=True)
    block_sum = jnp.sum(got.astype(f32), axis=0).astype(bf16)
    blocks = [block_sum] + [lax.ppermute(block_sum, "fsdp", [(k, 0)]) for k in range(1, shards)]
    lead_cols = jnp.where(s == 0, jnp.concatenate(blocks, axis=0), second[:, :bs])
    second = jnp.concatenate([lead_cols, second[:, bs:]], axis=1)
    top = second[:bs]
    lead_rows = jnp.where(d == 0, top, 0).astype(bf16)
    for k in range(1, ds):
        lead_rows = lead_rows + lax.ppermute(top, "dp", [(0, k)])

    all_c = over_dp(stat_cb)
    c_factor_new, c_moment_new, _ = advance_all(
        scale_width, ids, total_k, all_c, c_factor, c_moment, lead_c
    )
    precond, up = rows(ids, second, lead_rows, c_rows)
    over_y = lax.ppermute(up, "dp", [(2, 0), (3, 1)])
    up_sum = up.astype(f32) + over_y.astype(f32)
    over_core = lax.ppermute(up_sum.astype(bf16), "dp", [(1, 0)])
    up_sum = (up_sum + over_core.astype(f32)).astype(bf16)
    precond = precond.at[:bs].set(jnp.where(d == 0, up_sum, precond[:bs]))
    return (k_factor_new, c_factor_new, k_moment_new, c_moment_new, precond)


def spread(value, axis, source):
    kept = jnp.where(lax.axis_index(axis) == source, value, 0).astype(value.dtype)
    return lax.psum(kept, axis)


def owner_image(columns, lead_columns, diag_half, side_half):
    row_count = columns.shape[0]
    block_count = diag_half.shape[0]
    block_size = diag_half.shape[1]
    blocked = columns.reshape(row_count, block_count, block_size)
    image_sum = jnp.einsum("tnk,nkj->tnj", blocked, diag_half, preferred_element_type=jnp.float32)
    image_sum = image_sum + jnp.einsum(
        "tk,nkj->tnj", lead_columns, side_half, preferred_element_type=jnp.float32
    )
    return image_sum.astype(jnp.bfloat16).reshape(row_count, block_count * block_size)


def to_owners(pair):
    return (
        lax.all_to_all(pair[0], "fsdp", split_axis=1, concat_axis=0, tiled=True),
        lax.all_to_all(pair[1], "fsdp", split_axis=1, concat_axis=0, tiled=True),
    )


def fetch_lead(before):
    return (
        lax.all_gather(before[0], "fsdp", axis=0, tiled=True),
        lax.all_gather(before[1], "fsdp", axis=0, tiled=True),
    )


def block_stats(owned, lead_image, block_count, block_size):
    blocked = owned.reshape(owned.shape[0], block_count, block_size)
    own_sum = jnp.einsum("tni,tnj->nij", blocked, blocked, preferred_element_type=jnp.float32)
    cross_sum = jnp.einsum("ti,tnj->nij", lead_image, blocked, preferred_element_type=jnp.float32)
    return (own_sum, cross_sum)


def gram_trace(factor, border_keep):
    block_size = factor.shape[1]
    diag_part = factor[:, :, :block_size]
    side_part = factor[:, :, block_size:] * border_keep
    return jnp.sum(diag_part * diag_part) + jnp.sum(side_part * side_part)


def advance(factor, moment, own_sum, cross_sum, lead_block, border_keep, other_h, other_g, width):
    block_size = factor.shape[1]
    diag_part = factor[:, :, :block_size]
    side_part = factor[:, :, block_size:] * border_keep
    gram_diag = jnp.einsum("nki,nkj->nij", diag_part, diag_part, precision=highest)
    gram_diag = gram_diag + jnp.einsum("nki,nkj->nij", side_part, side_part, precision=highest)
    gram_side = jnp.einsum("ki,nkj->nij", lead_block, side_part, precision=highest)
    identity = jnp.eye(block_size, dtype=jnp.float32)
    fresh_diag = (other_h * own_sum + damping * other_g * gram_diag - width * identity) / (
        2.0 * width
    )
    fresh_side = (other_h * cross_sum + damping * other_g * gram_side) * border_keep / (2.0 * width)
    moment_diag = momentum_rate * moment[:, :, :block_size] + fresh_diag
    moment_side = (momentum_rate * moment[:, :, block_size:] + fresh_side) * border_keep
    new_diag = diag_part - step_rate * jnp.einsum(
        "nik,nkj->nij", diag_part, moment_diag, precision=highest
    )
    side_change = jnp.einsum("ik,nkj->nij", lead_block, moment_side, precision=highest)
    side_change = side_change + jnp.einsum(
        "nik,nkj->nij", side_part, moment_diag, precision=highest
    )
    new_side = (side_part - step_rate * side_change) * border_keep
    return (
        jnp.concatenate([new_diag, new_side], axis=-1),
        jnp.concatenate([moment_diag, moment_side], axis=-1),
    )


def general(acts, out_grads, token_counts, k_factor, c_factor, k_moment, c_moment, grad_weight):
    tok_dev, width = acts.shape
    blocks_dev = k_factor.shape[0]
    block_size = k_factor.shape[1]
    group_count = lax.axis_size("dp")
    shard_count = lax.axis_size("fsdp")
    group_id = lax.axis_index("dp")
    shard_id = lax.axis_index("fsdp")
    token_total = jnp.sum(token_counts).astype(jnp.float32)
    valid_limit = jnp.sum(jnp.where(lax.iota(jnp.int32, group_count) == group_id, token_counts, 0))
    positions = shard_id * tok_dev + lax.iota(jnp.int32, tok_dev)
    row_keep = (positions < valid_limit).astype(jnp.bfloat16)[:, None]
    masked_acts = acts * row_keep
    masked_grads = out_grads * row_keep
    block_ids = shard_id * blocks_dev + lax.iota(jnp.int32, blocks_dev)
    border_keep = (block_ids > 0).astype(jnp.float32)[:, None, None]
    lead_k, lead_c = (
        spread(k_factor[0, :, :block_size], "fsdp", 0),
        spread(c_factor[0, :, :block_size], "fsdp", 0),
    )
    raw_acts, raw_grads = to_owners((masked_acts, masked_grads))
    lead_raw_acts, lead_raw_grads = fetch_lead(
        (masked_acts[:, :block_size], masked_grads[:, :block_size])
    )
    k_diag_half = k_factor[:, :, :block_size].astype(jnp.bfloat16)
    k_side_half = (k_factor[:, :, block_size:] * border_keep).astype(jnp.bfloat16)
    c_diag_half = c_factor[:, :, :block_size].astype(jnp.bfloat16)
    c_side_half = (c_factor[:, :, block_size:] * border_keep).astype(jnp.bfloat16)
    owned_acts = owner_image(raw_acts, lead_raw_acts, k_diag_half, k_side_half)
    owned_grads = owner_image(raw_grads, lead_raw_grads, c_diag_half, c_side_half)
    lead_acts = jnp.dot(
        lead_raw_acts, lead_k.astype(jnp.bfloat16), preferred_element_type=jnp.float32
    ).astype(jnp.bfloat16)
    lead_grads = jnp.dot(
        lead_raw_grads, lead_c.astype(jnp.bfloat16), preferred_element_type=jnp.float32
    ).astype(jnp.bfloat16)
    own_k, cross_k = block_stats(owned_acts, lead_acts, blocks_dev, block_size)
    own_c, cross_c = block_stats(owned_grads, lead_grads, blocks_dev, block_size)
    summed = lax.psum((own_k, cross_k, own_c, cross_c), "dp")
    gram_k = gram_trace(k_factor, border_keep)
    gram_c = gram_trace(c_factor, border_keep)
    local_traces = jnp.stack(
        [
            jnp.sum(jnp.trace(summed[0], axis1=1, axis2=2)),
            jnp.sum(jnp.trace(summed[2], axis1=1, axis2=2)),
            gram_k,
            gram_c,
        ]
    )
    totals = lax.psum(local_traces, "fsdp")
    trace_hk = totals[0] / token_total
    trace_hc = totals[1] / token_total
    scale_width = float(width)
    k_factor_new, k_moment_new = advance(
        k_factor,
        k_moment,
        summed[0] / token_total,
        summed[1] / token_total,
        lead_k,
        border_keep,
        trace_hc,
        totals[3],
        scale_width,
    )
    c_factor_new, c_moment_new = advance(
        c_factor,
        c_moment,
        summed[2] / token_total,
        summed[3] / token_total,
        lead_c,
        border_keep,
        trace_hk,
        totals[2],
        scale_width,
    )
    grad_rows = grad_weight.shape[0]
    grad_lead = spread(grad_weight[:, :block_size], "fsdp", 0)
    k_diag = k_factor_new[:, :, :block_size].astype(jnp.bfloat16)
    k_side = k_factor_new[:, :, block_size:].astype(jnp.bfloat16)
    grad_blocked = grad_weight.reshape(grad_rows, blocks_dev, block_size)
    first_sum = jnp.einsum("rnk,nkj->rnj", grad_blocked, k_diag, preferred_element_type=jnp.float32)
    first_sum = first_sum + jnp.einsum(
        "rk,nkj->rnj", grad_lead, k_side, preferred_element_type=jnp.float32
    )
    first_product = first_sum.astype(jnp.bfloat16)
    own_second = jnp.einsum(
        "rnk,njk->rnj", first_product, k_diag, preferred_element_type=jnp.float32
    )
    lead_term = jnp.einsum("rnk,njk->rj", first_product, k_side, preferred_element_type=jnp.float32)
    lead_sum = lax.psum(lead_term, "fsdp")
    lead_mask = (block_ids == 0).astype(jnp.float32)[None, :, None]
    second_product = (own_second + lead_mask * lead_sum[:, None, :]).astype(jnp.bfloat16)
    row_blocks = grad_rows // block_size
    owner_count = shard_count // group_count
    c_half = c_factor_new.astype(jnp.bfloat16)
    fetched = []
    for owner_step in range(owner_count):
        fetched.append(spread(c_half, "fsdp", group_id * owner_count + owner_step))
    row_factor = jnp.concatenate(fetched, axis=0)
    c_diag = row_factor[:, :, :block_size]
    c_side = row_factor[:, :, block_size:]
    by_rows = second_product.reshape(row_blocks, block_size, blocks_dev * block_size)
    lead_rows = spread(by_rows[0], "dp", 0)
    third_sum = jnp.einsum("nki,nkc->nic", c_diag, by_rows, preferred_element_type=jnp.float32)
    third_sum = third_sum + jnp.einsum(
        "nki,kc->nic", c_side, lead_rows, preferred_element_type=jnp.float32
    )
    third_product = third_sum.astype(jnp.bfloat16)
    own_fourth = jnp.einsum(
        "nik,nkc->nic", c_diag, third_product, preferred_element_type=jnp.float32
    )
    row_term = jnp.einsum("nik,nkc->ic", c_side, third_product, preferred_element_type=jnp.float32)
    row_sum = lax.psum(row_term, "dp")
    row_ids = group_id * row_blocks + lax.iota(jnp.int32, row_blocks)
    row_mask = (row_ids == 0).astype(jnp.float32)[:, None, None]
    precond = (
        (own_fourth + row_mask * row_sum[None, :, :])
        .astype(jnp.bfloat16)
        .reshape(grad_rows, blocks_dev * block_size)
    )
    return (k_factor_new, c_factor_new, k_moment_new, c_moment_new, precond)


def per_device(*args):
    blocks = args[3].shape[0]
    groups, shards = lax.axis_size("dp"), lax.axis_size("fsdp")
    fits = blocks == 4 and groups == 4 and shards == 8
    return (planned if fits else general)(*args)


def solution(mesh):
    in_specs = (
        P(("dp", "fsdp"), None),
        P(("dp", "fsdp"), None),
        P(),
        P("fsdp", None, None),
        P("fsdp", None, None),
        P("fsdp", None, None),
        P("fsdp", None, None),
        P("dp", "fsdp"),
    )
    out_specs = (
        P("fsdp", None, None),
        P("fsdp", None, None),
        P("fsdp", None, None),
        P("fsdp", None, None),
        P("dp", "fsdp"),
    )
    return jax.shard_map(
        per_device, mesh=mesh, in_specs=in_specs, out_specs=out_specs, check_vma=False
    )
```

```python
import functools

import jax
import jax.numpy as jnp
from jax import lax
from jax.experimental import pallas as pl
from jax.experimental.pallas import tpu as pltpu
from jax.sharding import PartitionSpec as P

damping = 0.1
momentum_rate = 0.5
step_rate = 0.2
highest = lax.Precision.HIGHEST
both = ("dp", "fsdp")
f32 = jnp.float32
bf16 = jnp.bfloat16
vmem_cap = 48 * 1024 * 1024


def params(*semantics):
    return pltpu.CompilerParams(dimension_semantics=semantics, vmem_limit_bytes=vmem_cap)


def dot(a, b, dims=((1,), (0,)), precision=None):
    return lax.dot_general(a, b, (dims, ((), ())), precision=precision, preferred_element_type=f32)


nn = ((1,), (0,))
tn = ((0,), (0,))
nt = ((1,), (1,))


def pack_body(zs, xs, ds, bs, tile, lim_ref, a_ref, o_ref):
    rows = pl.program_id(0) * tile + lax.broadcasted_iota(jnp.int32, (tile, bs), 0)
    keep = jnp.where(rows < lim_ref[0], 1.0, 0.0).astype(bf16)
    lead = a_ref[:, :bs] * keep
    for d in range(ds):
        for x in range(xs):
            for z in range(zs):
                n = (z * xs + x) * ds + d
                o_ref[d * xs + x, z] = a_ref[:, n * bs : (n + 1) * bs] * keep
            o_ref[d * xs + x, zs] = lead


def pack(limit, tokens, zs, xs, ds, bs):
    count, width = tokens.shape
    tile = 32
    return pl.pallas_call(
        functools.partial(pack_body, zs, xs, ds, bs, tile),
        grid=(count // tile,),
        in_specs=[
            pl.BlockSpec(memory_space=pltpu.SMEM),
            pl.BlockSpec((tile, width), lambda i: (i, 0)),
        ],
        out_specs=pl.BlockSpec((ds * xs, zs + 1, tile, bs), lambda i: (0, 0, i, 0)),
        out_shape=jax.ShapeDtypeStruct((ds * xs, zs + 1, count, bs), bf16),
        compiler_params=params("arbitrary"),
        name="pack_tokens",
    )(limit, tokens)


def stats_body(x_ref, l_ref, f_ref, b_ref, o_ref, t_ref, lead_image):
    groups, _, count, bs = x_ref.shape
    k = pl.program_id(0)
    cols = x_ref[:, 0].reshape(groups * count, bs)
    lead = l_ref[:, 0].reshape(groups * count, bs)

    @pl.when(k == 0)
    def _():
        lead_image[...] = dot(lead, b_ref[...]).astype(bf16)
        t_ref[...] = jnp.zeros_like(t_ref)

    image = (dot(cols, f_ref[0, :, :bs]) + dot(lead, f_ref[0, :, bs:])).astype(bf16)
    o_ref[0, 0] = dot(image, image, tn).astype(bf16)
    o_ref[0, 1] = dot(lead_image[...], image, tn).astype(bf16)
    wide = image.astype(f32)
    t_ref[...] = t_ref[...] + jnp.sum(wide * wide)


def stats(ids, owned, blocks, lead):
    groups, slots, count, bs = owned.shape
    zs = slots - 1

    def body(ids_ref, *refs):
        stats_body(*refs)

    return pl.pallas_call(
        body,
        grid_spec=pltpu.PrefetchScalarGridSpec(
            num_scalar_prefetch=1,
            grid=(zs,),
            in_specs=[
                pl.BlockSpec((groups, 1, count, bs), lambda k, ids: (0, ids[0] ^ k, 0, 0)),
                pl.BlockSpec((groups, 1, count, bs), lambda k, ids: (0, zs, 0, 0)),
                pl.BlockSpec((1, bs, 2 * bs), lambda k, ids: (k, 0, 0)),
                pl.BlockSpec((bs, bs), lambda k, ids: (0, 0)),
            ],
            out_specs=[
                pl.BlockSpec((1, 2, bs, bs), lambda k, ids: (k, 0, 0, 0)),
                pl.BlockSpec((8, 128), lambda k, ids: (0, 0)),
            ],
            scratch_shapes=[pltpu.VMEM((groups * count, bs), bf16)],
        ),
        out_shape=[
            jax.ShapeDtypeStruct((zs, 2, bs, bs), bf16),
            jax.ShapeDtypeStruct((8, 128), f32),
        ],
        compiler_params=params("arbitrary"),
        name="plane_stats",
    )(ids, owned, owned, blocks, lead)


def advance_block(width, own, cross, fac, mom, b0, other_h, other_g, keep):
    bs = fac.shape[0]
    diag = fac[:, :bs]
    side = fac[:, bs:] * keep
    db = diag.astype(bf16)
    sb = side.astype(bf16)
    gram_d = dot(db, db, tn) + dot(sb, sb, tn)
    gram_s = dot(b0, sb, tn)
    row = lax.broadcasted_iota(jnp.int32, (bs, bs), 0)
    col = lax.broadcasted_iota(jnp.int32, (bs, bs), 1)
    ident = jnp.where(row == col, width, 0.0)
    scale = 1.0 / (2.0 * width)
    md = momentum_rate * mom[:, :bs] + (other_h * own + damping * other_g * gram_d - ident) * scale
    ms = momentum_rate * mom[:, bs:] + (other_h * cross + damping * other_g * gram_s) * scale
    ms = ms * keep
    mdb = md.astype(bf16)
    new_d = diag - step_rate * dot(db, mdb)
    new_s = side - step_rate * (dot(b0, ms.astype(bf16)) + dot(sb, mdb)) * keep
    return md, ms, new_d, new_s


def order_of(ids, m):
    return ids[1] ^ ((m & 1) * 2 + (m >> 1))


def advance_body(width, ids_ref, sc_ref, h_ref, fac_ref, mom_ref, lead_ref, fn_ref, mn_ref, fb_ref):
    bs = lead_ref.shape[0]
    j = order_of(ids_ref, pl.program_id(0))
    keep = jnp.where(ids_ref[2] + j > 0, 1.0, 0.0)
    md, ms, new_d, new_s = advance_block(
        width,
        h_ref[0, 0].astype(f32),
        h_ref[0, 1].astype(f32),
        fac_ref[0],
        mom_ref[0],
        lead_ref[...],
        sc_ref[0],
        sc_ref[1],
        keep,
    )
    fn_ref[0, :, :bs] = new_d
    fn_ref[0, :, bs:] = new_s
    mn_ref[0, :, :bs] = md
    mn_ref[0, :, bs:] = ms
    fb_ref[0, :, :bs] = new_d.astype(bf16)
    fb_ref[0, :, bs:] = new_s.astype(bf16)


def advance_all(width, ids, scalars, stats, factor, moment, lead):
    blocks, bs, wide = factor.shape
    spec = pl.BlockSpec((1, bs, wide), lambda m, ids: (order_of(ids, m), 0, 0))
    return pl.pallas_call(
        functools.partial(advance_body, width),
        grid_spec=pltpu.PrefetchScalarGridSpec(
            num_scalar_prefetch=1,
            grid=(blocks,),
            in_specs=[
                pl.BlockSpec(memory_space=pltpu.SMEM),
                pl.BlockSpec((1, 2, bs, bs), lambda m, ids: (m, 0, 0, 0)),
                spec,
                spec,
                pl.BlockSpec((bs, bs), lambda m, ids: (0, 0)),
            ],
            out_specs=[spec, spec, spec],
        ),
        out_shape=[
            jax.ShapeDtypeStruct(factor.shape, f32),
            jax.ShapeDtypeStruct(factor.shape, f32),
            jax.ShapeDtypeStruct(factor.shape, bf16),
        ],
        compiler_params=params("arbitrary"),
        name="advance_all",
    )(ids, scalars, stats, factor, moment, lead)


def columns_body(ids_ref, g_ref, l_ref, k_ref, s_ref, t_ref):
    blocks, bs, _ = k_ref.shape
    lead = l_ref[...]
    term = None
    for n in range(blocks):
        kd = k_ref[n, :, :bs]
        ks = k_ref[n, :, bs:]
        first = (dot(g_ref[:, n * bs : (n + 1) * bs], kd) + dot(lead, ks)).astype(bf16)
        second = dot(first, kd, nt)
        s_ref[:, n * bs : (n + 1) * bs] = second.astype(bf16)
        part = dot(first, ks, nt)
        if n == 0:
            part = part + second * jnp.where(ids_ref[2] == 0, 1.0, 0.0)
        term = part if term is None else term + part
    t_ref[...] = term.astype(bf16)


def columns(ids, grad, lead, kb):
    rows, wide = grad.shape
    blocks, bs, _ = kb.shape
    tile = 512
    return pl.pallas_call(
        columns_body,
        grid_spec=pltpu.PrefetchScalarGridSpec(
            num_scalar_prefetch=1,
            grid=(rows // tile,),
            in_specs=[
                pl.BlockSpec((tile, wide), lambda i, ids: (i, 0)),
                pl.BlockSpec((tile, bs), lambda i, ids: (i, 0)),
                pl.BlockSpec(kb.shape, lambda i, ids: (0, 0, 0)),
            ],
            out_specs=[
                pl.BlockSpec((tile, wide), lambda i, ids: (i, 0)),
                pl.BlockSpec((tile, bs), lambda i, ids: (i, 0)),
            ],
        ),
        out_shape=[
            jax.ShapeDtypeStruct((rows, wide), bf16),
            jax.ShapeDtypeStruct((rows, bs), bf16),
        ],
        compiler_params=params("arbitrary"),
        name="column_products",
    )(ids, grad, lead, kb)


def row_of(ids, k):
    per = ids[4]
    return ((ids[3] & 1) ^ (k // per)) * per + k % per


def rows_body(ids_ref, s_ref, g_ref, l_ref, c_ref, p_ref, u_ref, acc_ref):
    k = pl.program_id(0)
    bs = l_ref.shape[0]
    cd = c_ref[0, :, :bs]
    cs = c_ref[0, :, bs:]
    lead = jnp.where(ids_ref[3] == 0, g_ref[...], s_ref[:, :bs])
    second = jnp.concatenate([lead, s_ref[:, bs:]], axis=1)
    third = (dot(cd, second, tn) + dot(cs, l_ref[...], tn)).astype(bf16)
    fourth = dot(cd, third)
    p_ref[...] = fourth.astype(bf16)
    is_first = (ids_ref[1] == 0) & (row_of(ids_ref, k) == 0)
    term = dot(cs, third) + fourth * jnp.where(is_first, 1.0, 0.0)

    @pl.when(k == 0)
    def _():
        acc_ref[...] = term

    @pl.when(k > 0)
    def _():
        acc_ref[...] = acc_ref[...] + term

    @pl.when(k == pl.num_programs(0) - 1)
    def _():
        u_ref[...] = acc_ref[...].astype(bf16)


def rows(ids, second, gathered, lead, cb):
    count, wide = second.shape
    blocks, bs, _ = cb.shape
    spec = pl.BlockSpec((bs, wide), lambda k, ids: (row_of(ids, k), 0))
    whole = pl.BlockSpec((bs, wide), lambda k, ids: (0, 0))
    return pl.pallas_call(
        rows_body,
        grid_spec=pltpu.PrefetchScalarGridSpec(
            num_scalar_prefetch=1,
            grid=(blocks,),
            in_specs=[
                spec,
                pl.BlockSpec((bs, bs), lambda k, ids: (row_of(ids, k), 0)),
                whole,
                pl.BlockSpec((1, bs, 2 * bs), lambda k, ids: (k, 0, 0)),
            ],
            out_specs=[spec, whole],
            scratch_shapes=[pltpu.VMEM((bs, wide), f32)],
        ),
        out_shape=[
            jax.ShapeDtypeStruct((count, wide), bf16),
            jax.ShapeDtypeStruct((bs, wide), bf16),
        ],
        compiler_params=params("arbitrary"),
        name="row_products",
    )(ids, second, gathered, lead, cb)


def put_top_body(ids_ref, p_ref, low_ref, high_ref, o_ref):
    half = low_ref.shape[0]
    first = ids_ref[1] == 0

    @pl.when(first)
    def _():
        o_ref[:half] = low_ref[...]
        o_ref[half:] = high_ref[...]

    @pl.when(jnp.logical_not(first))
    def _():
        o_ref[...] = p_ref[...]


def put_top(ids, tile, low, high):
    half, wide = low.shape
    top = pl.BlockSpec((2 * half, wide), lambda i, ids: (0, 0))
    part = pl.BlockSpec((half, wide), lambda i, ids: (0, 0))
    return pl.pallas_call(
        put_top_body,
        grid_spec=pltpu.PrefetchScalarGridSpec(
            num_scalar_prefetch=1, grid=(1,), in_specs=[top, part, part], out_specs=top
        ),
        out_shape=jax.ShapeDtypeStruct(tile.shape, tile.dtype),
        input_output_aliases={1: 0},
        compiler_params=params("arbitrary"),
        name="put_top",
    )(ids, tile, low, high)


def after(value, *earlier):
    return lax.optimization_barrier((value,) + earlier)[0]


def planned(acts, out_grads, token_counts, k_factor, c_factor, k_moment, c_moment, grad_weight):
    tok_dev, width = acts.shape
    ds, bs, _ = k_factor.shape
    shards = lax.axis_size("fsdp")
    xs = 2
    zs = shards // xs
    d = lax.axis_index("dp")
    s = lax.axis_index("fsdp")
    x = s % xs
    z = s // xs
    flat = lambda dd, ss: dd * shards + ss
    plane = [[flat(dd, zz * xs + xx) for dd in range(ds) for xx in range(xs)] for zz in range(zs)]
    flip_x = [(i, i ^ 1) for i in range(shards)]
    ids = jnp.stack([z, d, s * ds, s, jnp.int32(ds)]).astype(jnp.int32)
    token_total = jnp.sum(token_counts).astype(f32)
    valid = jnp.sum(jnp.where(lax.iota(jnp.int32, ds) == d, token_counts, 0))
    limit = (valid - s * tok_dev).reshape(1).astype(jnp.int32)

    def along_z(value, k):
        pairs = [(zz * xs + xx, (zz ^ k) * xs + xx) for zz in range(zs) for xx in range(xs)]
        return lax.ppermute(value, "fsdp", pairs)

    def from_plane_0(value):
        got = [
            lax.ppermute(value, "fsdp", [(xx, zz * xs + xx) for xx in range(xs)])
            for zz in range(1, zs)
        ]
        out = got[0]
        for g in got[1:]:
            out = out + g
        return jnp.where(z == 0, value, out)

    def block_along_z(factor, *earlier):
        own = lax.dynamic_index_in_dim(factor, d, 0, keepdims=False)
        side_keep = jnp.where(s * ds + d > 0, 1.0, 0.0)
        own = jnp.concatenate([own[:, :bs], own[:, bs:] * side_keep], axis=1).astype(bf16)
        own = after(own, *earlier)
        return jnp.stack([own] + [along_z(own, k) for k in range(1, zs)])

    def sum_along_z(partial):
        total = partial[0].astype(f32)
        for k in range(1, zs):
            total = total + along_z(partial[k], k).astype(f32)
        return (total / token_total).astype(bf16)

    def over_dp(value):
        pair = jnp.stack([value, lax.ppermute(value, "dp", [(i, i ^ 2) for i in range(ds)])])
        other = lax.ppermute(pair, "dp", [(i, i ^ 1) for i in range(ds)])
        return jnp.concatenate([pair, other], axis=0)

    def gram_part(factor):
        block_ids = s * ds + lax.iota(jnp.int32, ds)
        keep = (block_ids > 0).astype(f32)[:, None, None]
        side = factor[:, :, bs:] * keep
        return (jnp.sum(factor[:, :, :bs] ** 2) + jnp.sum(side * side)) / ds

    def exchange(packed):
        return lax.all_to_all(packed, both, 0, 0, tiled=True, axis_index_groups=plane)

    leads = jnp.stack([k_factor[0, :, :bs], c_factor[0, :, :bs]]).astype(bf16)
    leads = jnp.where(s == 0, leads, lax.ppermute(leads, "fsdp", [(0, 1)]))
    leads = from_plane_0(leads)
    lead_k, lead_c = leads[0], leads[1]
    grad_half = grad_weight.shape[0] // xs
    grad_low = grad_weight[:grad_half, :bs]
    grad_high = lax.ppermute(grad_weight[grad_half:, :bs], "fsdp", [(0, 1)])
    grad_mine = jnp.where(s == 0, grad_low, grad_high)

    owned_k = exchange(pack(limit, acts, zs, xs, ds, bs))
    blocks_k = block_along_z(k_factor)
    packed_c = after(pack(limit, out_grads, zs, xs, ds, bs), owned_k)
    owned_c = exchange(packed_c)
    partial_k, square_k = stats(ids, owned_k, blocks_k, lead_k)
    blocks_c = block_along_z(c_factor, owned_k)
    stat_k = sum_along_z(partial_k)
    grad_mine = from_plane_0(after(grad_mine, partial_k))
    all_k = over_dp(stat_k)
    gram_k = gram_part(k_factor)
    gram_c = gram_part(c_factor)

    partial_c, square_c = stats(ids, owned_c, blocks_c, lead_c)
    rows8 = lax.broadcasted_iota(jnp.int32, (8, 128), 0)
    sums = jnp.where(
        rows8 == 0,
        square_k,
        jnp.where(rows8 == 1, square_c, jnp.where(rows8 == 2, gram_k, gram_c)),
    )
    sums = jnp.broadcast_to(sums[None], (ds * shards, 8, 128))
    totals = jnp.sum(lax.all_to_all(sums, both, 0, 0, tiled=True), axis=0)[:, 0]
    for_k = jnp.stack([totals[1] / token_total, totals[3]])
    for_c = jnp.stack([totals[0] / token_total, totals[2]])
    stat_c = sum_along_z(partial_c)

    grad_other = lax.ppermute(after(grad_mine, owned_c), "fsdp", flip_x)
    grad_lead = jnp.concatenate(
        [jnp.where(x == 0, grad_mine, grad_other), jnp.where(x == 0, grad_other, grad_mine)], axis=0
    )
    scale_width = float(width)
    k_factor_new, k_moment_new, kb = advance_all(
        scale_width, ids, for_k, all_k, k_factor, k_moment, lead_k
    )
    second, term = columns(ids, grad_weight, grad_lead, kb)
    count = grad_weight.shape[0]
    by_shard = term.reshape(shards, count // shards, bs)
    got = lax.all_to_all(by_shard, "fsdp", 0, 0, tiled=True)
    block_sum = jnp.sum(got.astype(f32), axis=0).astype(bf16)

    all_c = over_dp(stat_c)
    c_factor_new, c_moment_new, cb = advance_all(
        scale_width, ids, for_c, all_c, c_factor, c_moment, lead_c
    )
    halves = []
    for h in range(2):
        turn = 2 * h
        pairs = [
            (flat(r ^ turn, zz * xs + xx), flat(zz, r * xs + xx))
            for r in range(ds)
            for zz in range(zs)
            for xx in range(xs)
        ]
        halves.append(lax.ppermute(cb[h * (ds // 2) : (h + 1) * (ds // 2)], both, pairs))
    others = [lax.ppermute(h, "fsdp", flip_x) for h in halves]
    c_rows = jnp.concatenate(halves + others, axis=0)

    pair = jnp.stack([block_sum, lax.ppermute(block_sum, "fsdp", [(2 * k + 1, 2 * k) for k in range(zs)])])
    gathered = [pair] + [lax.ppermute(pair, "fsdp", [(xs * k, 0)]) for k in range(1, zs)]
    gathered = jnp.concatenate(gathered, axis=0).reshape(count, bs)
    top = jnp.concatenate([jnp.where(s == 0, block_sum, second[:bs, :bs]), second[:bs, bs:]], axis=1)
    over_y = lax.ppermute(top, "dp", [(0, 2)])
    top = jnp.where(d == 0, top, over_y)
    over_core = lax.ppermute(top, "dp", [(0, 1), (2, 3)])
    lead_rows = jnp.where(d % 2 == 0, top, over_core)

    precond, up = rows(ids, second, gathered, lead_rows, c_rows)
    half = bs // 2
    core = d % 2
    mine = jnp.where(core == 0, up[:half], up[half:])
    theirs = jnp.where(core == 0, up[half:], up[:half])
    mine = mine.astype(f32) + lax.ppermute(theirs, "dp", [(i, i ^ 1) for i in range(ds)])
    low = mine.astype(bf16)
    mine = (mine + lax.ppermute(low, "dp", [(2, 0), (3, 1)])).astype(bf16)
    high = lax.ppermute(mine, "dp", [(1, 0)])
    precond = put_top(ids, precond, mine, high)
    return (k_factor_new, c_factor_new, k_moment_new, c_moment_new, precond)


def spread(value, axis, source):
    kept = jnp.where(lax.axis_index(axis) == source, value, 0).astype(value.dtype)
    return lax.psum(kept, axis)


def owner_image(columns, lead_columns, diag_half, side_half):
    row_count = columns.shape[0]
    block_count = diag_half.shape[0]
    block_size = diag_half.shape[1]
    blocked = columns.reshape(row_count, block_count, block_size)
    image_sum = jnp.einsum("tnk,nkj->tnj", blocked, diag_half, preferred_element_type=jnp.float32)
    image_sum = image_sum + jnp.einsum(
        "tk,nkj->tnj", lead_columns, side_half, preferred_element_type=jnp.float32
    )
    return image_sum.astype(jnp.bfloat16).reshape(row_count, block_count * block_size)


def to_owners(pair):
    return (
        lax.all_to_all(pair[0], "fsdp", split_axis=1, concat_axis=0, tiled=True),
        lax.all_to_all(pair[1], "fsdp", split_axis=1, concat_axis=0, tiled=True),
    )


def fetch_lead(before):
    return (
        lax.all_gather(before[0], "fsdp", axis=0, tiled=True),
        lax.all_gather(before[1], "fsdp", axis=0, tiled=True),
    )


def block_stats(owned, lead_image, block_count, block_size):
    blocked = owned.reshape(owned.shape[0], block_count, block_size)
    own_sum = jnp.einsum("tni,tnj->nij", blocked, blocked, preferred_element_type=jnp.float32)
    cross_sum = jnp.einsum("ti,tnj->nij", lead_image, blocked, preferred_element_type=jnp.float32)
    return (own_sum, cross_sum)


def gram_trace(factor, border_keep):
    block_size = factor.shape[1]
    diag_part = factor[:, :, :block_size]
    side_part = factor[:, :, block_size:] * border_keep
    return jnp.sum(diag_part * diag_part) + jnp.sum(side_part * side_part)


def advance(factor, moment, own_sum, cross_sum, lead_block, border_keep, other_h, other_g, width):
    block_size = factor.shape[1]
    diag_part = factor[:, :, :block_size]
    side_part = factor[:, :, block_size:] * border_keep
    gram_diag = jnp.einsum("nki,nkj->nij", diag_part, diag_part, precision=highest)
    gram_diag = gram_diag + jnp.einsum("nki,nkj->nij", side_part, side_part, precision=highest)
    gram_side = jnp.einsum("ki,nkj->nij", lead_block, side_part, precision=highest)
    identity = jnp.eye(block_size, dtype=jnp.float32)
    fresh_diag = (other_h * own_sum + damping * other_g * gram_diag - width * identity) / (
        2.0 * width
    )
    fresh_side = (other_h * cross_sum + damping * other_g * gram_side) * border_keep / (2.0 * width)
    moment_diag = momentum_rate * moment[:, :, :block_size] + fresh_diag
    moment_side = (momentum_rate * moment[:, :, block_size:] + fresh_side) * border_keep
    new_diag = diag_part - step_rate * jnp.einsum(
        "nik,nkj->nij", diag_part, moment_diag, precision=highest
    )
    side_change = jnp.einsum("ik,nkj->nij", lead_block, moment_side, precision=highest)
    side_change = side_change + jnp.einsum(
        "nik,nkj->nij", side_part, moment_diag, precision=highest
    )
    new_side = (side_part - step_rate * side_change) * border_keep
    return (
        jnp.concatenate([new_diag, new_side], axis=-1),
        jnp.concatenate([moment_diag, moment_side], axis=-1),
    )


def general(acts, out_grads, token_counts, k_factor, c_factor, k_moment, c_moment, grad_weight):
    tok_dev, width = acts.shape
    blocks_dev = k_factor.shape[0]
    block_size = k_factor.shape[1]
    group_count = lax.axis_size("dp")
    shard_count = lax.axis_size("fsdp")
    group_id = lax.axis_index("dp")
    shard_id = lax.axis_index("fsdp")
    token_total = jnp.sum(token_counts).astype(jnp.float32)
    valid_limit = jnp.sum(jnp.where(lax.iota(jnp.int32, group_count) == group_id, token_counts, 0))
    positions = shard_id * tok_dev + lax.iota(jnp.int32, tok_dev)
    row_keep = (positions < valid_limit).astype(jnp.bfloat16)[:, None]
    masked_acts = acts * row_keep
    masked_grads = out_grads * row_keep
    block_ids = shard_id * blocks_dev + lax.iota(jnp.int32, blocks_dev)
    border_keep = (block_ids > 0).astype(jnp.float32)[:, None, None]
    lead_k, lead_c = (
        spread(k_factor[0, :, :block_size], "fsdp", 0),
        spread(c_factor[0, :, :block_size], "fsdp", 0),
    )
    raw_acts, raw_grads = to_owners((masked_acts, masked_grads))
    lead_raw_acts, lead_raw_grads = fetch_lead(
        (masked_acts[:, :block_size], masked_grads[:, :block_size])
    )
    k_diag_half = k_factor[:, :, :block_size].astype(jnp.bfloat16)
    k_side_half = (k_factor[:, :, block_size:] * border_keep).astype(jnp.bfloat16)
    c_diag_half = c_factor[:, :, :block_size].astype(jnp.bfloat16)
    c_side_half = (c_factor[:, :, block_size:] * border_keep).astype(jnp.bfloat16)
    owned_acts = owner_image(raw_acts, lead_raw_acts, k_diag_half, k_side_half)
    owned_grads = owner_image(raw_grads, lead_raw_grads, c_diag_half, c_side_half)
    lead_acts = jnp.dot(
        lead_raw_acts, lead_k.astype(jnp.bfloat16), preferred_element_type=jnp.float32
    ).astype(jnp.bfloat16)
    lead_grads = jnp.dot(
        lead_raw_grads, lead_c.astype(jnp.bfloat16), preferred_element_type=jnp.float32
    ).astype(jnp.bfloat16)
    own_k, cross_k = block_stats(owned_acts, lead_acts, blocks_dev, block_size)
    own_c, cross_c = block_stats(owned_grads, lead_grads, blocks_dev, block_size)
    summed = lax.psum((own_k, cross_k, own_c, cross_c), "dp")
    gram_k = gram_trace(k_factor, border_keep)
    gram_c = gram_trace(c_factor, border_keep)
    local_traces = jnp.stack(
        [
            jnp.sum(jnp.trace(summed[0], axis1=1, axis2=2)),
            jnp.sum(jnp.trace(summed[2], axis1=1, axis2=2)),
            gram_k,
            gram_c,
        ]
    )
    totals = lax.psum(local_traces, "fsdp")
    trace_hk = totals[0] / token_total
    trace_hc = totals[1] / token_total
    scale_width = float(width)
    k_factor_new, k_moment_new = advance(
        k_factor,
        k_moment,
        summed[0] / token_total,
        summed[1] / token_total,
        lead_k,
        border_keep,
        trace_hc,
        totals[3],
        scale_width,
    )
    c_factor_new, c_moment_new = advance(
        c_factor,
        c_moment,
        summed[2] / token_total,
        summed[3] / token_total,
        lead_c,
        border_keep,
        trace_hk,
        totals[2],
        scale_width,
    )
    grad_rows = grad_weight.shape[0]
    grad_lead = spread(grad_weight[:, :block_size], "fsdp", 0)
    k_diag = k_factor_new[:, :, :block_size].astype(jnp.bfloat16)
    k_side = k_factor_new[:, :, block_size:].astype(jnp.bfloat16)
    grad_blocked = grad_weight.reshape(grad_rows, blocks_dev, block_size)
    first_sum = jnp.einsum("rnk,nkj->rnj", grad_blocked, k_diag, preferred_element_type=jnp.float32)
    first_sum = first_sum + jnp.einsum(
        "rk,nkj->rnj", grad_lead, k_side, preferred_element_type=jnp.float32
    )
    first_product = first_sum.astype(jnp.bfloat16)
    own_second = jnp.einsum(
        "rnk,njk->rnj", first_product, k_diag, preferred_element_type=jnp.float32
    )
    lead_term = jnp.einsum("rnk,njk->rj", first_product, k_side, preferred_element_type=jnp.float32)
    lead_sum = lax.psum(lead_term, "fsdp")
    lead_mask = (block_ids == 0).astype(jnp.float32)[None, :, None]
    second_product = (own_second + lead_mask * lead_sum[:, None, :]).astype(jnp.bfloat16)
    row_blocks = grad_rows // block_size
    owner_count = shard_count // group_count
    c_half = c_factor_new.astype(jnp.bfloat16)
    fetched = []
    for owner_step in range(owner_count):
        fetched.append(spread(c_half, "fsdp", group_id * owner_count + owner_step))
    row_factor = jnp.concatenate(fetched, axis=0)
    c_diag = row_factor[:, :, :block_size]
    c_side = row_factor[:, :, block_size:]
    by_rows = second_product.reshape(row_blocks, block_size, blocks_dev * block_size)
    lead_rows = spread(by_rows[0], "dp", 0)
    third_sum = jnp.einsum("nki,nkc->nic", c_diag, by_rows, preferred_element_type=jnp.float32)
    third_sum = third_sum + jnp.einsum(
        "nki,kc->nic", c_side, lead_rows, preferred_element_type=jnp.float32
    )
    third_product = third_sum.astype(jnp.bfloat16)
    own_fourth = jnp.einsum(
        "nik,nkc->nic", c_diag, third_product, preferred_element_type=jnp.float32
    )
    row_term = jnp.einsum("nik,nkc->ic", c_side, third_product, preferred_element_type=jnp.float32)
    row_sum = lax.psum(row_term, "dp")
    row_ids = group_id * row_blocks + lax.iota(jnp.int32, row_blocks)
    row_mask = (row_ids == 0).astype(jnp.float32)[:, None, None]
    precond = (
        (own_fourth + row_mask * row_sum[None, :, :])
        .astype(jnp.bfloat16)
        .reshape(grad_rows, blocks_dev * block_size)
    )
    return (k_factor_new, c_factor_new, k_moment_new, c_moment_new, precond)


def per_device(*args):
    blocks = args[3].shape[0]
    groups, shards = lax.axis_size("dp"), lax.axis_size("fsdp")
    fits = blocks == 4 and groups == 4 and shards == 8
    return (planned if fits else general)(*args)


def solution(mesh):
    in_specs = (
        P(("dp", "fsdp"), None),
        P(("dp", "fsdp"), None),
        P(),
        P("fsdp", None, None),
        P("fsdp", None, None),
        P("fsdp", None, None),
        P("fsdp", None, None),
        P("dp", "fsdp"),
    )
    out_specs = (
        P("fsdp", None, None),
        P("fsdp", None, None),
        P("fsdp", None, None),
        P("fsdp", None, None),
        P("dp", "fsdp"),
    )
    return jax.shard_map(
        per_device, mesh=mesh, in_specs=in_specs, out_specs=out_specs, check_vma=False
    )
```

```python
import functools

import jax
import jax.numpy as jnp
from jax import lax
from jax.experimental import pallas as pl
from jax.experimental.pallas import tpu as pltpu
from jax.sharding import PartitionSpec as P

damping = 0.1
momentum_rate = 0.5
step_rate = 0.2
highest = lax.Precision.HIGHEST
both = ("dp", "fsdp")
f32 = jnp.float32
bf16 = jnp.bfloat16
vmem_cap = 48 * 1024 * 1024


def params(*semantics):
    return pltpu.CompilerParams(dimension_semantics=semantics, vmem_limit_bytes=vmem_cap)


light = pl.CostEstimate(flops=1, transcendentals=0, bytes_accessed=1)


def dot(a, b, dims=((1,), (0,)), precision=None):
    return lax.dot_general(a, b, (dims, ((), ())), precision=precision, preferred_element_type=f32)


nn = ((1,), (0,))
tn = ((0,), (0,))
nt = ((1,), (1,))


def pack_body(zs, xs, ds, bs, tile, lim_ref, a_ref, o_ref):
    rows = pl.program_id(0) * tile + lax.broadcasted_iota(jnp.int32, (tile, bs), 0)
    keep = jnp.where(rows < lim_ref[0], 1.0, 0.0).astype(bf16)
    lead = a_ref[:, :bs] * keep
    for d in range(ds):
        for x in range(xs):
            for z in range(zs):
                n = (z * xs + x) * ds + d
                o_ref[d * xs + x, z] = a_ref[:, n * bs : (n + 1) * bs] * keep
            o_ref[d * xs + x, zs] = lead


def pack(limit, tokens, zs, xs, ds, bs):
    count, width = tokens.shape
    tile = 32
    return pl.pallas_call(
        functools.partial(pack_body, zs, xs, ds, bs, tile),
        grid=(count // tile,),
        in_specs=[
            pl.BlockSpec(memory_space=pltpu.SMEM),
            pl.BlockSpec((tile, width), lambda i: (i, 0)),
        ],
        out_specs=pl.BlockSpec((ds * xs, zs + 1, tile, bs), lambda i: (0, 0, i, 0)),
        out_shape=jax.ShapeDtypeStruct((ds * xs, zs + 1, count, bs), bf16),
        cost_estimate=light,
        compiler_params=params("arbitrary"),
        name="pack_tokens",
    )(limit, tokens)


def moments_body(ids_ref, x_ref, l_ref, o_ref):
    groups, _, count, bs = x_ref.shape
    cols = x_ref[:, 0].reshape(groups * count, bs)
    lead = l_ref[:, 0].reshape(groups * count, bs)
    o_ref[0, 0] = dot(cols, cols, tn).astype(bf16)
    o_ref[0, 1] = dot(lead, cols, tn).astype(bf16)
    o_ref[0, 2] = dot(lead, lead, tn).astype(bf16)


def raw_moments(ids, owned):
    groups, slots, count, bs = owned.shape
    zs = slots - 1
    return pl.pallas_call(
        moments_body,
        grid_spec=pltpu.PrefetchScalarGridSpec(
            num_scalar_prefetch=1,
            grid=(zs,),
            in_specs=[
                pl.BlockSpec((groups, 1, count, bs), lambda k, ids: (0, ids[0] ^ k, 0, 0)),
                pl.BlockSpec((groups, 1, count, bs), lambda k, ids: (0, zs, 0, 0)),
            ],
            out_specs=pl.BlockSpec((1, 3, bs, bs), lambda k, ids: (k, 0, 0, 0)),
        ),
        out_shape=jax.ShapeDtypeStruct((zs, 3, bs, bs), bf16),
        cost_estimate=light,
        compiler_params=params("arbitrary"),
        name="raw_moments",
    )(ids, owned, owned)


def image_stats_body(count, ids_ref, sc_ref, *refs):
    parts = refs[:count]
    fac_ref, h_ref, tr_ref = refs[count:]
    bs = fac_ref.shape[1]
    keep = jnp.where(ids_ref[2] + ids_ref[1] > 0, 1.0, 0.0)
    total = parts[0][...].astype(f32)
    for part in parts[1:]:
        total = total + part[...].astype(f32)
    fac = fac_ref[0]
    bn = fac[:, :bs].astype(bf16).astype(f32)
    pn = (fac[:, bs:] * keep).astype(bf16).astype(f32)
    mm = functools.partial(dot, precision=highest)
    t1 = mm(total[0], bn) + mm(total[1], pn, tn)
    t0 = mm(total[1], bn) + mm(total[2], pn)
    own = (mm(bn, t1, tn) + mm(pn, t0, tn)) * sc_ref[0]
    h_ref[0] = own.astype(bf16)
    h_ref[1] = (t0 * sc_ref[0]).astype(bf16)
    row = lax.broadcasted_iota(jnp.int32, (bs, bs), 0)
    col = lax.broadcasted_iota(jnp.int32, (bs, bs), 1)
    tr_ref[...] = jnp.zeros_like(tr_ref) + jnp.sum(jnp.where(row == col, own, 0.0))


def image_stats(ids, scalars, parts, factor):
    _, bs, wide = factor.shape
    whole = lambda shape: pl.BlockSpec(shape, lambda i, ids: (0,) * len(shape))
    return pl.pallas_call(
        functools.partial(image_stats_body, len(parts)),
        grid_spec=pltpu.PrefetchScalarGridSpec(
            num_scalar_prefetch=1,
            grid=(1,),
            in_specs=[pl.BlockSpec(memory_space=pltpu.SMEM)]
            + [whole((3, bs, bs)) for _ in parts]
            + [pl.BlockSpec((1, bs, wide), lambda i, ids: (ids[1], 0, 0))],
            out_specs=[whole((2, bs, bs)), whole((8, 128))],
        ),
        out_shape=[
            jax.ShapeDtypeStruct((2, bs, bs), bf16),
            jax.ShapeDtypeStruct((8, 128), f32),
        ],
        cost_estimate=light,
        compiler_params=params("arbitrary"),
        name="image_stats",
    )(ids, scalars, *parts, factor)


def stats_body(x_ref, l_ref, f_ref, o_ref, t_ref):
    groups, _, count, bs = x_ref.shape
    k = pl.program_id(0)
    cols = x_ref[:, 0].reshape(groups * count, bs)
    lead = l_ref[:, 0].reshape(groups * count, bs)

    @pl.when(k == 0)
    def _():
        t_ref[...] = jnp.zeros_like(t_ref)

    image = (dot(cols, f_ref[0, :, :bs]) + dot(lead, f_ref[0, :, bs:])).astype(bf16)
    o_ref[0, 0] = dot(image, image, tn).astype(bf16)
    o_ref[0, 1] = dot(lead, image, tn).astype(bf16)
    wide = image.astype(f32)
    t_ref[...] = t_ref[...] + jnp.sum(wide * wide)


def stats(ids, owned, blocks):
    groups, slots, count, bs = owned.shape
    zs = slots - 1

    def body(ids_ref, *refs):
        stats_body(*refs)

    return pl.pallas_call(
        body,
        grid_spec=pltpu.PrefetchScalarGridSpec(
            num_scalar_prefetch=1,
            grid=(zs,),
            in_specs=[
                pl.BlockSpec((groups, 1, count, bs), lambda k, ids: (0, ids[0] ^ k, 0, 0)),
                pl.BlockSpec((groups, 1, count, bs), lambda k, ids: (0, zs, 0, 0)),
                pl.BlockSpec((1, bs, 2 * bs), lambda k, ids: (k, 0, 0)),
            ],
            out_specs=[
                pl.BlockSpec((1, 2, bs, bs), lambda k, ids: (k, 0, 0, 0)),
                pl.BlockSpec((8, 128), lambda k, ids: (0, 0)),
            ],
        ),
        out_shape=[
            jax.ShapeDtypeStruct((zs, 2, bs, bs), bf16),
            jax.ShapeDtypeStruct((8, 128), f32),
        ],
        cost_estimate=light,
        compiler_params=params("arbitrary"),
        name="plane_stats",
    )(ids, owned, owned, blocks)


def advance_block(width, own, cross, fac, mom, b0, other_h, other_g, keep):
    bs = fac.shape[0]
    diag = fac[:, :bs]
    side = fac[:, bs:] * keep
    db = diag.astype(bf16)
    sb = side.astype(bf16)
    gram_d = dot(db, db, tn) + dot(sb, sb, tn)
    gram_s = dot(b0, sb, tn)
    row = lax.broadcasted_iota(jnp.int32, (bs, bs), 0)
    col = lax.broadcasted_iota(jnp.int32, (bs, bs), 1)
    ident = jnp.where(row == col, width, 0.0)
    scale = 1.0 / (2.0 * width)
    md = momentum_rate * mom[:, :bs] + (other_h * own + damping * other_g * gram_d - ident) * scale
    ms = momentum_rate * mom[:, bs:] + (other_h * cross + damping * other_g * gram_s) * scale
    ms = ms * keep
    mdb = md.astype(bf16)
    new_d = diag - step_rate * dot(db, mdb)
    new_s = side - step_rate * (dot(b0, ms.astype(bf16)) + dot(sb, mdb)) * keep
    return md, ms, new_d, new_s


def order_of(ids, m):
    return ids[1] ^ ((m & 1) * 2 + (m >> 1))


def advance_body(width, ids_ref, sc_ref, h_ref, fac_ref, mom_ref, lead_ref, fn_ref, mn_ref, fb_ref):
    bs = lead_ref.shape[0]
    j = order_of(ids_ref, pl.program_id(0))
    keep = jnp.where(ids_ref[2] + j > 0, 1.0, 0.0)
    md, ms, new_d, new_s = advance_block(
        width,
        h_ref[0, 0].astype(f32),
        dot(lead_ref[...], h_ref[0, 1], tn),
        fac_ref[0],
        mom_ref[0],
        lead_ref[...],
        sc_ref[0],
        sc_ref[1],
        keep,
    )
    fn_ref[0, :, :bs] = new_d
    fn_ref[0, :, bs:] = new_s
    mn_ref[0, :, :bs] = md
    mn_ref[0, :, bs:] = ms
    fb_ref[0, :, :bs] = new_d.astype(bf16)
    fb_ref[0, :, bs:] = new_s.astype(bf16)


def advance_all(width, ids, scalars, stats, factor, moment, lead):
    blocks, bs, wide = factor.shape
    spec = pl.BlockSpec((1, bs, wide), lambda m, ids: (order_of(ids, m), 0, 0))
    return pl.pallas_call(
        functools.partial(advance_body, width),
        grid_spec=pltpu.PrefetchScalarGridSpec(
            num_scalar_prefetch=1,
            grid=(blocks,),
            in_specs=[
                pl.BlockSpec(memory_space=pltpu.SMEM),
                pl.BlockSpec((1, 2, bs, bs), lambda m, ids: (m, 0, 0, 0)),
                spec,
                spec,
                pl.BlockSpec((bs, bs), lambda m, ids: (0, 0)),
            ],
            out_specs=[spec, spec, spec],
        ),
        out_shape=[
            jax.ShapeDtypeStruct(factor.shape, f32),
            jax.ShapeDtypeStruct(factor.shape, f32),
            jax.ShapeDtypeStruct(factor.shape, bf16),
        ],
        cost_estimate=light,
        compiler_params=params("arbitrary"),
        name="advance_all",
    )(ids, scalars, stats, factor, moment, lead)


def columns_body(ids_ref, g_ref, l_ref, k_ref, s_ref, t_ref):
    blocks, bs, _ = k_ref.shape
    lead = l_ref[...]
    term = None
    for n in range(blocks):
        kd = k_ref[n, :, :bs]
        ks = k_ref[n, :, bs:]
        first = (dot(g_ref[:, n * bs : (n + 1) * bs], kd) + dot(lead, ks)).astype(bf16)
        second = dot(first, kd, nt)
        s_ref[:, n * bs : (n + 1) * bs] = second.astype(bf16)
        part = dot(first, ks, nt)
        if n == 0:
            part = part + second * jnp.where(ids_ref[2] == 0, 1.0, 0.0)
        term = part if term is None else term + part
    t_ref[...] = term.astype(bf16)


def columns(ids, grad, lead, kb):
    rows, wide = grad.shape
    blocks, bs, _ = kb.shape
    tile = 512
    return pl.pallas_call(
        columns_body,
        grid_spec=pltpu.PrefetchScalarGridSpec(
            num_scalar_prefetch=1,
            grid=(rows // tile,),
            in_specs=[
                pl.BlockSpec((tile, wide), lambda i, ids: (i, 0)),
                pl.BlockSpec((tile, bs), lambda i, ids: (i, 0)),
                pl.BlockSpec(kb.shape, lambda i, ids: (0, 0, 0)),
            ],
            out_specs=[
                pl.BlockSpec((tile, wide), lambda i, ids: (i, 0)),
                pl.BlockSpec((tile, bs), lambda i, ids: (i, 0)),
            ],
        ),
        out_shape=[
            jax.ShapeDtypeStruct((rows, wide), bf16),
            jax.ShapeDtypeStruct((rows, bs), bf16),
        ],
        cost_estimate=light,
        compiler_params=params("arbitrary"),
        name="column_products",
    )(ids, grad, lead, kb)


def row_of(ids, k):
    per = ids[4]
    return ((ids[3] & 1) ^ (k // per)) * per + k % per


def gathered_at(ids, k):
    i = row_of(ids, k)
    return (i % ids[4]) * 2 + i // ids[4]


def rows_body(ids_ref, s_ref, l_ref, c_ref, p_ref, u_ref, acc_ref):
    k = pl.program_id(0)
    bs = c_ref.shape[1]
    cd = c_ref[0, :, :bs]
    cs = c_ref[0, :, bs:]
    third = (dot(cd, s_ref[:, bs:], tn) + dot(cs, l_ref[...], tn)).astype(bf16)
    fourth = dot(cd, third)
    p_ref[:, bs:] = fourth.astype(bf16)
    is_first = (ids_ref[1] == 0) & (row_of(ids_ref, k) == 0)
    term = dot(cs, third) + fourth * jnp.where(is_first, 1.0, 0.0)

    @pl.when(k == 0)
    def _():
        acc_ref[...] = term

    @pl.when(k > 0)
    def _():
        acc_ref[...] = acc_ref[...] + term

    @pl.when(k == pl.num_programs(0) - 1)
    def _():
        u_ref[...] = acc_ref[...].astype(bf16)


def rows(ids, second, lead, cb):
    count, wide = second.shape
    blocks, bs, _ = cb.shape
    rest = wide - bs
    spec = pl.BlockSpec((bs, wide), lambda k, ids: (row_of(ids, k), 0))
    whole = pl.BlockSpec((bs, rest), lambda k, ids: (0, 0))
    return pl.pallas_call(
        rows_body,
        grid_spec=pltpu.PrefetchScalarGridSpec(
            num_scalar_prefetch=1,
            grid=(blocks,),
            in_specs=[
                spec,
                whole,
                pl.BlockSpec((1, bs, 2 * bs), lambda k, ids: (k, 0, 0)),
            ],
            out_specs=[spec, whole],
            scratch_shapes=[pltpu.VMEM((bs, rest), f32)],
        ),
        out_shape=[
            jax.ShapeDtypeStruct((count, wide), bf16),
            jax.ShapeDtypeStruct((bs, rest), bf16),
        ],
        cost_estimate=light,
        compiler_params=params("arbitrary"),
        name="row_products",
    )(ids, second, lead, cb)


def lead_rows_body(ids_ref, s_ref, g_ref, l_ref, c_ref, _, p_ref, u_ref):
    blocks, bs, _ = c_ref.shape
    total = jnp.zeros((bs, bs), f32)
    for k in range(blocks):
        i = row_of(ids_ref, k)
        own = s_ref[pl.ds(pl.multiple_of(i * bs, bs), bs), :]
        whole = g_ref[pl.ds(pl.multiple_of(gathered_at(ids_ref, k) * bs, bs), bs), :]
        second = jnp.where(ids_ref[3] == 0, whole, own)
        cd = c_ref[k, :, :bs]
        cs = c_ref[k, :, bs:]
        third = (dot(cd, second, tn) + dot(cs, l_ref[...], tn)).astype(bf16)
        fourth = dot(cd, third)
        p_ref[pl.ds(pl.multiple_of(i * bs, bs), bs), :] = fourth.astype(bf16)
        is_first = (ids_ref[1] == 0) & (i == 0)
        total = total + dot(cs, third) + fourth * jnp.where(is_first, 1.0, 0.0)
    u_ref[...] = total.astype(bf16)


def lead_rows_products(ids, second, gathered, lead, cb, tile):
    count, _ = second.shape
    blocks, bs, _ = cb.shape
    column = pl.BlockSpec((count, bs), lambda i, ids: (0, 0))
    square = pl.BlockSpec((bs, bs), lambda i, ids: (0, 0))
    return pl.pallas_call(
        lead_rows_body,
        grid_spec=pltpu.PrefetchScalarGridSpec(
            num_scalar_prefetch=1,
            grid=(1,),
            in_specs=[
                column,
                column,
                square,
                pl.BlockSpec(cb.shape, lambda i, ids: (0, 0, 0)),
                pl.BlockSpec(memory_space=pl.ANY),
            ],
            out_specs=[column, square],
        ),
        out_shape=[
            jax.ShapeDtypeStruct(tile.shape, bf16),
            jax.ShapeDtypeStruct((bs, bs), bf16),
        ],
        input_output_aliases={5: 0},
        cost_estimate=light,
        compiler_params=params("arbitrary"),
        name="lead_row_products",
    )(ids, second, gathered, lead, cb, tile)


def put_top_body(ids_ref, p_ref, lead_ref, rest_ref, o_ref):
    bs = lead_ref.shape[1]
    first = ids_ref[1] == 0

    @pl.when(first)
    def _():
        o_ref[:, :bs] = lead_ref[...]
        o_ref[:, bs:] = rest_ref[...]

    @pl.when(jnp.logical_not(first))
    def _():
        o_ref[...] = p_ref[...]


def put_top(ids, tile, lead, rest):
    bs = lead.shape[0]
    spec = lambda width: pl.BlockSpec((bs, width), lambda i, ids: (0, 0))
    top = spec(tile.shape[1])
    return pl.pallas_call(
        put_top_body,
        grid_spec=pltpu.PrefetchScalarGridSpec(
            num_scalar_prefetch=1,
            grid=(1,),
            in_specs=[top, spec(bs), spec(rest.shape[1])],
            out_specs=top,
        ),
        out_shape=jax.ShapeDtypeStruct(tile.shape, tile.dtype),
        input_output_aliases={1: 0},
        cost_estimate=light,
        compiler_params=params("arbitrary"),
        name="put_top",
    )(ids, tile, lead, rest)


def after(value, *earlier):
    return lax.optimization_barrier((value,) + earlier)[0]


def planned(acts, out_grads, token_counts, k_factor, c_factor, k_moment, c_moment, grad_weight):
    tok_dev, width = acts.shape
    ds, bs, _ = k_factor.shape
    shards = lax.axis_size("fsdp")
    xs = 2
    zs = shards // xs
    d = lax.axis_index("dp")
    s = lax.axis_index("fsdp")
    x = s % xs
    z = s // xs
    flat = lambda dd, ss: dd * shards + ss
    plane = [[flat(dd, zz * xs + xx) for dd in range(ds) for xx in range(xs)] for zz in range(zs)]
    flip_x = [(i, i ^ 1) for i in range(shards)]
    ids = jnp.stack([z, d, s * ds, s, jnp.int32(ds)]).astype(jnp.int32)
    token_total = jnp.sum(token_counts).astype(f32)
    valid = jnp.sum(jnp.where(lax.iota(jnp.int32, ds) == d, token_counts, 0))
    stat_scalars = (1.0 / token_total).reshape(1)
    limit = (valid - s * tok_dev).reshape(1).astype(jnp.int32)

    def along_z(value, k):
        pairs = [(zz * xs + xx, (zz ^ k) * xs + xx) for zz in range(zs) for xx in range(xs)]
        return lax.ppermute(value, "fsdp", pairs)

    def from_group_0(value):
        value = jnp.where(d == 0, value, lax.ppermute(value, "dp", [(0, 2)]))
        return jnp.where(d % 2 == 0, value, lax.ppermute(value, "dp", [(0, 1), (2, 3)]))

    def block_along_z(factor, *earlier):
        own = lax.dynamic_index_in_dim(factor, d, 0, keepdims=False)
        side_keep = jnp.where(s * ds + d > 0, 1.0, 0.0)
        own = jnp.concatenate([own[:, :bs], own[:, bs:] * side_keep], axis=1).astype(bf16)
        own = after(own, *earlier)
        return jnp.stack([own] + [along_z(own, k) for k in range(1, zs)])

    def mean_of(parts):
        total = parts[0].astype(f32)
        for part in parts[1:]:
            total = total + part.astype(f32)
        return (total / token_total).astype(bf16)

    def each_along_z(partial):
        return [partial[0]] + [along_z(partial[k], k) for k in range(1, zs)]

    def over_dp(value):
        pair = jnp.stack([value, lax.ppermute(value, "dp", [(i, i ^ 2) for i in range(ds)])])
        other = lax.ppermute(pair, "dp", [(i, i ^ 1) for i in range(ds)])
        return jnp.concatenate([pair, other], axis=0)

    def gram_part(factor):
        block_ids = s * ds + lax.iota(jnp.int32, ds)
        keep = (block_ids > 0).astype(f32)[:, None, None]
        side = factor[:, :, bs:] * keep
        return (jnp.sum(factor[:, :, :bs] ** 2) + jnp.sum(side * side)) / ds

    def exchange(packed):
        return lax.all_to_all(packed, both, 0, 0, tiled=True, axis_index_groups=plane)

    load = jnp.concatenate(
        [k_factor[0, :, :bs].astype(bf16), c_factor[0, :, :bs].astype(bf16), grad_weight[:, :bs]]
    )
    load_half = load.shape[0] // xs
    load_x = lax.ppermute(load[load_half:], "fsdp", [(0, 1)])

    def down_z(value, stride):
        pairs = [
            (zz * xs + xx, (zz + stride) * xs + xx)
            for zz in range(0, zs, 2 * stride)
            for xx in range(xs)
        ]
        return lax.ppermute(value, "fsdp", pairs)

    owned_k = exchange(pack(limit, acts, zs, xs, ds, bs))
    blocks_c = block_along_z(c_factor)
    packed_c = pack(limit, out_grads, zs, xs, ds, bs)
    gram_k = gram_part(k_factor)
    gram_c = gram_part(c_factor)
    packed_c, owned_k, blocks_c, gram_k, gram_c = lax.optimization_barrier(
        (packed_c, owned_k, blocks_c, gram_k, gram_c)
    )
    owned_c = exchange(packed_c)

    raw_k = raw_moments(ids, after(owned_k, load_x))
    sent_k = each_along_z(raw_k)
    stride = zs // 2
    mine = jnp.where(s == 0, load[:load_half], after(load_x, raw_k))
    while stride > 1:
        got = after(down_z(mine, stride), *sent_k)
        mine = jnp.where(z % (2 * stride) == 0, mine, got)
        stride //= 2
    last_z = down_z(mine, 1)

    stat_k, trace_k = image_stats(ids, stat_scalars, sent_k, k_factor)
    partial_c, square_c = stats(ids, after(owned_c, trace_k), blocks_c)
    rows8 = lax.broadcasted_iota(jnp.int32, (8, 128), 0)
    sums = jnp.where(
        rows8 == 0,
        trace_k,
        jnp.where(rows8 == 1, square_c, jnp.where(rows8 == 2, gram_k, gram_c)),
    )
    sent_c = each_along_z(partial_c)
    sums = jnp.broadcast_to(sums[None], (ds * shards, 8, 128))
    totals = jnp.sum(lax.all_to_all(sums, both, 0, 0, tiled=True), axis=0)[:, 0]
    for_k = jnp.stack([totals[1] / token_total, totals[3]])
    for_c = jnp.stack([totals[0], totals[2]])
    all_k = over_dp(after(stat_k, partial_c))
    mine = jnp.where(z % 2 == 0, mine, after(last_z, partial_c))
    other = lax.ppermute(mine, "fsdp", flip_x)
    load = jnp.concatenate([jnp.where(x == 0, mine, other), jnp.where(x == 0, other, mine)])
    lead_k, lead_c, grad_lead = load[:bs], load[bs : 2 * bs], load[2 * bs :]

    scale_width = float(width)
    k_factor_new, k_moment_new, kb = advance_all(
        scale_width, ids, for_k, all_k, k_factor, k_moment, lead_k
    )
    second, term = columns(ids, grad_weight, grad_lead, kb)
    count = grad_weight.shape[0]
    kept = lax.dynamic_slice_in_dim(term, x * (count // xs), count // xs, 0)
    passed = lax.dynamic_slice_in_dim(term, (1 - x) * (count // xs), count // xs, 0)
    passed = lax.ppermute(passed, "fsdp", flip_x)

    stat_c = mean_of([after(part, term) for part in sent_c])
    all_c = over_dp(stat_c)

    c_factor_new, c_moment_new, cb = advance_all(
        scale_width, ids, for_c, all_c, c_factor, c_moment, lead_c
    )
    halves = []
    for h in range(2):
        turn = 2 * h
        pairs = [
            (flat(r ^ turn, zz * xs + xx), flat(zz, r * xs + xx))
            for r in range(ds)
            for zz in range(zs)
            for xx in range(xs)
        ]
        halves.append(lax.ppermute(cb[h * (ds // 2) : (h + 1) * (ds // 2)], both, pairs))
    others = [lax.ppermute(h, "fsdp", flip_x) for h in halves]

    halved = (kept.astype(f32) + passed.astype(f32)).astype(bf16).reshape(zs, bs, bs)
    turned = [lax.dynamic_index_in_dim(halved, z ^ k, 0, keepdims=False) for k in range(zs)]
    got = [after(g, cb) for g in each_along_z(turned)]

    c_rows = jnp.concatenate(halves + others, axis=0)

    top_rest = from_group_0(second[:bs, bs:])

    block_sum = got[0].astype(f32)
    for g in got[1:]:
        block_sum = block_sum + g.astype(f32)
    block_sum = block_sum.astype(bf16)
    pair = jnp.stack([block_sum, lax.ppermute(block_sum, "fsdp", [(2 * k + 1, 2 * k) for k in range(zs)])])
    gathered = [pair] + [lax.ppermute(pair, "fsdp", [(xs * k, 0)]) for k in range(1, zs)]
    gathered = jnp.concatenate(gathered, axis=0).reshape(count, bs)
    top_lead = from_group_0(jnp.where(s == 0, block_sum, second[:bs, :bs]))
    def sum_to_group_0(value):
        total = value.astype(f32) + lax.ppermute(value, "dp", [(2, 0), (3, 1)]).astype(f32)
        other = lax.ppermute(total.astype(bf16), "dp", [(1, 0)])
        return (total + other.astype(f32)).astype(bf16)

    precond, up_rest = rows(ids, second, top_rest, c_rows)
    up_rest = sum_to_group_0(up_rest)
    precond, up_lead = lead_rows_products(ids, second, gathered, top_lead, c_rows, precond)
    precond = put_top(ids, precond, sum_to_group_0(up_lead), up_rest)
    return (k_factor_new, c_factor_new, k_moment_new, c_moment_new, precond)


def spread(value, axis, source):
    kept = jnp.where(lax.axis_index(axis) == source, value, 0).astype(value.dtype)
    return lax.psum(kept, axis)


def owner_image(columns, lead_columns, diag_half, side_half):
    row_count = columns.shape[0]
    block_count = diag_half.shape[0]
    block_size = diag_half.shape[1]
    blocked = columns.reshape(row_count, block_count, block_size)
    image_sum = jnp.einsum("tnk,nkj->tnj", blocked, diag_half, preferred_element_type=jnp.float32)
    image_sum = image_sum + jnp.einsum(
        "tk,nkj->tnj", lead_columns, side_half, preferred_element_type=jnp.float32
    )
    return image_sum.astype(jnp.bfloat16).reshape(row_count, block_count * block_size)


def to_owners(pair):
    return (
        lax.all_to_all(pair[0], "fsdp", split_axis=1, concat_axis=0, tiled=True),
        lax.all_to_all(pair[1], "fsdp", split_axis=1, concat_axis=0, tiled=True),
    )


def fetch_lead(before):
    return (
        lax.all_gather(before[0], "fsdp", axis=0, tiled=True),
        lax.all_gather(before[1], "fsdp", axis=0, tiled=True),
    )


def block_stats(owned, lead_image, block_count, block_size):
    blocked = owned.reshape(owned.shape[0], block_count, block_size)
    own_sum = jnp.einsum("tni,tnj->nij", blocked, blocked, preferred_element_type=jnp.float32)
    cross_sum = jnp.einsum("ti,tnj->nij", lead_image, blocked, preferred_element_type=jnp.float32)
    return (own_sum, cross_sum)


def gram_trace(factor, border_keep):
    block_size = factor.shape[1]
    diag_part = factor[:, :, :block_size]
    side_part = factor[:, :, block_size:] * border_keep
    return jnp.sum(diag_part * diag_part) + jnp.sum(side_part * side_part)


def advance(factor, moment, own_sum, cross_sum, lead_block, border_keep, other_h, other_g, width):
    block_size = factor.shape[1]
    diag_part = factor[:, :, :block_size]
    side_part = factor[:, :, block_size:] * border_keep
    gram_diag = jnp.einsum("nki,nkj->nij", diag_part, diag_part, precision=highest)
    gram_diag = gram_diag + jnp.einsum("nki,nkj->nij", side_part, side_part, precision=highest)
    gram_side = jnp.einsum("ki,nkj->nij", lead_block, side_part, precision=highest)
    identity = jnp.eye(block_size, dtype=jnp.float32)
    fresh_diag = (other_h * own_sum + damping * other_g * gram_diag - width * identity) / (
        2.0 * width
    )
    fresh_side = (other_h * cross_sum + damping * other_g * gram_side) * border_keep / (2.0 * width)
    moment_diag = momentum_rate * moment[:, :, :block_size] + fresh_diag
    moment_side = (momentum_rate * moment[:, :, block_size:] + fresh_side) * border_keep
    new_diag = diag_part - step_rate * jnp.einsum(
        "nik,nkj->nij", diag_part, moment_diag, precision=highest
    )
    side_change = jnp.einsum("ik,nkj->nij", lead_block, moment_side, precision=highest)
    side_change = side_change + jnp.einsum(
        "nik,nkj->nij", side_part, moment_diag, precision=highest
    )
    new_side = (side_part - step_rate * side_change) * border_keep
    return (
        jnp.concatenate([new_diag, new_side], axis=-1),
        jnp.concatenate([moment_diag, moment_side], axis=-1),
    )


def general(acts, out_grads, token_counts, k_factor, c_factor, k_moment, c_moment, grad_weight):
    tok_dev, width = acts.shape
    blocks_dev = k_factor.shape[0]
    block_size = k_factor.shape[1]
    group_count = lax.axis_size("dp")
    shard_count = lax.axis_size("fsdp")
    group_id = lax.axis_index("dp")
    shard_id = lax.axis_index("fsdp")
    token_total = jnp.sum(token_counts).astype(jnp.float32)
    valid_limit = jnp.sum(jnp.where(lax.iota(jnp.int32, group_count) == group_id, token_counts, 0))
    positions = shard_id * tok_dev + lax.iota(jnp.int32, tok_dev)
    row_keep = (positions < valid_limit).astype(jnp.bfloat16)[:, None]
    masked_acts = acts * row_keep
    masked_grads = out_grads * row_keep
    block_ids = shard_id * blocks_dev + lax.iota(jnp.int32, blocks_dev)
    border_keep = (block_ids > 0).astype(jnp.float32)[:, None, None]
    lead_k, lead_c = (
        spread(k_factor[0, :, :block_size], "fsdp", 0),
        spread(c_factor[0, :, :block_size], "fsdp", 0),
    )
    raw_acts, raw_grads = to_owners((masked_acts, masked_grads))
    lead_raw_acts, lead_raw_grads = fetch_lead(
        (masked_acts[:, :block_size], masked_grads[:, :block_size])
    )
    k_diag_half = k_factor[:, :, :block_size].astype(jnp.bfloat16)
    k_side_half = (k_factor[:, :, block_size:] * border_keep).astype(jnp.bfloat16)
    c_diag_half = c_factor[:, :, :block_size].astype(jnp.bfloat16)
    c_side_half = (c_factor[:, :, block_size:] * border_keep).astype(jnp.bfloat16)
    owned_acts = owner_image(raw_acts, lead_raw_acts, k_diag_half, k_side_half)
    owned_grads = owner_image(raw_grads, lead_raw_grads, c_diag_half, c_side_half)
    lead_acts = jnp.dot(
        lead_raw_acts, lead_k.astype(jnp.bfloat16), preferred_element_type=jnp.float32
    ).astype(jnp.bfloat16)
    lead_grads = jnp.dot(
        lead_raw_grads, lead_c.astype(jnp.bfloat16), preferred_element_type=jnp.float32
    ).astype(jnp.bfloat16)
    own_k, cross_k = block_stats(owned_acts, lead_acts, blocks_dev, block_size)
    own_c, cross_c = block_stats(owned_grads, lead_grads, blocks_dev, block_size)
    summed = lax.psum((own_k, cross_k, own_c, cross_c), "dp")
    gram_k = gram_trace(k_factor, border_keep)
    gram_c = gram_trace(c_factor, border_keep)
    local_traces = jnp.stack(
        [
            jnp.sum(jnp.trace(summed[0], axis1=1, axis2=2)),
            jnp.sum(jnp.trace(summed[2], axis1=1, axis2=2)),
            gram_k,
            gram_c,
        ]
    )
    totals = lax.psum(local_traces, "fsdp")
    trace_hk = totals[0] / token_total
    trace_hc = totals[1] / token_total
    scale_width = float(width)
    k_factor_new, k_moment_new = advance(
        k_factor,
        k_moment,
        summed[0] / token_total,
        summed[1] / token_total,
        lead_k,
        border_keep,
        trace_hc,
        totals[3],
        scale_width,
    )
    c_factor_new, c_moment_new = advance(
        c_factor,
        c_moment,
        summed[2] / token_total,
        summed[3] / token_total,
        lead_c,
        border_keep,
        trace_hk,
        totals[2],
        scale_width,
    )
    grad_rows = grad_weight.shape[0]
    grad_lead = spread(grad_weight[:, :block_size], "fsdp", 0)
    k_diag = k_factor_new[:, :, :block_size].astype(jnp.bfloat16)
    k_side = k_factor_new[:, :, block_size:].astype(jnp.bfloat16)
    grad_blocked = grad_weight.reshape(grad_rows, blocks_dev, block_size)
    first_sum = jnp.einsum("rnk,nkj->rnj", grad_blocked, k_diag, preferred_element_type=jnp.float32)
    first_sum = first_sum + jnp.einsum(
        "rk,nkj->rnj", grad_lead, k_side, preferred_element_type=jnp.float32
    )
    first_product = first_sum.astype(jnp.bfloat16)
    own_second = jnp.einsum(
        "rnk,njk->rnj", first_product, k_diag, preferred_element_type=jnp.float32
    )
    lead_term = jnp.einsum("rnk,njk->rj", first_product, k_side, preferred_element_type=jnp.float32)
    lead_sum = lax.psum(lead_term, "fsdp")
    lead_mask = (block_ids == 0).astype(jnp.float32)[None, :, None]
    second_product = (own_second + lead_mask * lead_sum[:, None, :]).astype(jnp.bfloat16)
    row_blocks = grad_rows // block_size
    owner_count = shard_count // group_count
    c_half = c_factor_new.astype(jnp.bfloat16)
    fetched = []
    for owner_step in range(owner_count):
        fetched.append(spread(c_half, "fsdp", group_id * owner_count + owner_step))
    row_factor = jnp.concatenate(fetched, axis=0)
    c_diag = row_factor[:, :, :block_size]
    c_side = row_factor[:, :, block_size:]
    by_rows = second_product.reshape(row_blocks, block_size, blocks_dev * block_size)
    lead_rows = spread(by_rows[0], "dp", 0)
    third_sum = jnp.einsum("nki,nkc->nic", c_diag, by_rows, preferred_element_type=jnp.float32)
    third_sum = third_sum + jnp.einsum(
        "nki,kc->nic", c_side, lead_rows, preferred_element_type=jnp.float32
    )
    third_product = third_sum.astype(jnp.bfloat16)
    own_fourth = jnp.einsum(
        "nik,nkc->nic", c_diag, third_product, preferred_element_type=jnp.float32
    )
    row_term = jnp.einsum("nik,nkc->ic", c_side, third_product, preferred_element_type=jnp.float32)
    row_sum = lax.psum(row_term, "dp")
    row_ids = group_id * row_blocks + lax.iota(jnp.int32, row_blocks)
    row_mask = (row_ids == 0).astype(jnp.float32)[:, None, None]
    precond = (
        (own_fourth + row_mask * row_sum[None, :, :])
        .astype(jnp.bfloat16)
        .reshape(grad_rows, blocks_dev * block_size)
    )
    return (k_factor_new, c_factor_new, k_moment_new, c_moment_new, precond)


def per_device(*args):
    blocks = args[3].shape[0]
    groups, shards = lax.axis_size("dp"), lax.axis_size("fsdp")
    fits = blocks == 4 and groups == 4 and shards == 8
    return (planned if fits else general)(*args)


def solution(mesh):
    in_specs = (
        P(("dp", "fsdp"), None),
        P(("dp", "fsdp"), None),
        P(),
        P("fsdp", None, None),
        P("fsdp", None, None),
        P("fsdp", None, None),
        P("fsdp", None, None),
        P("dp", "fsdp"),
    )
    out_specs = (
        P("fsdp", None, None),
        P("fsdp", None, None),
        P("fsdp", None, None),
        P("fsdp", None, None),
        P("dp", "fsdp"),
    )
    return jax.shard_map(
        per_device, mesh=mesh, in_specs=in_specs, out_specs=out_specs, check_vma=False
    )
```

```python
import functools

import jax
import jax.numpy as jnp
from jax import lax
from jax.experimental import pallas as pl
from jax.experimental.pallas import tpu as pltpu
from jax.sharding import PartitionSpec as P

damping = 0.1
momentum_rate = 0.5
step_rate = 0.2
highest = lax.Precision.HIGHEST
both = ("dp", "fsdp")
f32 = jnp.float32
bf16 = jnp.bfloat16
vmem_cap = 48 * 1024 * 1024


def params(*semantics):
    return pltpu.CompilerParams(dimension_semantics=semantics, vmem_limit_bytes=vmem_cap)


light = pl.CostEstimate(flops=1, transcendentals=0, bytes_accessed=1)


def dot(a, b, dims=((1,), (0,)), precision=None):
    return lax.dot_general(a, b, (dims, ((), ())), precision=precision, preferred_element_type=f32)


nn = ((1,), (0,))
tn = ((0,), (0,))
nt = ((1,), (1,))


def pack_body(zs, xs, ds, bs, tile, lim_ref, a_ref, o_ref):
    rows = pl.program_id(0) * tile + lax.broadcasted_iota(jnp.int32, (tile, bs), 0)
    keep = jnp.where(rows < lim_ref[0], 1.0, 0.0).astype(bf16)
    lead = a_ref[:, :bs] * keep
    for d in range(ds):
        for x in range(xs):
            for z in range(zs):
                n = (z * xs + x) * ds + d
                o_ref[d * xs + x, z] = a_ref[:, n * bs : (n + 1) * bs] * keep
            o_ref[d * xs + x, zs] = lead


def pack(limit, tokens, zs, xs, ds, bs):
    count, width = tokens.shape
    tile = 32
    return pl.pallas_call(
        functools.partial(pack_body, zs, xs, ds, bs, tile),
        grid=(count // tile,),
        in_specs=[
            pl.BlockSpec(memory_space=pltpu.SMEM),
            pl.BlockSpec((tile, width), lambda i: (i, 0)),
        ],
        out_specs=pl.BlockSpec((ds * xs, zs + 1, tile, bs), lambda i: (0, 0, i, 0)),
        out_shape=jax.ShapeDtypeStruct((ds * xs, zs + 1, count, bs), bf16),
        cost_estimate=light,
        compiler_params=params("arbitrary"),
        name="pack_tokens",
    )(limit, tokens)


def moments_body(ids_ref, x_ref, l_ref, o_ref):
    groups, _, count, bs = x_ref.shape
    cols = x_ref[:, 0].reshape(groups * count, bs)
    lead = l_ref[:, 0].reshape(groups * count, bs)
    o_ref[0, 0] = dot(cols, cols, tn).astype(bf16)
    o_ref[0, 1] = dot(lead, cols, tn).astype(bf16)
    o_ref[0, 2] = dot(lead, lead, tn).astype(bf16)


def raw_moments(ids, owned):
    groups, slots, count, bs = owned.shape
    zs = slots - 1
    return pl.pallas_call(
        moments_body,
        grid_spec=pltpu.PrefetchScalarGridSpec(
            num_scalar_prefetch=1,
            grid=(zs,),
            in_specs=[
                pl.BlockSpec((groups, 1, count, bs), lambda k, ids: (0, ids[0] ^ k, 0, 0)),
                pl.BlockSpec((groups, 1, count, bs), lambda k, ids: (0, zs, 0, 0)),
            ],
            out_specs=pl.BlockSpec((1, 3, bs, bs), lambda k, ids: (k, 0, 0, 0)),
        ),
        out_shape=jax.ShapeDtypeStruct((zs, 3, bs, bs), bf16),
        cost_estimate=light,
        compiler_params=params("arbitrary"),
        name="raw_moments",
    )(ids, owned, owned)


def image_stats_body(count, ids_ref, sc_ref, *refs):
    parts = refs[:count]
    fac_ref, h_ref, tr_ref = refs[count:]
    bs = fac_ref.shape[1]
    keep = jnp.where(ids_ref[2] + ids_ref[1] > 0, 1.0, 0.0)
    total = parts[0][...].astype(f32)
    for part in parts[1:]:
        total = total + part[...].astype(f32)
    fac = fac_ref[0]
    bn = fac[:, :bs].astype(bf16).astype(f32)
    pn = (fac[:, bs:] * keep).astype(bf16).astype(f32)
    mm = functools.partial(dot, precision=highest)
    t1 = mm(total[0], bn) + mm(total[1], pn, tn)
    t0 = mm(total[1], bn) + mm(total[2], pn)
    own = (mm(bn, t1, tn) + mm(pn, t0, tn)) * sc_ref[0]
    h_ref[0] = own.astype(bf16)
    h_ref[1] = (t0 * sc_ref[0]).astype(bf16)
    row = lax.broadcasted_iota(jnp.int32, (bs, bs), 0)
    col = lax.broadcasted_iota(jnp.int32, (bs, bs), 1)
    tr_ref[...] = jnp.zeros_like(tr_ref) + jnp.sum(jnp.where(row == col, own, 0.0))


def image_stats(ids, scalars, parts, factor):
    _, bs, wide = factor.shape
    whole = lambda shape: pl.BlockSpec(shape, lambda i, ids: (0,) * len(shape))
    return pl.pallas_call(
        functools.partial(image_stats_body, len(parts)),
        grid_spec=pltpu.PrefetchScalarGridSpec(
            num_scalar_prefetch=1,
            grid=(1,),
            in_specs=[pl.BlockSpec(memory_space=pltpu.SMEM)]
            + [whole((3, bs, bs)) for _ in parts]
            + [pl.BlockSpec((1, bs, wide), lambda i, ids: (ids[1], 0, 0))],
            out_specs=[whole((2, bs, bs)), whole((8, 128))],
        ),
        out_shape=[
            jax.ShapeDtypeStruct((2, bs, bs), bf16),
            jax.ShapeDtypeStruct((8, 128), f32),
        ],
        cost_estimate=light,
        compiler_params=params("arbitrary"),
        name="image_stats",
    )(ids, scalars, *parts, factor)


def stats_body(x_ref, l_ref, f_ref, o_ref, t_ref):
    groups, _, count, bs = x_ref.shape
    k = pl.program_id(0)
    cols = x_ref[:, 0].reshape(groups * count, bs)
    lead = l_ref[:, 0].reshape(groups * count, bs)

    @pl.when(k == 0)
    def _():
        t_ref[...] = jnp.zeros_like(t_ref)

    image = (dot(cols, f_ref[0, :, :bs]) + dot(lead, f_ref[0, :, bs:])).astype(bf16)
    o_ref[0, 0] = dot(image, image, tn).astype(bf16)
    o_ref[0, 1] = dot(lead, image, tn).astype(bf16)
    wide = image.astype(f32)
    t_ref[...] = t_ref[...] + jnp.sum(wide * wide)


def stats(ids, owned, blocks):
    groups, slots, count, bs = owned.shape
    zs = slots - 1

    def body(ids_ref, *refs):
        stats_body(*refs)

    return pl.pallas_call(
        body,
        grid_spec=pltpu.PrefetchScalarGridSpec(
            num_scalar_prefetch=1,
            grid=(zs,),
            in_specs=[
                pl.BlockSpec((groups, 1, count, bs), lambda k, ids: (0, ids[0] ^ k, 0, 0)),
                pl.BlockSpec((groups, 1, count, bs), lambda k, ids: (0, zs, 0, 0)),
                pl.BlockSpec((1, bs, 2 * bs), lambda k, ids: (k, 0, 0)),
            ],
            out_specs=[
                pl.BlockSpec((1, 2, bs, bs), lambda k, ids: (k, 0, 0, 0)),
                pl.BlockSpec((8, 128), lambda k, ids: (0, 0)),
            ],
        ),
        out_shape=[
            jax.ShapeDtypeStruct((zs, 2, bs, bs), bf16),
            jax.ShapeDtypeStruct((8, 128), f32),
        ],
        cost_estimate=light,
        compiler_params=params("arbitrary"),
        name="plane_stats",
    )(ids, owned, owned, blocks)


def advance_block(width, own, cross, fac, mom, b0, other_h, other_g, keep):
    bs = fac.shape[0]
    diag = fac[:, :bs]
    side = fac[:, bs:] * keep
    db = diag.astype(bf16)
    sb = side.astype(bf16)
    gram_d = dot(db, db, tn) + dot(sb, sb, tn)
    gram_s = dot(b0, sb, tn)
    row = lax.broadcasted_iota(jnp.int32, (bs, bs), 0)
    col = lax.broadcasted_iota(jnp.int32, (bs, bs), 1)
    ident = jnp.where(row == col, width, 0.0)
    scale = 1.0 / (2.0 * width)
    md = momentum_rate * mom[:, :bs] + (other_h * own + damping * other_g * gram_d - ident) * scale
    ms = momentum_rate * mom[:, bs:] + (other_h * cross + damping * other_g * gram_s) * scale
    ms = ms * keep
    mdb = md.astype(bf16)
    new_d = diag - step_rate * dot(db, mdb)
    new_s = side - step_rate * (dot(b0, ms.astype(bf16)) + dot(sb, mdb)) * keep
    return md, ms, new_d, new_s


def order_of(ids, m):
    return ids[1] ^ ((m & 1) * 2 + (m >> 1))


def advance_body(width, ids_ref, sc_ref, h_ref, fac_ref, mom_ref, lead_ref, fn_ref, mn_ref, fb_ref):
    bs = lead_ref.shape[0]
    j = order_of(ids_ref, pl.program_id(0))
    keep = jnp.where(ids_ref[2] + j > 0, 1.0, 0.0)
    md, ms, new_d, new_s = advance_block(
        width,
        h_ref[0, 0].astype(f32),
        dot(lead_ref[...], h_ref[0, 1], tn),
        fac_ref[0],
        mom_ref[0],
        lead_ref[...],
        sc_ref[0],
        sc_ref[1],
        keep,
    )
    fn_ref[0, :, :bs] = new_d
    fn_ref[0, :, bs:] = new_s
    mn_ref[0, :, :bs] = md
    mn_ref[0, :, bs:] = ms
    fb_ref[0, :, :bs] = new_d.astype(bf16)
    fb_ref[0, :, bs:] = new_s.astype(bf16)


def advance_all(width, ids, scalars, stats, factor, moment, lead):
    blocks, bs, wide = factor.shape
    spec = pl.BlockSpec((1, bs, wide), lambda m, ids: (order_of(ids, m), 0, 0))
    return pl.pallas_call(
        functools.partial(advance_body, width),
        grid_spec=pltpu.PrefetchScalarGridSpec(
            num_scalar_prefetch=1,
            grid=(blocks,),
            in_specs=[
                pl.BlockSpec(memory_space=pltpu.SMEM),
                pl.BlockSpec((1, 2, bs, bs), lambda m, ids: (m, 0, 0, 0)),
                spec,
                spec,
                pl.BlockSpec((bs, bs), lambda m, ids: (0, 0)),
            ],
            out_specs=[spec, spec, spec],
        ),
        out_shape=[
            jax.ShapeDtypeStruct(factor.shape, f32),
            jax.ShapeDtypeStruct(factor.shape, f32),
            jax.ShapeDtypeStruct(factor.shape, bf16),
        ],
        cost_estimate=light,
        compiler_params=params("arbitrary"),
        name="advance_all",
    )(ids, scalars, stats, factor, moment, lead)


def columns_body(ids_ref, g_ref, l_ref, k_ref, s_ref, t_ref):
    blocks, bs, _ = k_ref.shape
    lead = l_ref[...]
    term = None
    for n in range(blocks):
        kd = k_ref[n, :, :bs]
        ks = k_ref[n, :, bs:]
        first = (dot(g_ref[:, n * bs : (n + 1) * bs], kd) + dot(lead, ks)).astype(bf16)
        second = dot(first, kd, nt)
        s_ref[:, n * bs : (n + 1) * bs] = second.astype(bf16)
        part = dot(first, ks, nt)
        if n == 0:
            part = part + second * jnp.where(ids_ref[2] == 0, 1.0, 0.0)
        term = part if term is None else term + part
    t_ref[...] = term.astype(bf16)


def columns(ids, grad, lead, kb):
    rows, wide = grad.shape
    blocks, bs, _ = kb.shape
    tile = 512
    return pl.pallas_call(
        columns_body,
        grid_spec=pltpu.PrefetchScalarGridSpec(
            num_scalar_prefetch=1,
            grid=(rows // tile,),
            in_specs=[
                pl.BlockSpec((tile, wide), lambda i, ids: (i, 0)),
                pl.BlockSpec((tile, bs), lambda i, ids: (i, 0)),
                pl.BlockSpec(kb.shape, lambda i, ids: (0, 0, 0)),
            ],
            out_specs=[
                pl.BlockSpec((tile, wide), lambda i, ids: (i, 0)),
                pl.BlockSpec((tile, bs), lambda i, ids: (i, 0)),
            ],
        ),
        out_shape=[
            jax.ShapeDtypeStruct((rows, wide), bf16),
            jax.ShapeDtypeStruct((rows, bs), bf16),
        ],
        cost_estimate=light,
        compiler_params=params("arbitrary"),
        name="column_products",
    )(ids, grad, lead, kb)


def row_of(ids, k):
    per = ids[4]
    return ((ids[3] & 1) ^ (k // per)) * per + k % per


def gathered_at(ids, k):
    i = row_of(ids, k)
    return (i % ids[4]) * 2 + i // ids[4]


def rows_body(ids_ref, s_ref, l_ref, c_ref, p_ref, u_ref, acc_ref):
    k = pl.program_id(0)
    bs = c_ref.shape[1]
    cd = c_ref[0, :, :bs]
    cs = c_ref[0, :, bs:]
    third = (dot(cd, s_ref[:, bs:], tn) + dot(cs, l_ref[...], tn)).astype(bf16)
    fourth = dot(cd, third)
    p_ref[:, bs:] = fourth.astype(bf16)
    is_first = (ids_ref[1] == 0) & (row_of(ids_ref, k) == 0)
    term = dot(cs, third) + fourth * jnp.where(is_first, 1.0, 0.0)

    @pl.when(k == 0)
    def _():
        acc_ref[...] = term

    @pl.when(k > 0)
    def _():
        acc_ref[...] = acc_ref[...] + term

    @pl.when(k == pl.num_programs(0) - 1)
    def _():
        u_ref[...] = acc_ref[...].astype(bf16)


def rows(ids, second, lead, cb):
    count, wide = second.shape
    blocks, bs, _ = cb.shape
    rest = wide - bs
    spec = pl.BlockSpec((bs, wide), lambda k, ids: (row_of(ids, k), 0))
    whole = pl.BlockSpec((bs, rest), lambda k, ids: (0, 0))
    return pl.pallas_call(
        rows_body,
        grid_spec=pltpu.PrefetchScalarGridSpec(
            num_scalar_prefetch=1,
            grid=(blocks,),
            in_specs=[
                spec,
                whole,
                pl.BlockSpec((1, bs, 2 * bs), lambda k, ids: (k, 0, 0)),
            ],
            out_specs=[spec, whole],
            scratch_shapes=[pltpu.VMEM((bs, rest), f32)],
        ),
        out_shape=[
            jax.ShapeDtypeStruct((count, wide), bf16),
            jax.ShapeDtypeStruct((bs, rest), bf16),
        ],
        cost_estimate=light,
        compiler_params=params("arbitrary"),
        name="row_products",
    )(ids, second, lead, cb)


def lead_rows_body(ids_ref, s_ref, g_ref, l_ref, c_ref, _, p_ref, u_ref):
    blocks, bs, _ = c_ref.shape
    total = jnp.zeros((bs, bs), f32)
    for k in range(blocks):
        i = row_of(ids_ref, k)
        own = s_ref[pl.ds(pl.multiple_of(i * bs, bs), bs), :]
        whole = g_ref[pl.ds(pl.multiple_of(gathered_at(ids_ref, k) * bs, bs), bs), :]
        second = jnp.where(ids_ref[3] == 0, whole, own)
        cd = c_ref[k, :, :bs]
        cs = c_ref[k, :, bs:]
        third = (dot(cd, second, tn) + dot(cs, l_ref[...], tn)).astype(bf16)
        fourth = dot(cd, third)
        p_ref[pl.ds(pl.multiple_of(i * bs, bs), bs), :] = fourth.astype(bf16)
        is_first = (ids_ref[1] == 0) & (i == 0)
        total = total + dot(cs, third) + fourth * jnp.where(is_first, 1.0, 0.0)
    u_ref[...] = total.astype(bf16)


def lead_rows_products(ids, second, gathered, lead, cb, tile):
    count, _ = second.shape
    blocks, bs, _ = cb.shape
    column = pl.BlockSpec((count, bs), lambda i, ids: (0, 0))
    square = pl.BlockSpec((bs, bs), lambda i, ids: (0, 0))
    return pl.pallas_call(
        lead_rows_body,
        grid_spec=pltpu.PrefetchScalarGridSpec(
            num_scalar_prefetch=1,
            grid=(1,),
            in_specs=[
                column,
                column,
                square,
                pl.BlockSpec(cb.shape, lambda i, ids: (0, 0, 0)),
                pl.BlockSpec(memory_space=pl.ANY),
            ],
            out_specs=[column, square],
        ),
        out_shape=[
            jax.ShapeDtypeStruct(tile.shape, bf16),
            jax.ShapeDtypeStruct((bs, bs), bf16),
        ],
        input_output_aliases={5: 0},
        cost_estimate=light,
        compiler_params=params("arbitrary"),
        name="lead_row_products",
    )(ids, second, gathered, lead, cb, tile)


def put_top_body(ids_ref, p_ref, lead_ref, rest_ref, o_ref):
    bs = lead_ref.shape[1]
    first = ids_ref[1] == 0

    @pl.when(first)
    def _():
        o_ref[:, :bs] = lead_ref[...]
        o_ref[:, bs:] = rest_ref[...]

    @pl.when(jnp.logical_not(first))
    def _():
        o_ref[...] = p_ref[...]


def put_top(ids, tile, lead, rest):
    bs = lead.shape[0]
    spec = lambda width: pl.BlockSpec((bs, width), lambda i, ids: (0, 0))
    top = spec(tile.shape[1])
    return pl.pallas_call(
        put_top_body,
        grid_spec=pltpu.PrefetchScalarGridSpec(
            num_scalar_prefetch=1,
            grid=(1,),
            in_specs=[top, spec(bs), spec(rest.shape[1])],
            out_specs=top,
        ),
        out_shape=jax.ShapeDtypeStruct(tile.shape, tile.dtype),
        input_output_aliases={1: 0},
        cost_estimate=light,
        compiler_params=params("arbitrary"),
        name="put_top",
    )(ids, tile, lead, rest)


def after(value, *earlier):
    return lax.optimization_barrier((value,) + earlier)[0]


def planned(acts, out_grads, token_counts, k_factor, c_factor, k_moment, c_moment, grad_weight):
    tok_dev, width = acts.shape
    ds, bs, _ = k_factor.shape
    shards = lax.axis_size("fsdp")
    xs = 2
    zs = shards // xs
    d = lax.axis_index("dp")
    s = lax.axis_index("fsdp")
    x = s % xs
    z = s // xs
    flat = lambda dd, ss: dd * shards + ss
    plane = [[flat(dd, zz * xs + xx) for dd in range(ds) for xx in range(xs)] for zz in range(zs)]
    flip_x = [(i, i ^ 1) for i in range(shards)]
    ids = jnp.stack([z, d, s * ds, s, jnp.int32(ds)]).astype(jnp.int32)
    token_total = jnp.sum(token_counts).astype(f32)
    valid = jnp.sum(jnp.where(lax.iota(jnp.int32, ds) == d, token_counts, 0))
    stat_scalars = (1.0 / token_total).reshape(1)
    limit = (valid - s * tok_dev).reshape(1).astype(jnp.int32)

    def along_z(value, k):
        pairs = [(zz * xs + xx, (zz ^ k) * xs + xx) for zz in range(zs) for xx in range(xs)]
        return lax.ppermute(value, "fsdp", pairs)

    def from_group_0(value):
        value = jnp.where(d == 0, value, lax.ppermute(value, "dp", [(0, 2)]))
        return jnp.where(d % 2 == 0, value, lax.ppermute(value, "dp", [(0, 1), (2, 3)]))

    def block_along_z(factor, *earlier):
        own = lax.dynamic_index_in_dim(factor, d, 0, keepdims=False)
        side_keep = jnp.where(s * ds + d > 0, 1.0, 0.0)
        own = jnp.concatenate([own[:, :bs], own[:, bs:] * side_keep], axis=1).astype(bf16)
        own = after(own, *earlier)
        return jnp.stack([own] + [along_z(own, k) for k in range(1, zs)])

    def mean_of(parts):
        total = parts[0].astype(f32)
        for part in parts[1:]:
            total = total + part.astype(f32)
        return (total / token_total).astype(bf16)

    def each_along_z(partial):
        return [partial[0]] + [along_z(partial[k], k) for k in range(1, zs)]

    def over_dp(value):
        pair = jnp.stack([value, lax.ppermute(value, "dp", [(i, i ^ 2) for i in range(ds)])])
        other = lax.ppermute(pair, "dp", [(i, i ^ 1) for i in range(ds)])
        return jnp.concatenate([pair, other], axis=0)

    def gram_part(factor):
        block_ids = s * ds + lax.iota(jnp.int32, ds)
        keep = (block_ids > 0).astype(f32)[:, None, None]
        side = factor[:, :, bs:] * keep
        return (jnp.sum(factor[:, :, :bs] ** 2) + jnp.sum(side * side)) / ds

    def exchange(packed):
        return lax.all_to_all(packed, both, 0, 0, tiled=True, axis_index_groups=plane)

    load = jnp.concatenate(
        [k_factor[0, :, :bs].astype(bf16), c_factor[0, :, :bs].astype(bf16), grad_weight[:, :bs]]
    )
    load_half = load.shape[0] // xs
    load_x = lax.ppermute(load[load_half:], "fsdp", [(0, 1)])

    def down_z(value, stride):
        pairs = [
            (zz * xs + xx, (zz + stride) * xs + xx)
            for zz in range(0, zs, 2 * stride)
            for xx in range(xs)
        ]
        return lax.ppermute(value, "fsdp", pairs)

    owned_k = exchange(pack(limit, acts, zs, xs, ds, bs))
    blocks_c = block_along_z(c_factor)
    packed_c = pack(limit, out_grads, zs, xs, ds, bs)
    gram_k = gram_part(k_factor)
    gram_c = gram_part(c_factor)
    packed_c, owned_k, blocks_c, gram_k, gram_c = lax.optimization_barrier(
        (packed_c, owned_k, blocks_c, gram_k, gram_c)
    )
    owned_c = exchange(packed_c)

    raw_k = raw_moments(ids, owned_k)
    sent_k = each_along_z(raw_k)
    stride = zs // 2
    mine = jnp.where(s == 0, load[:load_half], after(load_x, *sent_k))
    while stride > 1:
        got = down_z(mine, stride)
        mine = jnp.where(z % (2 * stride) == 0, mine, got)
        stride //= 2
    last_z = down_z(mine, 1)

    stat_k, trace_k = image_stats(ids, stat_scalars, sent_k, k_factor)
    partial_c, square_c = stats(ids, after(owned_c, trace_k), blocks_c)
    rows8 = lax.broadcasted_iota(jnp.int32, (8, 128), 0)
    sums = jnp.where(
        rows8 == 0,
        trace_k,
        jnp.where(rows8 == 1, square_c, jnp.where(rows8 == 2, gram_k, gram_c)),
    )
    sent_c = each_along_z(partial_c)
    sums = jnp.broadcast_to(sums[None], (ds * shards, 8, 128))
    totals = jnp.sum(lax.all_to_all(sums, both, 0, 0, tiled=True), axis=0)[:, 0]
    for_k = jnp.stack([totals[1] / token_total, totals[3]])
    for_c = jnp.stack([totals[0], totals[2]])
    all_k = over_dp(after(stat_k, partial_c))
    mine = jnp.where(z % 2 == 0, mine, after(last_z, partial_c))
    other = lax.ppermute(mine, "fsdp", flip_x)
    load = jnp.concatenate([jnp.where(x == 0, mine, other), jnp.where(x == 0, other, mine)])
    lead_k, lead_c, grad_lead = load[:bs], load[bs : 2 * bs], load[2 * bs :]

    scale_width = float(width)
    k_factor_new, k_moment_new, kb = advance_all(
        scale_width, ids, for_k, all_k, k_factor, k_moment, lead_k
    )
    second, term = columns(ids, grad_weight, grad_lead, kb)
    count = grad_weight.shape[0]
    kept = lax.dynamic_slice_in_dim(term, x * (count // xs), count // xs, 0)
    passed = lax.dynamic_slice_in_dim(term, (1 - x) * (count // xs), count // xs, 0)
    passed = lax.ppermute(passed, "fsdp", flip_x)

    stat_c = mean_of([after(part, term) for part in sent_c])
    all_c = over_dp(stat_c)

    c_factor_new, c_moment_new, cb = advance_all(
        scale_width, ids, for_c, all_c, c_factor, c_moment, lead_c
    )
    halves = []
    for h in range(2):
        turn = 2 * h
        pairs = [
            (flat(r ^ turn, zz * xs + xx), flat(zz, r * xs + xx))
            for r in range(ds)
            for zz in range(zs)
            for xx in range(xs)
        ]
        halves.append(lax.ppermute(cb[h * (ds // 2) : (h + 1) * (ds // 2)], both, pairs))
    others = [lax.ppermute(h, "fsdp", flip_x) for h in halves]

    halved = (kept.astype(f32) + passed.astype(f32)).astype(bf16).reshape(zs, bs, bs)
    turned = [lax.dynamic_index_in_dim(halved, z ^ k, 0, keepdims=False) for k in range(zs)]
    got = [after(g, cb) for g in each_along_z(turned)]

    c_rows = jnp.concatenate(halves + others, axis=0)

    top_rest = from_group_0(second[:bs, bs:])

    block_sum = got[0].astype(f32)
    for g in got[1:]:
        block_sum = block_sum + g.astype(f32)
    block_sum = block_sum.astype(bf16)
    pair = jnp.stack([block_sum, lax.ppermute(block_sum, "fsdp", [(2 * k + 1, 2 * k) for k in range(zs)])])
    gathered = [pair] + [lax.ppermute(pair, "fsdp", [(xs * k, 0)]) for k in range(1, zs)]
    top_lead = jnp.where(s == 0, block_sum, second[:bs, :bs])
    top_lead = from_group_0(after(top_lead, halves[0]))
    def sum_to_group_0(value):
        total = value.astype(f32) + lax.ppermute(value, "dp", [(2, 0), (3, 1)]).astype(f32)
        other = lax.ppermute(total.astype(bf16), "dp", [(1, 0)])
        return (total + other.astype(f32)).astype(bf16)

    precond, up_rest = rows(ids, second, top_rest, c_rows)
    gathered = [after(g, up_rest) for g in gathered]
    gathered = jnp.concatenate(gathered, axis=0).reshape(count, bs)
    up_rest = sum_to_group_0(up_rest)
    precond, up_lead = lead_rows_products(ids, second, gathered, top_lead, c_rows, precond)
    precond = put_top(ids, precond, sum_to_group_0(up_lead), up_rest)
    return (k_factor_new, c_factor_new, k_moment_new, c_moment_new, precond)


def spread(value, axis, source):
    kept = jnp.where(lax.axis_index(axis) == source, value, 0).astype(value.dtype)
    return lax.psum(kept, axis)


def owner_image(columns, lead_columns, diag_half, side_half):
    row_count = columns.shape[0]
    block_count = diag_half.shape[0]
    block_size = diag_half.shape[1]
    blocked = columns.reshape(row_count, block_count, block_size)
    image_sum = jnp.einsum("tnk,nkj->tnj", blocked, diag_half, preferred_element_type=jnp.float32)
    image_sum = image_sum + jnp.einsum(
        "tk,nkj->tnj", lead_columns, side_half, preferred_element_type=jnp.float32
    )
    return image_sum.astype(jnp.bfloat16).reshape(row_count, block_count * block_size)


def to_owners(pair):
    return (
        lax.all_to_all(pair[0], "fsdp", split_axis=1, concat_axis=0, tiled=True),
        lax.all_to_all(pair[1], "fsdp", split_axis=1, concat_axis=0, tiled=True),
    )


def fetch_lead(before):
    return (
        lax.all_gather(before[0], "fsdp", axis=0, tiled=True),
        lax.all_gather(before[1], "fsdp", axis=0, tiled=True),
    )


def block_stats(owned, lead_image, block_count, block_size):
    blocked = owned.reshape(owned.shape[0], block_count, block_size)
    own_sum = jnp.einsum("tni,tnj->nij", blocked, blocked, preferred_element_type=jnp.float32)
    cross_sum = jnp.einsum("ti,tnj->nij", lead_image, blocked, preferred_element_type=jnp.float32)
    return (own_sum, cross_sum)


def gram_trace(factor, border_keep):
    block_size = factor.shape[1]
    diag_part = factor[:, :, :block_size]
    side_part = factor[:, :, block_size:] * border_keep
    return jnp.sum(diag_part * diag_part) + jnp.sum(side_part * side_part)


def advance(factor, moment, own_sum, cross_sum, lead_block, border_keep, other_h, other_g, width):
    block_size = factor.shape[1]
    diag_part = factor[:, :, :block_size]
    side_part = factor[:, :, block_size:] * border_keep
    gram_diag = jnp.einsum("nki,nkj->nij", diag_part, diag_part, precision=highest)
    gram_diag = gram_diag + jnp.einsum("nki,nkj->nij", side_part, side_part, precision=highest)
    gram_side = jnp.einsum("ki,nkj->nij", lead_block, side_part, precision=highest)
    identity = jnp.eye(block_size, dtype=jnp.float32)
    fresh_diag = (other_h * own_sum + damping * other_g * gram_diag - width * identity) / (
        2.0 * width
    )
    fresh_side = (other_h * cross_sum + damping * other_g * gram_side) * border_keep / (2.0 * width)
    moment_diag = momentum_rate * moment[:, :, :block_size] + fresh_diag
    moment_side = (momentum_rate * moment[:, :, block_size:] + fresh_side) * border_keep
    new_diag = diag_part - step_rate * jnp.einsum(
        "nik,nkj->nij", diag_part, moment_diag, precision=highest
    )
    side_change = jnp.einsum("ik,nkj->nij", lead_block, moment_side, precision=highest)
    side_change = side_change + jnp.einsum(
        "nik,nkj->nij", side_part, moment_diag, precision=highest
    )
    new_side = (side_part - step_rate * side_change) * border_keep
    return (
        jnp.concatenate([new_diag, new_side], axis=-1),
        jnp.concatenate([moment_diag, moment_side], axis=-1),
    )


def general(acts, out_grads, token_counts, k_factor, c_factor, k_moment, c_moment, grad_weight):
    tok_dev, width = acts.shape
    blocks_dev = k_factor.shape[0]
    block_size = k_factor.shape[1]
    group_count = lax.axis_size("dp")
    shard_count = lax.axis_size("fsdp")
    group_id = lax.axis_index("dp")
    shard_id = lax.axis_index("fsdp")
    token_total = jnp.sum(token_counts).astype(jnp.float32)
    valid_limit = jnp.sum(jnp.where(lax.iota(jnp.int32, group_count) == group_id, token_counts, 0))
    positions = shard_id * tok_dev + lax.iota(jnp.int32, tok_dev)
    row_keep = (positions < valid_limit).astype(jnp.bfloat16)[:, None]
    masked_acts = acts * row_keep
    masked_grads = out_grads * row_keep
    block_ids = shard_id * blocks_dev + lax.iota(jnp.int32, blocks_dev)
    border_keep = (block_ids > 0).astype(jnp.float32)[:, None, None]
    lead_k, lead_c = (
        spread(k_factor[0, :, :block_size], "fsdp", 0),
        spread(c_factor[0, :, :block_size], "fsdp", 0),
    )
    raw_acts, raw_grads = to_owners((masked_acts, masked_grads))
    lead_raw_acts, lead_raw_grads = fetch_lead(
        (masked_acts[:, :block_size], masked_grads[:, :block_size])
    )
    k_diag_half = k_factor[:, :, :block_size].astype(jnp.bfloat16)
    k_side_half = (k_factor[:, :, block_size:] * border_keep).astype(jnp.bfloat16)
    c_diag_half = c_factor[:, :, :block_size].astype(jnp.bfloat16)
    c_side_half = (c_factor[:, :, block_size:] * border_keep).astype(jnp.bfloat16)
    owned_acts = owner_image(raw_acts, lead_raw_acts, k_diag_half, k_side_half)
    owned_grads = owner_image(raw_grads, lead_raw_grads, c_diag_half, c_side_half)
    lead_acts = jnp.dot(
        lead_raw_acts, lead_k.astype(jnp.bfloat16), preferred_element_type=jnp.float32
    ).astype(jnp.bfloat16)
    lead_grads = jnp.dot(
        lead_raw_grads, lead_c.astype(jnp.bfloat16), preferred_element_type=jnp.float32
    ).astype(jnp.bfloat16)
    own_k, cross_k = block_stats(owned_acts, lead_acts, blocks_dev, block_size)
    own_c, cross_c = block_stats(owned_grads, lead_grads, blocks_dev, block_size)
    summed = lax.psum((own_k, cross_k, own_c, cross_c), "dp")
    gram_k = gram_trace(k_factor, border_keep)
    gram_c = gram_trace(c_factor, border_keep)
    local_traces = jnp.stack(
        [
            jnp.sum(jnp.trace(summed[0], axis1=1, axis2=2)),
            jnp.sum(jnp.trace(summed[2], axis1=1, axis2=2)),
            gram_k,
            gram_c,
        ]
    )
    totals = lax.psum(local_traces, "fsdp")
    trace_hk = totals[0] / token_total
    trace_hc = totals[1] / token_total
    scale_width = float(width)
    k_factor_new, k_moment_new = advance(
        k_factor,
        k_moment,
        summed[0] / token_total,
        summed[1] / token_total,
        lead_k,
        border_keep,
        trace_hc,
        totals[3],
        scale_width,
    )
    c_factor_new, c_moment_new = advance(
        c_factor,
        c_moment,
        summed[2] / token_total,
        summed[3] / token_total,
        lead_c,
        border_keep,
        trace_hk,
        totals[2],
        scale_width,
    )
    grad_rows = grad_weight.shape[0]
    grad_lead = spread(grad_weight[:, :block_size], "fsdp", 0)
    k_diag = k_factor_new[:, :, :block_size].astype(jnp.bfloat16)
    k_side = k_factor_new[:, :, block_size:].astype(jnp.bfloat16)
    grad_blocked = grad_weight.reshape(grad_rows, blocks_dev, block_size)
    first_sum = jnp.einsum("rnk,nkj->rnj", grad_blocked, k_diag, preferred_element_type=jnp.float32)
    first_sum = first_sum + jnp.einsum(
        "rk,nkj->rnj", grad_lead, k_side, preferred_element_type=jnp.float32
    )
    first_product = first_sum.astype(jnp.bfloat16)
    own_second = jnp.einsum(
        "rnk,njk->rnj", first_product, k_diag, preferred_element_type=jnp.float32
    )
    lead_term = jnp.einsum("rnk,njk->rj", first_product, k_side, preferred_element_type=jnp.float32)
    lead_sum = lax.psum(lead_term, "fsdp")
    lead_mask = (block_ids == 0).astype(jnp.float32)[None, :, None]
    second_product = (own_second + lead_mask * lead_sum[:, None, :]).astype(jnp.bfloat16)
    row_blocks = grad_rows // block_size
    owner_count = shard_count // group_count
    c_half = c_factor_new.astype(jnp.bfloat16)
    fetched = []
    for owner_step in range(owner_count):
        fetched.append(spread(c_half, "fsdp", group_id * owner_count + owner_step))
    row_factor = jnp.concatenate(fetched, axis=0)
    c_diag = row_factor[:, :, :block_size]
    c_side = row_factor[:, :, block_size:]
    by_rows = second_product.reshape(row_blocks, block_size, blocks_dev * block_size)
    lead_rows = spread(by_rows[0], "dp", 0)
    third_sum = jnp.einsum("nki,nkc->nic", c_diag, by_rows, preferred_element_type=jnp.float32)
    third_sum = third_sum + jnp.einsum(
        "nki,kc->nic", c_side, lead_rows, preferred_element_type=jnp.float32
    )
    third_product = third_sum.astype(jnp.bfloat16)
    own_fourth = jnp.einsum(
        "nik,nkc->nic", c_diag, third_product, preferred_element_type=jnp.float32
    )
    row_term = jnp.einsum("nik,nkc->ic", c_side, third_product, preferred_element_type=jnp.float32)
    row_sum = lax.psum(row_term, "dp")
    row_ids = group_id * row_blocks + lax.iota(jnp.int32, row_blocks)
    row_mask = (row_ids == 0).astype(jnp.float32)[:, None, None]
    precond = (
        (own_fourth + row_mask * row_sum[None, :, :])
        .astype(jnp.bfloat16)
        .reshape(grad_rows, blocks_dev * block_size)
    )
    return (k_factor_new, c_factor_new, k_moment_new, c_moment_new, precond)


def per_device(*args):
    blocks = args[3].shape[0]
    groups, shards = lax.axis_size("dp"), lax.axis_size("fsdp")
    fits = blocks == 4 and groups == 4 and shards == 8
    return (planned if fits else general)(*args)


def solution(mesh):
    in_specs = (
        P(("dp", "fsdp"), None),
        P(("dp", "fsdp"), None),
        P(),
        P("fsdp", None, None),
        P("fsdp", None, None),
        P("fsdp", None, None),
        P("fsdp", None, None),
        P("dp", "fsdp"),
    )
    out_specs = (
        P("fsdp", None, None),
        P("fsdp", None, None),
        P("fsdp", None, None),
        P("fsdp", None, None),
        P("dp", "fsdp"),
    )
    return jax.shard_map(
        per_device, mesh=mesh, in_specs=in_specs, out_specs=out_specs, check_vma=False
    )
```

```python
import functools

import jax
import jax.numpy as jnp
from jax import lax
from jax.experimental import pallas as pl
from jax.experimental.pallas import tpu as pltpu
from jax.sharding import PartitionSpec as P

damping = 0.1
momentum_rate = 0.5
step_rate = 0.2
highest = lax.Precision.HIGHEST
both = ("dp", "fsdp")
f32 = jnp.float32
bf16 = jnp.bfloat16
vmem_cap = 48 * 1024 * 1024


def params(*semantics):
    return pltpu.CompilerParams(dimension_semantics=semantics, vmem_limit_bytes=vmem_cap)


light = pl.CostEstimate(flops=1, transcendentals=0, bytes_accessed=1)


def dot(a, b, dims=((1,), (0,)), precision=None):
    return lax.dot_general(a, b, (dims, ((), ())), precision=precision, preferred_element_type=f32)


nn = ((1,), (0,))
tn = ((0,), (0,))
nt = ((1,), (1,))


def fold(full):
    half = full.shape[0] // 2
    low = full[half:, half:]
    low = jnp.concatenate([low[: half // 2], low[half // 2 :]], axis=1)
    return jnp.concatenate([full[:half], low], axis=0)


def unfold(packed):
    half = packed.shape[1] // 2
    top = packed[:half]
    low = packed[half:]
    low = jnp.concatenate([low[:, :half], low[:, half:]], axis=0)
    low = jnp.concatenate([top[:, half:].T, low], axis=1)
    return jnp.concatenate([top, low], axis=0)


def pack_body(zs, xs, ds, bs, tile, lim_ref, a_ref, o_ref):
    rows = pl.program_id(0) * tile + lax.broadcasted_iota(jnp.int32, (tile, bs), 0)
    keep = jnp.where(rows < lim_ref[0], 1.0, 0.0).astype(bf16)
    lead = a_ref[:, :bs] * keep
    for d in range(ds):
        for x in range(xs):
            for z in range(zs):
                n = (z * xs + x) * ds + d
                o_ref[d * xs + x, z] = a_ref[:, n * bs : (n + 1) * bs] * keep
            o_ref[d * xs + x, zs] = lead


def pack(limit, tokens, zs, xs, ds, bs):
    count, width = tokens.shape
    tile = 32
    return pl.pallas_call(
        functools.partial(pack_body, zs, xs, ds, bs, tile),
        grid=(count // tile,),
        in_specs=[
            pl.BlockSpec(memory_space=pltpu.SMEM),
            pl.BlockSpec((tile, width), lambda i: (i, 0)),
        ],
        out_specs=pl.BlockSpec((ds * xs, zs + 1, tile, bs), lambda i: (0, 0, i, 0)),
        out_shape=jax.ShapeDtypeStruct((ds * xs, zs + 1, count, bs), bf16),
        cost_estimate=light,
        compiler_params=params("arbitrary"),
        name="pack_tokens",
    )(limit, tokens)


def moments_body(ids_ref, x_ref, l_ref, o_ref):
    groups, _, count, bs = x_ref.shape
    cols = x_ref[:, 0].reshape(groups * count, bs)
    lead = l_ref[:, 0].reshape(groups * count, bs)
    fold_rows = 3 * bs // 4
    o_ref[0, :fold_rows] = fold(dot(cols, cols, tn)).astype(bf16)
    o_ref[0, fold_rows : fold_rows + bs] = dot(lead, cols, tn).astype(bf16)
    o_ref[0, fold_rows + bs :] = fold(dot(lead, lead, tn)).astype(bf16)


def raw_moments(ids, owned):
    groups, slots, count, bs = owned.shape
    zs = slots - 1
    return pl.pallas_call(
        moments_body,
        grid_spec=pltpu.PrefetchScalarGridSpec(
            num_scalar_prefetch=1,
            grid=(zs,),
            in_specs=[
                pl.BlockSpec((groups, 1, count, bs), lambda k, ids: (0, ids[0] ^ k, 0, 0)),
                pl.BlockSpec((groups, 1, count, bs), lambda k, ids: (0, zs, 0, 0)),
            ],
            out_specs=pl.BlockSpec((1, 5 * bs // 2, bs), lambda k, ids: (k, 0, 0)),
        ),
        out_shape=jax.ShapeDtypeStruct((zs, 5 * bs // 2, bs), bf16),
        cost_estimate=light,
        compiler_params=params("arbitrary"),
        name="raw_moments",
    )(ids, owned, owned)


def image_stats_body(count, ids_ref, sc_ref, *refs):
    parts = refs[:count]
    fac_ref, h_ref, tr_ref = refs[count:]
    bs = fac_ref.shape[1]
    keep = jnp.where(ids_ref[2] + ids_ref[1] > 0, 1.0, 0.0)
    total = parts[0][...].astype(f32)
    for part in parts[1:]:
        total = total + part[...].astype(f32)
    fold_rows = 3 * bs // 4
    own_raw = unfold(total[:fold_rows])
    cross_raw = total[fold_rows : fold_rows + bs]
    lead_raw = unfold(total[fold_rows + bs :])
    fac = fac_ref[0]
    bn = fac[:, :bs].astype(bf16).astype(f32)
    pn = (fac[:, bs:] * keep).astype(bf16).astype(f32)
    mm = functools.partial(dot, precision=highest)
    t1 = mm(own_raw, bn) + mm(cross_raw, pn, tn)
    t0 = mm(cross_raw, bn) + mm(lead_raw, pn)
    own = (mm(bn, t1, tn) + mm(pn, t0, tn)) * sc_ref[0]
    h_ref[:fold_rows] = fold(own).astype(bf16)
    h_ref[fold_rows:] = (t0 * sc_ref[0]).astype(bf16)
    row = lax.broadcasted_iota(jnp.int32, (bs, bs), 0)
    col = lax.broadcasted_iota(jnp.int32, (bs, bs), 1)
    tr_ref[...] = jnp.zeros_like(tr_ref) + jnp.sum(jnp.where(row == col, own, 0.0))


def image_stats(ids, scalars, parts, factor):
    _, bs, wide = factor.shape
    whole = lambda shape: pl.BlockSpec(shape, lambda i, ids: (0,) * len(shape))
    return pl.pallas_call(
        functools.partial(image_stats_body, len(parts)),
        grid_spec=pltpu.PrefetchScalarGridSpec(
            num_scalar_prefetch=1,
            grid=(1,),
            in_specs=[pl.BlockSpec(memory_space=pltpu.SMEM)]
            + [whole(part.shape) for part in parts]
            + [pl.BlockSpec((1, bs, wide), lambda i, ids: (ids[1], 0, 0))],
            out_specs=[whole((7 * bs // 4, bs)), whole((8, 128))],
        ),
        out_shape=[
            jax.ShapeDtypeStruct((7 * bs // 4, bs), bf16),
            jax.ShapeDtypeStruct((8, 128), f32),
        ],
        cost_estimate=light,
        compiler_params=params("arbitrary"),
        name="image_stats",
    )(ids, scalars, *parts, factor)


def stats_body(x_ref, l_ref, f_ref, o_ref, t_ref):
    groups, _, count, bs = x_ref.shape
    k = pl.program_id(0)
    cols = x_ref[:, 0].reshape(groups * count, bs)
    lead = l_ref[:, 0].reshape(groups * count, bs)

    @pl.when(k == 0)
    def _():
        t_ref[...] = jnp.zeros_like(t_ref)

    image = (dot(cols, f_ref[0, :, :bs]) + dot(lead, f_ref[0, :, bs:])).astype(bf16)
    fold_rows = 3 * bs // 4
    o_ref[0, :fold_rows] = fold(dot(image, image, tn)).astype(bf16)
    o_ref[0, fold_rows:] = dot(lead, image, tn).astype(bf16)
    wide = image.astype(f32)
    t_ref[...] = t_ref[...] + jnp.sum(wide * wide)


def stats(ids, owned, blocks):
    groups, slots, count, bs = owned.shape
    zs = slots - 1

    def body(ids_ref, *refs):
        stats_body(*refs)

    return pl.pallas_call(
        body,
        grid_spec=pltpu.PrefetchScalarGridSpec(
            num_scalar_prefetch=1,
            grid=(zs,),
            in_specs=[
                pl.BlockSpec((groups, 1, count, bs), lambda k, ids: (0, ids[0] ^ k, 0, 0)),
                pl.BlockSpec((groups, 1, count, bs), lambda k, ids: (0, zs, 0, 0)),
                pl.BlockSpec((1, bs, 2 * bs), lambda k, ids: (k, 0, 0)),
            ],
            out_specs=[
                pl.BlockSpec((1, 7 * bs // 4, bs), lambda k, ids: (k, 0, 0)),
                pl.BlockSpec((8, 128), lambda k, ids: (0, 0)),
            ],
        ),
        out_shape=[
            jax.ShapeDtypeStruct((zs, 7 * bs // 4, bs), bf16),
            jax.ShapeDtypeStruct((8, 128), f32),
        ],
        cost_estimate=light,
        compiler_params=params("arbitrary"),
        name="plane_stats",
    )(ids, owned, owned, blocks)


def advance_block(width, own, cross, fac, mom, b0, other_h, other_g, keep):
    bs = fac.shape[0]
    diag = fac[:, :bs]
    side = fac[:, bs:] * keep
    db = diag.astype(bf16)
    sb = side.astype(bf16)
    gram_d = dot(db, db, tn) + dot(sb, sb, tn)
    gram_s = dot(b0, sb, tn)
    row = lax.broadcasted_iota(jnp.int32, (bs, bs), 0)
    col = lax.broadcasted_iota(jnp.int32, (bs, bs), 1)
    ident = jnp.where(row == col, width, 0.0)
    scale = 1.0 / (2.0 * width)
    md = momentum_rate * mom[:, :bs] + (other_h * own + damping * other_g * gram_d - ident) * scale
    ms = momentum_rate * mom[:, bs:] + (other_h * cross + damping * other_g * gram_s) * scale
    ms = ms * keep
    mdb = md.astype(bf16)
    new_d = diag - step_rate * dot(db, mdb)
    new_s = side - step_rate * (dot(b0, ms.astype(bf16)) + dot(sb, mdb)) * keep
    return md, ms, new_d, new_s


def order_of(ids, m):
    return ids[1] ^ ((m & 1) * 2 + (m >> 1))


def advance_body(width, ids_ref, sc_ref, h_ref, fac_ref, mom_ref, lead_ref, fn_ref, mn_ref, fb_ref):
    bs = lead_ref.shape[0]
    j = order_of(ids_ref, pl.program_id(0))
    keep = jnp.where(ids_ref[2] + j > 0, 1.0, 0.0)
    md, ms, new_d, new_s = advance_block(
        width,
        unfold(h_ref[0, : 3 * bs // 4].astype(f32)),
        dot(lead_ref[...], h_ref[0, 3 * bs // 4 :], tn),
        fac_ref[0],
        mom_ref[0],
        lead_ref[...],
        sc_ref[0],
        sc_ref[1],
        keep,
    )
    fn_ref[0, :, :bs] = new_d
    fn_ref[0, :, bs:] = new_s
    mn_ref[0, :, :bs] = md
    mn_ref[0, :, bs:] = ms
    fb_ref[0, :, :bs] = new_d.astype(bf16)
    fb_ref[0, :, bs:] = new_s.astype(bf16)


def advance_all(width, ids, scalars, stats, factor, moment, lead):
    blocks, bs, wide = factor.shape
    spec = pl.BlockSpec((1, bs, wide), lambda m, ids: (order_of(ids, m), 0, 0))
    return pl.pallas_call(
        functools.partial(advance_body, width),
        grid_spec=pltpu.PrefetchScalarGridSpec(
            num_scalar_prefetch=1,
            grid=(blocks,),
            in_specs=[
                pl.BlockSpec(memory_space=pltpu.SMEM),
                pl.BlockSpec((1, 7 * bs // 4, bs), lambda m, ids: (m, 0, 0)),
                spec,
                spec,
                pl.BlockSpec((bs, bs), lambda m, ids: (0, 0)),
            ],
            out_specs=[spec, spec, spec],
        ),
        out_shape=[
            jax.ShapeDtypeStruct(factor.shape, f32),
            jax.ShapeDtypeStruct(factor.shape, f32),
            jax.ShapeDtypeStruct(factor.shape, bf16),
        ],
        cost_estimate=light,
        compiler_params=params("arbitrary"),
        name="advance_all",
    )(ids, scalars, stats, factor, moment, lead)


def columns_body(ids_ref, g_ref, l_ref, k_ref, s_ref, t_ref):
    blocks, bs, _ = k_ref.shape
    lead = l_ref[...]
    term = None
    for n in range(blocks):
        kd = k_ref[n, :, :bs]
        ks = k_ref[n, :, bs:]
        first = (dot(g_ref[:, n * bs : (n + 1) * bs], kd) + dot(lead, ks)).astype(bf16)
        second = dot(first, kd, nt)
        s_ref[:, n * bs : (n + 1) * bs] = second.astype(bf16)
        part = dot(first, ks, nt)
        if n == 0:
            part = part + second * jnp.where(ids_ref[2] == 0, 1.0, 0.0)
        term = part if term is None else term + part
    t_ref[...] = term.astype(bf16)


def columns(ids, grad, lead, kb):
    rows, wide = grad.shape
    blocks, bs, _ = kb.shape
    tile = 512
    return pl.pallas_call(
        columns_body,
        grid_spec=pltpu.PrefetchScalarGridSpec(
            num_scalar_prefetch=1,
            grid=(rows // tile,),
            in_specs=[
                pl.BlockSpec((tile, wide), lambda i, ids: (i, 0)),
                pl.BlockSpec((tile, bs), lambda i, ids: (i, 0)),
                pl.BlockSpec(kb.shape, lambda i, ids: (0, 0, 0)),
            ],
            out_specs=[
                pl.BlockSpec((tile, wide), lambda i, ids: (i, 0)),
                pl.BlockSpec((tile, bs), lambda i, ids: (i, 0)),
            ],
        ),
        out_shape=[
            jax.ShapeDtypeStruct((rows, wide), bf16),
            jax.ShapeDtypeStruct((rows, bs), bf16),
        ],
        cost_estimate=light,
        compiler_params=params("arbitrary"),
        name="column_products",
    )(ids, grad, lead, kb)


def row_of(ids, k):
    per = ids[4]
    return ((ids[3] & 1) ^ (k // per)) * per + k % per


def gathered_at(ids, k):
    i = row_of(ids, k)
    return (i % ids[4]) * 2 + i // ids[4]


def rows_body(ids_ref, s_ref, l_ref, c_ref, p_ref, u_ref, acc_ref):
    k = pl.program_id(0)
    bs = c_ref.shape[1]
    cd = c_ref[0, :, :bs]
    cs = c_ref[0, :, bs:]
    third = (dot(cd, s_ref[:, bs:], tn) + dot(cs, l_ref[...], tn)).astype(bf16)
    fourth = dot(cd, third)
    p_ref[:, bs:] = fourth.astype(bf16)
    is_first = (ids_ref[1] == 0) & (row_of(ids_ref, k) == 0)
    term = dot(cs, third) + fourth * jnp.where(is_first, 1.0, 0.0)

    @pl.when(k == 0)
    def _():
        acc_ref[...] = term

    @pl.when(k > 0)
    def _():
        acc_ref[...] = acc_ref[...] + term

    @pl.when(k == pl.num_programs(0) - 1)
    def _():
        u_ref[...] = acc_ref[...].astype(bf16)


def rows(ids, second, lead, cb):
    count, wide = second.shape
    blocks, bs, _ = cb.shape
    rest = wide - bs
    spec = pl.BlockSpec((bs, wide), lambda k, ids: (row_of(ids, k), 0))
    whole = pl.BlockSpec((bs, rest), lambda k, ids: (0, 0))
    return pl.pallas_call(
        rows_body,
        grid_spec=pltpu.PrefetchScalarGridSpec(
            num_scalar_prefetch=1,
            grid=(blocks,),
            in_specs=[
                spec,
                whole,
                pl.BlockSpec((1, bs, 2 * bs), lambda k, ids: (k, 0, 0)),
            ],
            out_specs=[spec, whole],
            scratch_shapes=[pltpu.VMEM((bs, rest), f32)],
        ),
        out_shape=[
            jax.ShapeDtypeStruct((count, wide), bf16),
            jax.ShapeDtypeStruct((bs, rest), bf16),
        ],
        cost_estimate=light,
        compiler_params=params("arbitrary"),
        name="row_products",
    )(ids, second, lead, cb)


def lead_rows_body(ids_ref, s_ref, g_ref, l_ref, c_ref, _, p_ref, u_ref):
    blocks, bs, _ = c_ref.shape
    total = jnp.zeros((bs, bs), f32)
    for k in range(blocks):
        i = row_of(ids_ref, k)
        own = s_ref[pl.ds(pl.multiple_of(i * bs, bs), bs), :]
        whole = g_ref[pl.ds(pl.multiple_of(gathered_at(ids_ref, k) * bs, bs), bs), :]
        second = jnp.where(ids_ref[3] == 0, whole, own)
        cd = c_ref[k, :, :bs]
        cs = c_ref[k, :, bs:]
        third = (dot(cd, second, tn) + dot(cs, l_ref[...], tn)).astype(bf16)
        fourth = dot(cd, third)
        p_ref[pl.ds(pl.multiple_of(i * bs, bs), bs), :] = fourth.astype(bf16)
        is_first = (ids_ref[1] == 0) & (i == 0)
        total = total + dot(cs, third) + fourth * jnp.where(is_first, 1.0, 0.0)
    u_ref[...] = total.astype(bf16)


def lead_rows_products(ids, second, gathered, lead, cb, tile):
    count, _ = second.shape
    blocks, bs, _ = cb.shape
    column = pl.BlockSpec((count, bs), lambda i, ids: (0, 0))
    square = pl.BlockSpec((bs, bs), lambda i, ids: (0, 0))
    return pl.pallas_call(
        lead_rows_body,
        grid_spec=pltpu.PrefetchScalarGridSpec(
            num_scalar_prefetch=1,
            grid=(1,),
            in_specs=[
                column,
                column,
                square,
                pl.BlockSpec(cb.shape, lambda i, ids: (0, 0, 0)),
                pl.BlockSpec(memory_space=pl.ANY),
            ],
            out_specs=[column, square],
        ),
        out_shape=[
            jax.ShapeDtypeStruct(tile.shape, bf16),
            jax.ShapeDtypeStruct((bs, bs), bf16),
        ],
        input_output_aliases={5: 0},
        cost_estimate=light,
        compiler_params=params("arbitrary"),
        name="lead_row_products",
    )(ids, second, gathered, lead, cb, tile)


def put_top_body(ids_ref, p_ref, lead_ref, rest_ref, o_ref):
    bs = lead_ref.shape[1]
    first = ids_ref[1] == 0

    @pl.when(first)
    def _():
        o_ref[:, :bs] = lead_ref[...]
        o_ref[:, bs:] = rest_ref[...]

    @pl.when(jnp.logical_not(first))
    def _():
        o_ref[...] = p_ref[...]


def put_top(ids, tile, lead, rest):
    bs = lead.shape[0]
    spec = lambda width: pl.BlockSpec((bs, width), lambda i, ids: (0, 0))
    top = spec(tile.shape[1])
    return pl.pallas_call(
        put_top_body,
        grid_spec=pltpu.PrefetchScalarGridSpec(
            num_scalar_prefetch=1,
            grid=(1,),
            in_specs=[top, spec(bs), spec(rest.shape[1])],
            out_specs=top,
        ),
        out_shape=jax.ShapeDtypeStruct(tile.shape, tile.dtype),
        input_output_aliases={1: 0},
        cost_estimate=light,
        compiler_params=params("arbitrary"),
        name="put_top",
    )(ids, tile, lead, rest)


def after(value, *earlier):
    return lax.optimization_barrier((value,) + earlier)[0]


def planned(acts, out_grads, token_counts, k_factor, c_factor, k_moment, c_moment, grad_weight):
    tok_dev, width = acts.shape
    ds, bs, _ = k_factor.shape
    shards = lax.axis_size("fsdp")
    xs = 2
    zs = shards // xs
    d = lax.axis_index("dp")
    s = lax.axis_index("fsdp")
    x = s % xs
    z = s // xs
    flat = lambda dd, ss: dd * shards + ss
    plane = [[flat(dd, zz * xs + xx) for dd in range(ds) for xx in range(xs)] for zz in range(zs)]
    flip_x = [(i, i ^ 1) for i in range(shards)]
    ids = jnp.stack([z, d, s * ds, s, jnp.int32(ds)]).astype(jnp.int32)
    token_total = jnp.sum(token_counts).astype(f32)
    valid = jnp.sum(jnp.where(lax.iota(jnp.int32, ds) == d, token_counts, 0))
    stat_scalars = (1.0 / token_total).reshape(1)
    limit = (valid - s * tok_dev).reshape(1).astype(jnp.int32)

    def along_z(value, k):
        pairs = [(zz * xs + xx, (zz ^ k) * xs + xx) for zz in range(zs) for xx in range(xs)]
        return lax.ppermute(value, "fsdp", pairs)

    def from_group_0(value):
        value = jnp.where(d == 0, value, lax.ppermute(value, "dp", [(0, 2)]))
        return jnp.where(d % 2 == 0, value, lax.ppermute(value, "dp", [(0, 1), (2, 3)]))

    def block_along_z(factor, *earlier):
        own = lax.dynamic_index_in_dim(factor, d, 0, keepdims=False)
        side_keep = jnp.where(s * ds + d > 0, 1.0, 0.0)
        own = jnp.concatenate([own[:, :bs], own[:, bs:] * side_keep], axis=1).astype(bf16)
        own = after(own, *earlier)
        return jnp.stack([own] + [along_z(own, k) for k in range(1, zs)])

    def mean_of(parts):
        total = parts[0].astype(f32)
        for part in parts[1:]:
            total = total + part.astype(f32)
        return (total / token_total).astype(bf16)

    def each_along_z(partial):
        return [partial[0]] + [along_z(partial[k], k) for k in range(1, zs)]

    def over_dp(value):
        pair = jnp.stack([value, lax.ppermute(value, "dp", [(i, i ^ 2) for i in range(ds)])])
        other = lax.ppermute(pair, "dp", [(i, i ^ 1) for i in range(ds)])
        return jnp.concatenate([pair, other], axis=0)

    def gram_part(factor):
        block_ids = s * ds + lax.iota(jnp.int32, ds)
        keep = (block_ids > 0).astype(f32)[:, None, None]
        side = factor[:, :, bs:] * keep
        return (jnp.sum(factor[:, :, :bs] ** 2) + jnp.sum(side * side)) / ds

    def exchange(packed):
        return lax.all_to_all(packed, both, 0, 0, tiled=True, axis_index_groups=plane)

    load = jnp.concatenate(
        [k_factor[0, :, :bs].astype(bf16), c_factor[0, :, :bs].astype(bf16), grad_weight[:, :bs]]
    )
    load_half = load.shape[0] // xs
    load_x = lax.ppermute(load[load_half:], "fsdp", [(0, 1)])

    def down_z(value, stride):
        pairs = [
            (zz * xs + xx, (zz + stride) * xs + xx)
            for zz in range(0, zs, 2 * stride)
            for xx in range(xs)
        ]
        return lax.ppermute(value, "fsdp", pairs)

    owned_k = exchange(pack(limit, acts, zs, xs, ds, bs))
    blocks_c = block_along_z(c_factor)
    packed_c = pack(limit, out_grads, zs, xs, ds, bs)
    gram_k = gram_part(k_factor)
    gram_c = gram_part(c_factor)
    packed_c, owned_k, blocks_c, gram_k, gram_c = lax.optimization_barrier(
        (packed_c, owned_k, blocks_c, gram_k, gram_c)
    )
    owned_c = exchange(packed_c)

    raw_k = raw_moments(ids, owned_k)
    sent_k = each_along_z(raw_k)
    stride = zs // 2
    mine = jnp.where(s == 0, load[:load_half], after(load_x, *sent_k))
    while stride > 1:
        got = down_z(mine, stride)
        mine = jnp.where(z % (2 * stride) == 0, mine, got)
        stride //= 2
    last_z = down_z(mine, 1)

    stat_k, trace_k = image_stats(ids, stat_scalars, sent_k, k_factor)
    partial_c, square_c = stats(ids, after(owned_c, trace_k), blocks_c)
    rows8 = lax.broadcasted_iota(jnp.int32, (8, 128), 0)
    sums = jnp.where(
        rows8 == 0,
        trace_k,
        jnp.where(rows8 == 1, square_c, jnp.where(rows8 == 2, gram_k, gram_c)),
    )
    sent_c = each_along_z(partial_c)
    sums = jnp.broadcast_to(sums[None], (ds * shards, 8, 128))
    totals = jnp.sum(lax.all_to_all(sums, both, 0, 0, tiled=True), axis=0)[:, 0]
    for_k = jnp.stack([totals[1] / token_total, totals[3]])
    for_c = jnp.stack([totals[0], totals[2]])
    all_k = over_dp(after(stat_k, partial_c))
    mine = jnp.where(z % 2 == 0, mine, after(last_z, partial_c))
    other = lax.ppermute(mine, "fsdp", flip_x)
    load = jnp.concatenate([jnp.where(x == 0, mine, other), jnp.where(x == 0, other, mine)])
    lead_k, lead_c, grad_lead = load[:bs], load[bs : 2 * bs], load[2 * bs :]

    scale_width = float(width)
    k_factor_new, k_moment_new, kb = advance_all(
        scale_width, ids, for_k, all_k, k_factor, k_moment, lead_k
    )
    second, term = columns(ids, grad_weight, grad_lead, kb)
    count = grad_weight.shape[0]
    kept = lax.dynamic_slice_in_dim(term, x * (count // xs), count // xs, 0)
    passed = lax.dynamic_slice_in_dim(term, (1 - x) * (count // xs), count // xs, 0)
    passed = lax.ppermute(passed, "fsdp", flip_x)

    stat_c = mean_of([after(part, term) for part in sent_c])
    all_c = over_dp(stat_c)

    c_factor_new, c_moment_new, cb = advance_all(
        scale_width, ids, for_c, all_c, c_factor, c_moment, lead_c
    )
    halves = []
    for h in range(2):
        turn = 2 * h
        pairs = [
            (flat(r ^ turn, zz * xs + xx), flat(zz, r * xs + xx))
            for r in range(ds)
            for zz in range(zs)
            for xx in range(xs)
        ]
        halves.append(lax.ppermute(cb[h * (ds // 2) : (h + 1) * (ds // 2)], both, pairs))
    others = [lax.ppermute(h, "fsdp", flip_x) for h in halves]

    halved = (kept.astype(f32) + passed.astype(f32)).astype(bf16).reshape(zs, bs, bs)
    turned = [lax.dynamic_index_in_dim(halved, z ^ k, 0, keepdims=False) for k in range(zs)]
    got = [after(g, cb) for g in each_along_z(turned)]

    c_rows = jnp.concatenate(halves + others, axis=0)

    top_rest = from_group_0(second[:bs, bs:])

    block_sum = got[0].astype(f32)
    for g in got[1:]:
        block_sum = block_sum + g.astype(f32)
    block_sum = block_sum.astype(bf16)
    pair = jnp.stack([block_sum, lax.ppermute(block_sum, "fsdp", [(2 * k + 1, 2 * k) for k in range(zs)])])
    pair = after(pair, *halves)
    gathered = [pair] + [lax.ppermute(pair, "fsdp", [(xs * k, 0)]) for k in range(1, zs)]
    top_lead = jnp.where(s == 0, block_sum, second[:bs, :bs])
    top_lead = from_group_0(top_lead)
    def sum_to_group_0(value):
        total = value.astype(f32) + lax.ppermute(value, "dp", [(2, 0), (3, 1)]).astype(f32)
        other = lax.ppermute(total.astype(bf16), "dp", [(1, 0)])
        return (total + other.astype(f32)).astype(bf16)

    precond, up_rest = rows(ids, second, top_rest, c_rows)
    gathered = [after(g, up_rest) for g in gathered]
    gathered = jnp.concatenate(gathered, axis=0).reshape(count, bs)
    up_rest = sum_to_group_0(up_rest)
    precond, up_lead = lead_rows_products(ids, second, gathered, top_lead, c_rows, precond)
    precond = put_top(ids, precond, sum_to_group_0(up_lead), up_rest)
    return (k_factor_new, c_factor_new, k_moment_new, c_moment_new, precond)


def spread(value, axis, source):
    kept = jnp.where(lax.axis_index(axis) == source, value, 0).astype(value.dtype)
    return lax.psum(kept, axis)


def owner_image(columns, lead_columns, diag_half, side_half):
    row_count = columns.shape[0]
    block_count = diag_half.shape[0]
    block_size = diag_half.shape[1]
    blocked = columns.reshape(row_count, block_count, block_size)
    image_sum = jnp.einsum("tnk,nkj->tnj", blocked, diag_half, preferred_element_type=jnp.float32)
    image_sum = image_sum + jnp.einsum(
        "tk,nkj->tnj", lead_columns, side_half, preferred_element_type=jnp.float32
    )
    return image_sum.astype(jnp.bfloat16).reshape(row_count, block_count * block_size)


def to_owners(pair):
    return (
        lax.all_to_all(pair[0], "fsdp", split_axis=1, concat_axis=0, tiled=True),
        lax.all_to_all(pair[1], "fsdp", split_axis=1, concat_axis=0, tiled=True),
    )


def fetch_lead(before):
    return (
        lax.all_gather(before[0], "fsdp", axis=0, tiled=True),
        lax.all_gather(before[1], "fsdp", axis=0, tiled=True),
    )


def block_stats(owned, lead_image, block_count, block_size):
    blocked = owned.reshape(owned.shape[0], block_count, block_size)
    own_sum = jnp.einsum("tni,tnj->nij", blocked, blocked, preferred_element_type=jnp.float32)
    cross_sum = jnp.einsum("ti,tnj->nij", lead_image, blocked, preferred_element_type=jnp.float32)
    return (own_sum, cross_sum)


def gram_trace(factor, border_keep):
    block_size = factor.shape[1]
    diag_part = factor[:, :, :block_size]
    side_part = factor[:, :, block_size:] * border_keep
    return jnp.sum(diag_part * diag_part) + jnp.sum(side_part * side_part)


def advance(factor, moment, own_sum, cross_sum, lead_block, border_keep, other_h, other_g, width):
    block_size = factor.shape[1]
    diag_part = factor[:, :, :block_size]
    side_part = factor[:, :, block_size:] * border_keep
    gram_diag = jnp.einsum("nki,nkj->nij", diag_part, diag_part, precision=highest)
    gram_diag = gram_diag + jnp.einsum("nki,nkj->nij", side_part, side_part, precision=highest)
    gram_side = jnp.einsum("ki,nkj->nij", lead_block, side_part, precision=highest)
    identity = jnp.eye(block_size, dtype=jnp.float32)
    fresh_diag = (other_h * own_sum + damping * other_g * gram_diag - width * identity) / (
        2.0 * width
    )
    fresh_side = (other_h * cross_sum + damping * other_g * gram_side) * border_keep / (2.0 * width)
    moment_diag = momentum_rate * moment[:, :, :block_size] + fresh_diag
    moment_side = (momentum_rate * moment[:, :, block_size:] + fresh_side) * border_keep
    new_diag = diag_part - step_rate * jnp.einsum(
        "nik,nkj->nij", diag_part, moment_diag, precision=highest
    )
    side_change = jnp.einsum("ik,nkj->nij", lead_block, moment_side, precision=highest)
    side_change = side_change + jnp.einsum(
        "nik,nkj->nij", side_part, moment_diag, precision=highest
    )
    new_side = (side_part - step_rate * side_change) * border_keep
    return (
        jnp.concatenate([new_diag, new_side], axis=-1),
        jnp.concatenate([moment_diag, moment_side], axis=-1),
    )


def general(acts, out_grads, token_counts, k_factor, c_factor, k_moment, c_moment, grad_weight):
    tok_dev, width = acts.shape
    blocks_dev = k_factor.shape[0]
    block_size = k_factor.shape[1]
    group_count = lax.axis_size("dp")
    shard_count = lax.axis_size("fsdp")
    group_id = lax.axis_index("dp")
    shard_id = lax.axis_index("fsdp")
    token_total = jnp.sum(token_counts).astype(jnp.float32)
    valid_limit = jnp.sum(jnp.where(lax.iota(jnp.int32, group_count) == group_id, token_counts, 0))
    positions = shard_id * tok_dev + lax.iota(jnp.int32, tok_dev)
    row_keep = (positions < valid_limit).astype(jnp.bfloat16)[:, None]
    masked_acts = acts * row_keep
    masked_grads = out_grads * row_keep
    block_ids = shard_id * blocks_dev + lax.iota(jnp.int32, blocks_dev)
    border_keep = (block_ids > 0).astype(jnp.float32)[:, None, None]
    lead_k, lead_c = (
        spread(k_factor[0, :, :block_size], "fsdp", 0),
        spread(c_factor[0, :, :block_size], "fsdp", 0),
    )
    raw_acts, raw_grads = to_owners((masked_acts, masked_grads))
    lead_raw_acts, lead_raw_grads = fetch_lead(
        (masked_acts[:, :block_size], masked_grads[:, :block_size])
    )
    k_diag_half = k_factor[:, :, :block_size].astype(jnp.bfloat16)
    k_side_half = (k_factor[:, :, block_size:] * border_keep).astype(jnp.bfloat16)
    c_diag_half = c_factor[:, :, :block_size].astype(jnp.bfloat16)
    c_side_half = (c_factor[:, :, block_size:] * border_keep).astype(jnp.bfloat16)
    owned_acts = owner_image(raw_acts, lead_raw_acts, k_diag_half, k_side_half)
    owned_grads = owner_image(raw_grads, lead_raw_grads, c_diag_half, c_side_half)
    lead_acts = jnp.dot(
        lead_raw_acts, lead_k.astype(jnp.bfloat16), preferred_element_type=jnp.float32
    ).astype(jnp.bfloat16)
    lead_grads = jnp.dot(
        lead_raw_grads, lead_c.astype(jnp.bfloat16), preferred_element_type=jnp.float32
    ).astype(jnp.bfloat16)
    own_k, cross_k = block_stats(owned_acts, lead_acts, blocks_dev, block_size)
    own_c, cross_c = block_stats(owned_grads, lead_grads, blocks_dev, block_size)
    summed = lax.psum((own_k, cross_k, own_c, cross_c), "dp")
    gram_k = gram_trace(k_factor, border_keep)
    gram_c = gram_trace(c_factor, border_keep)
    local_traces = jnp.stack(
        [
            jnp.sum(jnp.trace(summed[0], axis1=1, axis2=2)),
            jnp.sum(jnp.trace(summed[2], axis1=1, axis2=2)),
            gram_k,
            gram_c,
        ]
    )
    totals = lax.psum(local_traces, "fsdp")
    trace_hk = totals[0] / token_total
    trace_hc = totals[1] / token_total
    scale_width = float(width)
    k_factor_new, k_moment_new = advance(
        k_factor,
        k_moment,
        summed[0] / token_total,
        summed[1] / token_total,
        lead_k,
        border_keep,
        trace_hc,
        totals[3],
        scale_width,
    )
    c_factor_new, c_moment_new = advance(
        c_factor,
        c_moment,
        summed[2] / token_total,
        summed[3] / token_total,
        lead_c,
        border_keep,
        trace_hk,
        totals[2],
        scale_width,
    )
    grad_rows = grad_weight.shape[0]
    grad_lead = spread(grad_weight[:, :block_size], "fsdp", 0)
    k_diag = k_factor_new[:, :, :block_size].astype(jnp.bfloat16)
    k_side = k_factor_new[:, :, block_size:].astype(jnp.bfloat16)
    grad_blocked = grad_weight.reshape(grad_rows, blocks_dev, block_size)
    first_sum = jnp.einsum("rnk,nkj->rnj", grad_blocked, k_diag, preferred_element_type=jnp.float32)
    first_sum = first_sum + jnp.einsum(
        "rk,nkj->rnj", grad_lead, k_side, preferred_element_type=jnp.float32
    )
    first_product = first_sum.astype(jnp.bfloat16)
    own_second = jnp.einsum(
        "rnk,njk->rnj", first_product, k_diag, preferred_element_type=jnp.float32
    )
    lead_term = jnp.einsum("rnk,njk->rj", first_product, k_side, preferred_element_type=jnp.float32)
    lead_sum = lax.psum(lead_term, "fsdp")
    lead_mask = (block_ids == 0).astype(jnp.float32)[None, :, None]
    second_product = (own_second + lead_mask * lead_sum[:, None, :]).astype(jnp.bfloat16)
    row_blocks = grad_rows // block_size
    owner_count = shard_count // group_count
    c_half = c_factor_new.astype(jnp.bfloat16)
    fetched = []
    for owner_step in range(owner_count):
        fetched.append(spread(c_half, "fsdp", group_id * owner_count + owner_step))
    row_factor = jnp.concatenate(fetched, axis=0)
    c_diag = row_factor[:, :, :block_size]
    c_side = row_factor[:, :, block_size:]
    by_rows = second_product.reshape(row_blocks, block_size, blocks_dev * block_size)
    lead_rows = spread(by_rows[0], "dp", 0)
    third_sum = jnp.einsum("nki,nkc->nic", c_diag, by_rows, preferred_element_type=jnp.float32)
    third_sum = third_sum + jnp.einsum(
        "nki,kc->nic", c_side, lead_rows, preferred_element_type=jnp.float32
    )
    third_product = third_sum.astype(jnp.bfloat16)
    own_fourth = jnp.einsum(
        "nik,nkc->nic", c_diag, third_product, preferred_element_type=jnp.float32
    )
    row_term = jnp.einsum("nik,nkc->ic", c_side, third_product, preferred_element_type=jnp.float32)
    row_sum = lax.psum(row_term, "dp")
    row_ids = group_id * row_blocks + lax.iota(jnp.int32, row_blocks)
    row_mask = (row_ids == 0).astype(jnp.float32)[:, None, None]
    precond = (
        (own_fourth + row_mask * row_sum[None, :, :])
        .astype(jnp.bfloat16)
        .reshape(grad_rows, blocks_dev * block_size)
    )
    return (k_factor_new, c_factor_new, k_moment_new, c_moment_new, precond)


def per_device(*args):
    blocks = args[3].shape[0]
    groups, shards = lax.axis_size("dp"), lax.axis_size("fsdp")
    fits = blocks == 4 and groups == 4 and shards == 8
    return (planned if fits else general)(*args)


def solution(mesh):
    in_specs = (
        P(("dp", "fsdp"), None),
        P(("dp", "fsdp"), None),
        P(),
        P("fsdp", None, None),
        P("fsdp", None, None),
        P("fsdp", None, None),
        P("fsdp", None, None),
        P("dp", "fsdp"),
    )
    out_specs = (
        P("fsdp", None, None),
        P("fsdp", None, None),
        P("fsdp", None, None),
        P("fsdp", None, None),
        P("dp", "fsdp"),
    )
    return jax.shard_map(
        per_device, mesh=mesh, in_specs=in_specs, out_specs=out_specs, check_vma=False
    )
```

```python
import functools

import jax
import jax.numpy as jnp
from jax import lax
from jax.experimental import pallas as pl
from jax.experimental.pallas import tpu as pltpu
from jax.sharding import PartitionSpec as P

damping = 0.1
momentum_rate = 0.5
step_rate = 0.2
highest = lax.Precision.HIGHEST
both = ("dp", "fsdp")
f32 = jnp.float32
bf16 = jnp.bfloat16
vmem_cap = 48 * 1024 * 1024


def params(*semantics):
    return pltpu.CompilerParams(dimension_semantics=semantics, vmem_limit_bytes=vmem_cap)


light = pl.CostEstimate(flops=1, transcendentals=0, bytes_accessed=1)


def dot(a, b, dims=((1,), (0,)), precision=None):
    return lax.dot_general(a, b, (dims, ((), ())), precision=precision, preferred_element_type=f32)


nn = ((1,), (0,))
tn = ((0,), (0,))
nt = ((1,), (1,))


def fold(full):
    half = full.shape[0] // 2
    low = full[half:, half:]
    low = jnp.concatenate([low[: half // 2], low[half // 2 :]], axis=1)
    return jnp.concatenate([full[:half], low], axis=0)


def unfold(packed):
    half = packed.shape[1] // 2
    top = packed[:half]
    low = packed[half:]
    low = jnp.concatenate([low[:, :half], low[:, half:]], axis=0)
    low = jnp.concatenate([top[:, half:].T, low], axis=1)
    return jnp.concatenate([top, low], axis=0)


def pack_body(zs, xs, ds, bs, tile, lim_ref, a_ref, o_ref):
    rows = pl.program_id(0) * tile + lax.broadcasted_iota(jnp.int32, (tile, bs), 0)
    keep = jnp.where(rows < lim_ref[0], 1.0, 0.0).astype(bf16)
    lead = a_ref[:, :bs] * keep
    for d in range(ds):
        for x in range(xs):
            for z in range(zs):
                n = (z * xs + x) * ds + d
                o_ref[d * xs + x, z] = a_ref[:, n * bs : (n + 1) * bs] * keep
            o_ref[d * xs + x, zs] = lead


def pack(limit, tokens, zs, xs, ds, bs):
    count, width = tokens.shape
    tile = 32
    return pl.pallas_call(
        functools.partial(pack_body, zs, xs, ds, bs, tile),
        grid=(count // tile,),
        in_specs=[
            pl.BlockSpec(memory_space=pltpu.SMEM),
            pl.BlockSpec((tile, width), lambda i: (i, 0)),
        ],
        out_specs=pl.BlockSpec((ds * xs, zs + 1, tile, bs), lambda i: (0, 0, i, 0)),
        out_shape=jax.ShapeDtypeStruct((ds * xs, zs + 1, count, bs), bf16),
        cost_estimate=light,
        compiler_params=params("arbitrary"),
        name="pack_tokens",
    )(limit, tokens)


def moments_body(ids_ref, x_ref, l_ref, o_ref):
    groups, _, count, bs = x_ref.shape
    cols = x_ref[:, 0].reshape(groups * count, bs)
    lead = l_ref[:, 0].reshape(groups * count, bs)
    fold_rows = 3 * bs // 4
    o_ref[0, :fold_rows] = fold(dot(cols, cols, tn)).astype(bf16)
    o_ref[0, fold_rows : fold_rows + bs] = dot(lead, cols, tn).astype(bf16)
    o_ref[0, fold_rows + bs :] = fold(dot(lead, lead, tn)).astype(bf16)


def raw_moments(ids, owned):
    groups, slots, count, bs = owned.shape
    zs = slots - 1
    return pl.pallas_call(
        moments_body,
        grid_spec=pltpu.PrefetchScalarGridSpec(
            num_scalar_prefetch=1,
            grid=(zs,),
            in_specs=[
                pl.BlockSpec((groups, 1, count, bs), lambda k, ids: (0, ids[0] ^ k, 0, 0)),
                pl.BlockSpec((groups, 1, count, bs), lambda k, ids: (0, zs, 0, 0)),
            ],
            out_specs=pl.BlockSpec((1, 5 * bs // 2, bs), lambda k, ids: (k, 0, 0)),
        ),
        out_shape=jax.ShapeDtypeStruct((zs, 5 * bs // 2, bs), bf16),
        cost_estimate=light,
        compiler_params=params("arbitrary"),
        name="raw_moments",
    )(ids, owned, owned)


def image_stats_body(count, ids_ref, sc_ref, *refs):
    parts = refs[:count]
    fac_ref, h_ref, tr_ref = refs[count:]
    bs = fac_ref.shape[1]
    keep = jnp.where(ids_ref[2] + ids_ref[1] > 0, 1.0, 0.0)
    total = parts[0][...].astype(f32)
    for part in parts[1:]:
        total = total + part[...].astype(f32)
    fold_rows = 3 * bs // 4
    own_raw = unfold(total[:fold_rows])
    cross_raw = total[fold_rows : fold_rows + bs]
    lead_raw = unfold(total[fold_rows + bs :])
    fac = fac_ref[0]
    bn = fac[:, :bs].astype(bf16).astype(f32)
    pn = (fac[:, bs:] * keep).astype(bf16).astype(f32)
    mm = functools.partial(dot, precision=highest)
    t1 = mm(own_raw, bn) + mm(cross_raw, pn, tn)
    t0 = mm(cross_raw, bn) + mm(lead_raw, pn)
    own = (mm(bn, t1, tn) + mm(pn, t0, tn)) * sc_ref[0]
    h_ref[:fold_rows] = fold(own).astype(bf16)
    h_ref[fold_rows:] = (t0 * sc_ref[0]).astype(bf16)
    row = lax.broadcasted_iota(jnp.int32, (bs, bs), 0)
    col = lax.broadcasted_iota(jnp.int32, (bs, bs), 1)
    tr_ref[...] = jnp.zeros_like(tr_ref) + jnp.sum(jnp.where(row == col, own, 0.0))


def image_stats(ids, scalars, parts, factor):
    _, bs, wide = factor.shape
    whole = lambda shape: pl.BlockSpec(shape, lambda i, ids: (0,) * len(shape))
    return pl.pallas_call(
        functools.partial(image_stats_body, len(parts)),
        grid_spec=pltpu.PrefetchScalarGridSpec(
            num_scalar_prefetch=1,
            grid=(1,),
            in_specs=[pl.BlockSpec(memory_space=pltpu.SMEM)]
            + [whole(part.shape) for part in parts]
            + [pl.BlockSpec((1, bs, wide), lambda i, ids: (0, 0, 0))],
            out_specs=[whole((7 * bs // 4, bs)), whole((8, 128))],
        ),
        out_shape=[
            jax.ShapeDtypeStruct((7 * bs // 4, bs), bf16),
            jax.ShapeDtypeStruct((8, 128), f32),
        ],
        cost_estimate=light,
        compiler_params=params("arbitrary"),
        name="image_stats",
    )(ids, scalars, *parts, factor)


def stats_body(x_ref, l_ref, f_ref, o_ref, t_ref):
    groups, _, count, bs = x_ref.shape
    k = pl.program_id(0)
    cols = x_ref[:, 0].reshape(groups * count, bs)
    lead = l_ref[:, 0].reshape(groups * count, bs)

    @pl.when(k == 0)
    def _():
        t_ref[...] = jnp.zeros_like(t_ref)

    image = (dot(cols, f_ref[0, :, :bs]) + dot(lead, f_ref[0, :, bs:])).astype(bf16)
    fold_rows = 3 * bs // 4
    o_ref[0, :fold_rows] = fold(dot(image, image, tn)).astype(bf16)
    o_ref[0, fold_rows:] = dot(lead, image, tn).astype(bf16)
    wide = image.astype(f32)
    t_ref[...] = t_ref[...] + jnp.sum(wide * wide)


def stats(ids, owned, blocks):
    groups, slots, count, bs = owned.shape
    zs = slots - 1

    def body(ids_ref, *refs):
        stats_body(*refs)

    return pl.pallas_call(
        body,
        grid_spec=pltpu.PrefetchScalarGridSpec(
            num_scalar_prefetch=1,
            grid=(zs,),
            in_specs=[
                pl.BlockSpec((groups, 1, count, bs), lambda k, ids: (0, ids[0] ^ k, 0, 0)),
                pl.BlockSpec((groups, 1, count, bs), lambda k, ids: (0, zs, 0, 0)),
                pl.BlockSpec((1, bs, 2 * bs), lambda k, ids: (k, 0, 0)),
            ],
            out_specs=[
                pl.BlockSpec((1, 7 * bs // 4, bs), lambda k, ids: (k, 0, 0)),
                pl.BlockSpec((8, 128), lambda k, ids: (0, 0)),
            ],
        ),
        out_shape=[
            jax.ShapeDtypeStruct((zs, 7 * bs // 4, bs), bf16),
            jax.ShapeDtypeStruct((8, 128), f32),
        ],
        cost_estimate=light,
        compiler_params=params("arbitrary"),
        name="plane_stats",
    )(ids, owned, owned, blocks)


def advance_block(width, own, cross, fac, mom, b0, other_h, other_g, keep):
    bs = fac.shape[0]
    diag = fac[:, :bs]
    side = fac[:, bs:] * keep
    db = diag.astype(bf16)
    sb = side.astype(bf16)
    gram_d = dot(db, db, tn) + dot(sb, sb, tn)
    gram_s = dot(b0, sb, tn)
    row = lax.broadcasted_iota(jnp.int32, (bs, bs), 0)
    col = lax.broadcasted_iota(jnp.int32, (bs, bs), 1)
    ident = jnp.where(row == col, width, 0.0)
    scale = 1.0 / (2.0 * width)
    md = momentum_rate * mom[:, :bs] + (other_h * own + damping * other_g * gram_d - ident) * scale
    ms = momentum_rate * mom[:, bs:] + (other_h * cross + damping * other_g * gram_s) * scale
    ms = ms * keep
    mdb = md.astype(bf16)
    new_d = diag - step_rate * dot(db, mdb)
    new_s = side - step_rate * (dot(b0, ms.astype(bf16)) + dot(sb, mdb)) * keep
    return md, ms, new_d, new_s


def order_of(ids, m):
    return ids[1] ^ ((m & 1) * 2 + (m >> 1))


def advance_body(width, ids_ref, sc_ref, h_ref, fac_ref, mom_ref, lead_ref, fn_ref, mn_ref, fb_ref):
    bs = lead_ref.shape[0]
    j = order_of(ids_ref, pl.program_id(0))
    keep = jnp.where(ids_ref[2] + j > 0, 1.0, 0.0)
    md, ms, new_d, new_s = advance_block(
        width,
        unfold(h_ref[0, : 3 * bs // 4].astype(f32)),
        dot(lead_ref[...], h_ref[0, 3 * bs // 4 :], tn),
        fac_ref[0],
        mom_ref[0],
        lead_ref[...],
        sc_ref[0],
        sc_ref[1],
        keep,
    )
    fn_ref[0, :, :bs] = new_d
    fn_ref[0, :, bs:] = new_s
    mn_ref[0, :, :bs] = md
    mn_ref[0, :, bs:] = ms
    fb_ref[0, :, :bs] = new_d.astype(bf16)
    fb_ref[0, :, bs:] = new_s.astype(bf16)


def advance_all(width, ids, scalars, stats, factor, moment, lead):
    blocks, bs, wide = factor.shape
    spec = pl.BlockSpec((1, bs, wide), lambda m, ids: (order_of(ids, m), 0, 0))
    return pl.pallas_call(
        functools.partial(advance_body, width),
        grid_spec=pltpu.PrefetchScalarGridSpec(
            num_scalar_prefetch=1,
            grid=(blocks,),
            in_specs=[
                pl.BlockSpec(memory_space=pltpu.SMEM),
                pl.BlockSpec((1, 7 * bs // 4, bs), lambda m, ids: (m, 0, 0)),
                spec,
                spec,
                pl.BlockSpec((bs, bs), lambda m, ids: (0, 0)),
            ],
            out_specs=[spec, spec, spec],
        ),
        out_shape=[
            jax.ShapeDtypeStruct(factor.shape, f32),
            jax.ShapeDtypeStruct(factor.shape, f32),
            jax.ShapeDtypeStruct(factor.shape, bf16),
        ],
        cost_estimate=light,
        compiler_params=params("arbitrary"),
        name="advance_all",
    )(ids, scalars, stats, factor, moment, lead)


def columns_body(ids_ref, g_ref, l_ref, k_ref, s_ref, t_ref):
    blocks, bs, _ = k_ref.shape
    lead = l_ref[...]
    term = None
    for n in range(blocks):
        kd = k_ref[n, :, :bs]
        ks = k_ref[n, :, bs:]
        first = (dot(g_ref[:, n * bs : (n + 1) * bs], kd) + dot(lead, ks)).astype(bf16)
        second = dot(first, kd, nt)
        s_ref[:, n * bs : (n + 1) * bs] = second.astype(bf16)
        part = dot(first, ks, nt)
        if n == 0:
            part = part + second * jnp.where(ids_ref[2] == 0, 1.0, 0.0)
        term = part if term is None else term + part
    t_ref[...] = term.astype(bf16)


def columns(ids, grad, lead, kb):
    rows, wide = grad.shape
    blocks, bs, _ = kb.shape
    tile = 512
    return pl.pallas_call(
        columns_body,
        grid_spec=pltpu.PrefetchScalarGridSpec(
            num_scalar_prefetch=1,
            grid=(rows // tile,),
            in_specs=[
                pl.BlockSpec((tile, wide), lambda i, ids: (i, 0)),
                pl.BlockSpec((tile, bs), lambda i, ids: (i, 0)),
                pl.BlockSpec(kb.shape, lambda i, ids: (0, 0, 0)),
            ],
            out_specs=[
                pl.BlockSpec((tile, wide), lambda i, ids: (i, 0)),
                pl.BlockSpec((tile, bs), lambda i, ids: (i, 0)),
            ],
        ),
        out_shape=[
            jax.ShapeDtypeStruct((rows, wide), bf16),
            jax.ShapeDtypeStruct((rows, bs), bf16),
        ],
        cost_estimate=light,
        compiler_params=params("arbitrary"),
        name="column_products",
    )(ids, grad, lead, kb)


def row_of(ids, k):
    per = ids[4]
    return ((ids[3] & 1) ^ (k // per)) * per + k % per


def gathered_at(ids, k):
    i = row_of(ids, k)
    return (i % ids[4]) * 2 + i // ids[4]


def rows_body(ids_ref, s_ref, l_ref, c_ref, p_ref, u_ref, acc_ref):
    k = pl.program_id(0)
    bs = c_ref.shape[1]
    cd = c_ref[0, :, :bs]
    cs = c_ref[0, :, bs:]
    third = (dot(cd, s_ref[:, bs:], tn) + dot(cs, l_ref[...], tn)).astype(bf16)
    fourth = dot(cd, third)
    p_ref[:, bs:] = fourth.astype(bf16)
    is_first = (ids_ref[1] == 0) & (row_of(ids_ref, k) == 0)
    term = dot(cs, third) + fourth * jnp.where(is_first, 1.0, 0.0)

    @pl.when(k == 0)
    def _():
        acc_ref[...] = term

    @pl.when(k > 0)
    def _():
        acc_ref[...] = acc_ref[...] + term

    @pl.when(k == pl.num_programs(0) - 1)
    def _():
        u_ref[...] = acc_ref[...].astype(bf16)


def rows(ids, second, lead, cb):
    count, wide = second.shape
    blocks, bs, _ = cb.shape
    rest = wide - bs
    spec = pl.BlockSpec((bs, wide), lambda k, ids: (row_of(ids, k), 0))
    whole = pl.BlockSpec((bs, rest), lambda k, ids: (0, 0))
    return pl.pallas_call(
        rows_body,
        grid_spec=pltpu.PrefetchScalarGridSpec(
            num_scalar_prefetch=1,
            grid=(blocks,),
            in_specs=[
                spec,
                whole,
                pl.BlockSpec((1, bs, 2 * bs), lambda k, ids: (k, 0, 0)),
            ],
            out_specs=[spec, whole],
            scratch_shapes=[pltpu.VMEM((bs, rest), f32)],
        ),
        out_shape=[
            jax.ShapeDtypeStruct((count, wide), bf16),
            jax.ShapeDtypeStruct((bs, rest), bf16),
        ],
        cost_estimate=light,
        compiler_params=params("arbitrary"),
        name="row_products",
    )(ids, second, lead, cb)


def lead_rows_body(ids_ref, s_ref, g_ref, l_ref, c_ref, _, p_ref, u_ref):
    blocks, bs, _ = c_ref.shape
    total = jnp.zeros((bs, bs), f32)
    for k in range(blocks):
        i = row_of(ids_ref, k)
        own = s_ref[pl.ds(pl.multiple_of(i * bs, bs), bs), :]
        whole = g_ref[pl.ds(pl.multiple_of(gathered_at(ids_ref, k) * bs, bs), bs), :]
        second = jnp.where(ids_ref[3] == 0, whole, own)
        cd = c_ref[k, :, :bs]
        cs = c_ref[k, :, bs:]
        third = (dot(cd, second, tn) + dot(cs, l_ref[...], tn)).astype(bf16)
        fourth = dot(cd, third)
        p_ref[pl.ds(pl.multiple_of(i * bs, bs), bs), :] = fourth.astype(bf16)
        is_first = (ids_ref[1] == 0) & (i == 0)
        total = total + dot(cs, third) + fourth * jnp.where(is_first, 1.0, 0.0)
    u_ref[...] = total.astype(bf16)


def lead_rows_products(ids, second, gathered, lead, cb, tile):
    count, _ = second.shape
    blocks, bs, _ = cb.shape
    column = pl.BlockSpec((count, bs), lambda i, ids: (0, 0))
    square = pl.BlockSpec((bs, bs), lambda i, ids: (0, 0))
    return pl.pallas_call(
        lead_rows_body,
        grid_spec=pltpu.PrefetchScalarGridSpec(
            num_scalar_prefetch=1,
            grid=(1,),
            in_specs=[
                column,
                column,
                square,
                pl.BlockSpec(cb.shape, lambda i, ids: (0, 0, 0)),
                pl.BlockSpec(memory_space=pl.ANY),
            ],
            out_specs=[column, square],
        ),
        out_shape=[
            jax.ShapeDtypeStruct(tile.shape, bf16),
            jax.ShapeDtypeStruct((bs, bs), bf16),
        ],
        input_output_aliases={5: 0},
        cost_estimate=light,
        compiler_params=params("arbitrary"),
        name="lead_row_products",
    )(ids, second, gathered, lead, cb, tile)


def put_top_body(ids_ref, p_ref, lead_ref, rest_ref, o_ref):
    bs = lead_ref.shape[1]
    first = ids_ref[1] == 0

    @pl.when(first)
    def _():
        o_ref[:, :bs] = lead_ref[...]
        o_ref[:, bs:] = rest_ref[...]

    @pl.when(jnp.logical_not(first))
    def _():
        o_ref[...] = p_ref[...]


def put_top(ids, tile, lead, rest):
    bs = lead.shape[0]
    spec = lambda width: pl.BlockSpec((bs, width), lambda i, ids: (0, 0))
    top = spec(tile.shape[1])
    return pl.pallas_call(
        put_top_body,
        grid_spec=pltpu.PrefetchScalarGridSpec(
            num_scalar_prefetch=1,
            grid=(1,),
            in_specs=[top, spec(bs), spec(rest.shape[1])],
            out_specs=top,
        ),
        out_shape=jax.ShapeDtypeStruct(tile.shape, tile.dtype),
        input_output_aliases={1: 0},
        cost_estimate=light,
        compiler_params=params("arbitrary"),
        name="put_top",
    )(ids, tile, lead, rest)


def after(value, *earlier):
    return lax.optimization_barrier((value,) + earlier)[0]


def planned(acts, out_grads, token_counts, k_factor, c_factor, k_moment, c_moment, grad_weight):
    tok_dev, width = acts.shape
    ds, bs, _ = k_factor.shape
    shards = lax.axis_size("fsdp")
    xs = 2
    zs = shards // xs
    d = lax.axis_index("dp")
    s = lax.axis_index("fsdp")
    x = s % xs
    z = s // xs
    flat = lambda dd, ss: dd * shards + ss
    plane = [[flat(dd, zz * xs + xx) for dd in range(ds) for xx in range(xs)] for zz in range(zs)]
    flip_x = [(i, i ^ 1) for i in range(shards)]
    ids = jnp.stack([z, d, s * ds, s, jnp.int32(ds)]).astype(jnp.int32)
    token_total = jnp.sum(token_counts).astype(f32)
    valid = jnp.sum(jnp.where(lax.iota(jnp.int32, ds) == d, token_counts, 0))
    stat_scalars = (1.0 / token_total).reshape(1)
    limit = (valid - s * tok_dev).reshape(1).astype(jnp.int32)

    def along_z(value, k):
        pairs = [(zz * xs + xx, (zz ^ k) * xs + xx) for zz in range(zs) for xx in range(xs)]
        return lax.ppermute(value, "fsdp", pairs)

    def from_group_0(value):
        value = jnp.where(d == 0, value, lax.ppermute(value, "dp", [(0, 2)]))
        return jnp.where(d % 2 == 0, value, lax.ppermute(value, "dp", [(0, 1), (2, 3)]))

    def block_along_z(factor, *earlier):
        own = lax.dynamic_index_in_dim(factor, d, 0, keepdims=False)
        side_keep = jnp.where(s * ds + d > 0, 1.0, 0.0)
        own = jnp.concatenate([own[:, :bs], own[:, bs:] * side_keep], axis=1).astype(bf16)
        own = after(own, *earlier)
        return jnp.stack([own] + [along_z(own, k) for k in range(1, zs)])

    def mean_of(parts):
        total = parts[0].astype(f32)
        for part in parts[1:]:
            total = total + part.astype(f32)
        return (total / token_total).astype(bf16)

    def each_along_z(partial):
        return [partial[0]] + [along_z(partial[k], k) for k in range(1, zs)]

    def over_dp(value):
        pair = jnp.stack([value, lax.ppermute(value, "dp", [(i, i ^ 2) for i in range(ds)])])
        other = lax.ppermute(pair, "dp", [(i, i ^ 1) for i in range(ds)])
        return jnp.concatenate([pair, other], axis=0)

    def gram_part(factor):
        block_ids = s * ds + lax.iota(jnp.int32, ds)
        keep = (block_ids > 0).astype(f32)[:, None, None]
        side = factor[:, :, bs:] * keep
        return (jnp.sum(factor[:, :, :bs] ** 2) + jnp.sum(side * side)) / ds

    def exchange(packed):
        return lax.all_to_all(packed, both, 0, 0, tiled=True, axis_index_groups=plane)

    load = jnp.concatenate(
        [k_factor[0, :, :bs].astype(bf16), c_factor[0, :, :bs].astype(bf16), grad_weight[:, :bs]]
    )
    load_half = load.shape[0] // xs
    load_x = lax.ppermute(load[load_half:], "fsdp", [(0, 1)])

    def down_z(value, stride):
        pairs = [
            (zz * xs + xx, (zz + stride) * xs + xx)
            for zz in range(0, zs, 2 * stride)
            for xx in range(xs)
        ]
        return lax.ppermute(value, "fsdp", pairs)

    owned_k = exchange(pack(limit, acts, zs, xs, ds, bs))
    blocks_c = block_along_z(c_factor)
    own_k = lax.dynamic_slice_in_dim(k_factor, d, 1, 0)
    packed_c = pack(limit, out_grads, zs, xs, ds, bs)
    gram_k = gram_part(k_factor)
    gram_c = gram_part(c_factor)
    packed_c, owned_k, blocks_c, own_k, gram_k, gram_c = lax.optimization_barrier(
        (packed_c, owned_k, blocks_c, own_k, gram_k, gram_c)
    )
    owned_c = exchange(packed_c)

    raw_k = raw_moments(ids, owned_k)
    sent_k = each_along_z(raw_k)
    stride = zs // 2
    mine = jnp.where(s == 0, load[:load_half], after(load_x, *sent_k))
    while stride > 1:
        got = down_z(mine, stride)
        mine = jnp.where(z % (2 * stride) == 0, mine, got)
        stride //= 2
    last_z = down_z(mine, 1)

    stat_k, trace_k = image_stats(ids, stat_scalars, sent_k, own_k)
    partial_c, square_c = stats(ids, after(owned_c, trace_k), blocks_c)
    rows8 = lax.broadcasted_iota(jnp.int32, (8, 128), 0)
    sums = jnp.where(
        rows8 == 0,
        trace_k,
        jnp.where(rows8 == 1, square_c, jnp.where(rows8 == 2, gram_k, gram_c)),
    )
    sent_c = each_along_z(partial_c)
    sums = jnp.broadcast_to(sums[None], (ds * shards, 8, 128))
    totals = jnp.sum(lax.all_to_all(sums, both, 0, 0, tiled=True), axis=0)[:, 0]
    for_k = jnp.stack([totals[1] / token_total, totals[3]])
    for_c = jnp.stack([totals[0], totals[2]])
    all_k = over_dp(after(stat_k, partial_c))
    mine = jnp.where(z % 2 == 0, mine, after(last_z, partial_c))
    other = lax.ppermute(mine, "fsdp", flip_x)
    load = jnp.concatenate([jnp.where(x == 0, mine, other), jnp.where(x == 0, other, mine)])
    lead_k, lead_c, grad_lead = load[:bs], load[bs : 2 * bs], load[2 * bs :]

    scale_width = float(width)
    k_factor_new, k_moment_new, kb = advance_all(
        scale_width, ids, for_k, all_k, k_factor, k_moment, lead_k
    )
    second, term = columns(ids, grad_weight, grad_lead, kb)
    count = grad_weight.shape[0]
    kept = lax.dynamic_slice_in_dim(term, x * (count // xs), count // xs, 0)
    passed = lax.dynamic_slice_in_dim(term, (1 - x) * (count // xs), count // xs, 0)
    passed = lax.ppermute(passed, "fsdp", flip_x)

    stat_c = mean_of([after(part, term) for part in sent_c])
    all_c = over_dp(stat_c)

    c_factor_new, c_moment_new, cb = advance_all(
        scale_width, ids, for_c, all_c, c_factor, c_moment, lead_c
    )
    halves = []
    for h in range(2):
        turn = 2 * h
        pairs = [
            (flat(r ^ turn, zz * xs + xx), flat(zz, r * xs + xx))
            for r in range(ds)
            for zz in range(zs)
            for xx in range(xs)
        ]
        halves.append(lax.ppermute(cb[h * (ds // 2) : (h + 1) * (ds // 2)], both, pairs))
    others = [lax.ppermute(h, "fsdp", flip_x) for h in halves]

    halved = (kept.astype(f32) + passed.astype(f32)).astype(bf16).reshape(zs, bs, bs)
    turned = [lax.dynamic_index_in_dim(halved, z ^ k, 0, keepdims=False) for k in range(zs)]
    got = [after(g, cb) for g in each_along_z(turned)]

    c_rows = jnp.concatenate(halves + others, axis=0)

    top_rest = from_group_0(second[:bs, bs:])

    block_sum = got[0].astype(f32)
    for g in got[1:]:
        block_sum = block_sum + g.astype(f32)
    block_sum = block_sum.astype(bf16)
    pair = jnp.stack([block_sum, lax.ppermute(block_sum, "fsdp", [(2 * k + 1, 2 * k) for k in range(zs)])])
    pair = after(pair, halves[0])
    gathered = [pair] + [lax.ppermute(pair, "fsdp", [(xs * k, 0)]) for k in range(1, zs)]
    top_lead = jnp.where(s == 0, block_sum, second[:bs, :bs])
    top_lead = from_group_0(top_lead)
    def sum_to_group_0(value):
        total = value.astype(f32) + lax.ppermute(value, "dp", [(2, 0), (3, 1)]).astype(f32)
        other = lax.ppermute(total.astype(bf16), "dp", [(1, 0)])
        return (total + other.astype(f32)).astype(bf16)

    precond, up_rest = rows(ids, second, top_rest, c_rows)
    gathered = [after(g, up_rest) for g in gathered]
    gathered = jnp.concatenate(gathered, axis=0).reshape(count, bs)
    up_rest = sum_to_group_0(up_rest)
    precond, up_lead = lead_rows_products(ids, second, gathered, top_lead, c_rows, precond)
    precond = put_top(ids, precond, sum_to_group_0(up_lead), up_rest)
    return (k_factor_new, c_factor_new, k_moment_new, c_moment_new, precond)


def spread(value, axis, source):
    kept = jnp.where(lax.axis_index(axis) == source, value, 0).astype(value.dtype)
    return lax.psum(kept, axis)


def owner_image(columns, lead_columns, diag_half, side_half):
    row_count = columns.shape[0]
    block_count = diag_half.shape[0]
    block_size = diag_half.shape[1]
    blocked = columns.reshape(row_count, block_count, block_size)
    image_sum = jnp.einsum("tnk,nkj->tnj", blocked, diag_half, preferred_element_type=jnp.float32)
    image_sum = image_sum + jnp.einsum(
        "tk,nkj->tnj", lead_columns, side_half, preferred_element_type=jnp.float32
    )
    return image_sum.astype(jnp.bfloat16).reshape(row_count, block_count * block_size)


def to_owners(pair):
    return (
        lax.all_to_all(pair[0], "fsdp", split_axis=1, concat_axis=0, tiled=True),
        lax.all_to_all(pair[1], "fsdp", split_axis=1, concat_axis=0, tiled=True),
    )


def fetch_lead(before):
    return (
        lax.all_gather(before[0], "fsdp", axis=0, tiled=True),
        lax.all_gather(before[1], "fsdp", axis=0, tiled=True),
    )


def block_stats(owned, lead_image, block_count, block_size):
    blocked = owned.reshape(owned.shape[0], block_count, block_size)
    own_sum = jnp.einsum("tni,tnj->nij", blocked, blocked, preferred_element_type=jnp.float32)
    cross_sum = jnp.einsum("ti,tnj->nij", lead_image, blocked, preferred_element_type=jnp.float32)
    return (own_sum, cross_sum)


def gram_trace(factor, border_keep):
    block_size = factor.shape[1]
    diag_part = factor[:, :, :block_size]
    side_part = factor[:, :, block_size:] * border_keep
    return jnp.sum(diag_part * diag_part) + jnp.sum(side_part * side_part)


def advance(factor, moment, own_sum, cross_sum, lead_block, border_keep, other_h, other_g, width):
    block_size = factor.shape[1]
    diag_part = factor[:, :, :block_size]
    side_part = factor[:, :, block_size:] * border_keep
    gram_diag = jnp.einsum("nki,nkj->nij", diag_part, diag_part, precision=highest)
    gram_diag = gram_diag + jnp.einsum("nki,nkj->nij", side_part, side_part, precision=highest)
    gram_side = jnp.einsum("ki,nkj->nij", lead_block, side_part, precision=highest)
    identity = jnp.eye(block_size, dtype=jnp.float32)
    fresh_diag = (other_h * own_sum + damping * other_g * gram_diag - width * identity) / (
        2.0 * width
    )
    fresh_side = (other_h * cross_sum + damping * other_g * gram_side) * border_keep / (2.0 * width)
    moment_diag = momentum_rate * moment[:, :, :block_size] + fresh_diag
    moment_side = (momentum_rate * moment[:, :, block_size:] + fresh_side) * border_keep
    new_diag = diag_part - step_rate * jnp.einsum(
        "nik,nkj->nij", diag_part, moment_diag, precision=highest
    )
    side_change = jnp.einsum("ik,nkj->nij", lead_block, moment_side, precision=highest)
    side_change = side_change + jnp.einsum(
        "nik,nkj->nij", side_part, moment_diag, precision=highest
    )
    new_side = (side_part - step_rate * side_change) * border_keep
    return (
        jnp.concatenate([new_diag, new_side], axis=-1),
        jnp.concatenate([moment_diag, moment_side], axis=-1),
    )


def general(acts, out_grads, token_counts, k_factor, c_factor, k_moment, c_moment, grad_weight):
    tok_dev, width = acts.shape
    blocks_dev = k_factor.shape[0]
    block_size = k_factor.shape[1]
    group_count = lax.axis_size("dp")
    shard_count = lax.axis_size("fsdp")
    group_id = lax.axis_index("dp")
    shard_id = lax.axis_index("fsdp")
    token_total = jnp.sum(token_counts).astype(jnp.float32)
    valid_limit = jnp.sum(jnp.where(lax.iota(jnp.int32, group_count) == group_id, token_counts, 0))
    positions = shard_id * tok_dev + lax.iota(jnp.int32, tok_dev)
    row_keep = (positions < valid_limit).astype(jnp.bfloat16)[:, None]
    masked_acts = acts * row_keep
    masked_grads = out_grads * row_keep
    block_ids = shard_id * blocks_dev + lax.iota(jnp.int32, blocks_dev)
    border_keep = (block_ids > 0).astype(jnp.float32)[:, None, None]
    lead_k, lead_c = (
        spread(k_factor[0, :, :block_size], "fsdp", 0),
        spread(c_factor[0, :, :block_size], "fsdp", 0),
    )
    raw_acts, raw_grads = to_owners((masked_acts, masked_grads))
    lead_raw_acts, lead_raw_grads = fetch_lead(
        (masked_acts[:, :block_size], masked_grads[:, :block_size])
    )
    k_diag_half = k_factor[:, :, :block_size].astype(jnp.bfloat16)
    k_side_half = (k_factor[:, :, block_size:] * border_keep).astype(jnp.bfloat16)
    c_diag_half = c_factor[:, :, :block_size].astype(jnp.bfloat16)
    c_side_half = (c_factor[:, :, block_size:] * border_keep).astype(jnp.bfloat16)
    owned_acts = owner_image(raw_acts, lead_raw_acts, k_diag_half, k_side_half)
    owned_grads = owner_image(raw_grads, lead_raw_grads, c_diag_half, c_side_half)
    lead_acts = jnp.dot(
        lead_raw_acts, lead_k.astype(jnp.bfloat16), preferred_element_type=jnp.float32
    ).astype(jnp.bfloat16)
    lead_grads = jnp.dot(
        lead_raw_grads, lead_c.astype(jnp.bfloat16), preferred_element_type=jnp.float32
    ).astype(jnp.bfloat16)
    own_k, cross_k = block_stats(owned_acts, lead_acts, blocks_dev, block_size)
    own_c, cross_c = block_stats(owned_grads, lead_grads, blocks_dev, block_size)
    summed = lax.psum((own_k, cross_k, own_c, cross_c), "dp")
    gram_k = gram_trace(k_factor, border_keep)
    gram_c = gram_trace(c_factor, border_keep)
    local_traces = jnp.stack(
        [
            jnp.sum(jnp.trace(summed[0], axis1=1, axis2=2)),
            jnp.sum(jnp.trace(summed[2], axis1=1, axis2=2)),
            gram_k,
            gram_c,
        ]
    )
    totals = lax.psum(local_traces, "fsdp")
    trace_hk = totals[0] / token_total
    trace_hc = totals[1] / token_total
    scale_width = float(width)
    k_factor_new, k_moment_new = advance(
        k_factor,
        k_moment,
        summed[0] / token_total,
        summed[1] / token_total,
        lead_k,
        border_keep,
        trace_hc,
        totals[3],
        scale_width,
    )
    c_factor_new, c_moment_new = advance(
        c_factor,
        c_moment,
        summed[2] / token_total,
        summed[3] / token_total,
        lead_c,
        border_keep,
        trace_hk,
        totals[2],
        scale_width,
    )
    grad_rows = grad_weight.shape[0]
    grad_lead = spread(grad_weight[:, :block_size], "fsdp", 0)
    k_diag = k_factor_new[:, :, :block_size].astype(jnp.bfloat16)
    k_side = k_factor_new[:, :, block_size:].astype(jnp.bfloat16)
    grad_blocked = grad_weight.reshape(grad_rows, blocks_dev, block_size)
    first_sum = jnp.einsum("rnk,nkj->rnj", grad_blocked, k_diag, preferred_element_type=jnp.float32)
    first_sum = first_sum + jnp.einsum(
        "rk,nkj->rnj", grad_lead, k_side, preferred_element_type=jnp.float32
    )
    first_product = first_sum.astype(jnp.bfloat16)
    own_second = jnp.einsum(
        "rnk,njk->rnj", first_product, k_diag, preferred_element_type=jnp.float32
    )
    lead_term = jnp.einsum("rnk,njk->rj", first_product, k_side, preferred_element_type=jnp.float32)
    lead_sum = lax.psum(lead_term, "fsdp")
    lead_mask = (block_ids == 0).astype(jnp.float32)[None, :, None]
    second_product = (own_second + lead_mask * lead_sum[:, None, :]).astype(jnp.bfloat16)
    row_blocks = grad_rows // block_size
    owner_count = shard_count // group_count
    c_half = c_factor_new.astype(jnp.bfloat16)
    fetched = []
    for owner_step in range(owner_count):
        fetched.append(spread(c_half, "fsdp", group_id * owner_count + owner_step))
    row_factor = jnp.concatenate(fetched, axis=0)
    c_diag = row_factor[:, :, :block_size]
    c_side = row_factor[:, :, block_size:]
    by_rows = second_product.reshape(row_blocks, block_size, blocks_dev * block_size)
    lead_rows = spread(by_rows[0], "dp", 0)
    third_sum = jnp.einsum("nki,nkc->nic", c_diag, by_rows, preferred_element_type=jnp.float32)
    third_sum = third_sum + jnp.einsum(
        "nki,kc->nic", c_side, lead_rows, preferred_element_type=jnp.float32
    )
    third_product = third_sum.astype(jnp.bfloat16)
    own_fourth = jnp.einsum(
        "nik,nkc->nic", c_diag, third_product, preferred_element_type=jnp.float32
    )
    row_term = jnp.einsum("nik,nkc->ic", c_side, third_product, preferred_element_type=jnp.float32)
    row_sum = lax.psum(row_term, "dp")
    row_ids = group_id * row_blocks + lax.iota(jnp.int32, row_blocks)
    row_mask = (row_ids == 0).astype(jnp.float32)[:, None, None]
    precond = (
        (own_fourth + row_mask * row_sum[None, :, :])
        .astype(jnp.bfloat16)
        .reshape(grad_rows, blocks_dev * block_size)
    )
    return (k_factor_new, c_factor_new, k_moment_new, c_moment_new, precond)


def per_device(*args):
    blocks = args[3].shape[0]
    groups, shards = lax.axis_size("dp"), lax.axis_size("fsdp")
    fits = blocks == 4 and groups == 4 and shards == 8
    return (planned if fits else general)(*args)


def solution(mesh):
    in_specs = (
        P(("dp", "fsdp"), None),
        P(("dp", "fsdp"), None),
        P(),
        P("fsdp", None, None),
        P("fsdp", None, None),
        P("fsdp", None, None),
        P("fsdp", None, None),
        P("dp", "fsdp"),
    )
    out_specs = (
        P("fsdp", None, None),
        P("fsdp", None, None),
        P("fsdp", None, None),
        P("fsdp", None, None),
        P("dp", "fsdp"),
    )
    return jax.shard_map(
        per_device, mesh=mesh, in_specs=in_specs, out_specs=out_specs, check_vma=False
    )
```

```python
import functools

import jax
import jax.numpy as jnp
from jax import lax
from jax.experimental import pallas as pl
from jax.experimental.pallas import tpu as pltpu
from jax.sharding import PartitionSpec as P

damping = 0.1
momentum_rate = 0.5
step_rate = 0.2
highest = lax.Precision.HIGHEST
both = ("dp", "fsdp")
f32 = jnp.float32
bf16 = jnp.bfloat16
vmem_cap = 48 * 1024 * 1024


def params(*semantics):
    return pltpu.CompilerParams(dimension_semantics=semantics, vmem_limit_bytes=vmem_cap)


light = pl.CostEstimate(flops=1, transcendentals=0, bytes_accessed=1)


def dot(a, b, dims=((1,), (0,)), precision=None):
    return lax.dot_general(a, b, (dims, ((), ())), precision=precision, preferred_element_type=f32)


nn = ((1,), (0,))
tn = ((0,), (0,))
nt = ((1,), (1,))


def fold(full):
    half = full.shape[0] // 2
    low = full[half:, half:]
    low = jnp.concatenate([low[: half // 2], low[half // 2 :]], axis=1)
    return jnp.concatenate([full[:half], low], axis=0)


def unfold(packed):
    half = packed.shape[1] // 2
    top = packed[:half]
    low = packed[half:]
    low = jnp.concatenate([low[:, :half], low[:, half:]], axis=0)
    low = jnp.concatenate([top[:, half:].T, low], axis=1)
    return jnp.concatenate([top, low], axis=0)


def pack_body(zs, xs, ds, bs, tile, count_ref, a_ref, o_ref):
    start = (lax.axis_index("fsdp") * pl.num_programs(0) + pl.program_id(0)) * tile
    rows = start + lax.broadcasted_iota(jnp.int32, (tile, bs), 0)
    keep = jnp.where(rows < count_ref[lax.axis_index("dp")], 1.0, 0.0).astype(bf16)
    lead = a_ref[:, :bs] * keep
    for d in range(ds):
        for x in range(xs):
            for z in range(zs):
                n = (z * xs + x) * ds + d
                o_ref[d * xs + x, z] = a_ref[:, n * bs : (n + 1) * bs] * keep
            o_ref[d * xs + x, zs] = lead


def pack(token_counts, tokens, zs, xs, ds, bs):
    count, width = tokens.shape
    tile = 32
    return pl.pallas_call(
        functools.partial(pack_body, zs, xs, ds, bs, tile),
        grid=(count // tile,),
        in_specs=[
            pl.BlockSpec(memory_space=pltpu.SMEM),
            pl.BlockSpec((tile, width), lambda i: (i, 0)),
        ],
        out_specs=pl.BlockSpec((ds * xs, zs + 1, tile, bs), lambda i: (0, 0, i, 0)),
        out_shape=jax.ShapeDtypeStruct((ds * xs, zs + 1, count, bs), bf16),
        cost_estimate=light,
        compiler_params=params("arbitrary"),
        name="pack_tokens",
    )(token_counts, tokens)


def moments_body(ids_ref, x_ref, l_ref, o_ref):
    groups, _, count, bs = x_ref.shape
    cols = x_ref[:, 0].reshape(groups * count, bs)
    lead = l_ref[:, 0].reshape(groups * count, bs)
    fold_rows = 3 * bs // 4
    o_ref[0, :fold_rows] = fold(dot(cols, cols, tn)).astype(bf16)
    o_ref[0, fold_rows : fold_rows + bs] = dot(lead, cols, tn).astype(bf16)
    o_ref[0, fold_rows + bs :] = fold(dot(lead, lead, tn)).astype(bf16)


def raw_moments(ids, owned):
    groups, slots, count, bs = owned.shape
    zs = slots - 1
    return pl.pallas_call(
        moments_body,
        grid_spec=pltpu.PrefetchScalarGridSpec(
            num_scalar_prefetch=1,
            grid=(zs,),
            in_specs=[
                pl.BlockSpec((groups, 1, count, bs), lambda k, ids: (0, ids[0] ^ k, 0, 0)),
                pl.BlockSpec((groups, 1, count, bs), lambda k, ids: (0, zs, 0, 0)),
            ],
            out_specs=pl.BlockSpec((1, 5 * bs // 2, bs), lambda k, ids: (k, 0, 0)),
        ),
        out_shape=jax.ShapeDtypeStruct((zs, 5 * bs // 2, bs), bf16),
        cost_estimate=light,
        compiler_params=params("arbitrary"),
        name="raw_moments",
    )(ids, owned, owned)


def image_stats_body(count, ids_ref, sc_ref, *refs):
    parts = refs[:count]
    fac_ref, h_ref, tr_ref = refs[count:]
    bs = fac_ref.shape[1]
    keep = jnp.where(ids_ref[2] + ids_ref[1] > 0, 1.0, 0.0)
    total = parts[0][...].astype(f32)
    for part in parts[1:]:
        total = total + part[...].astype(f32)
    fold_rows = 3 * bs // 4
    own_raw = unfold(total[:fold_rows])
    cross_raw = total[fold_rows : fold_rows + bs]
    lead_raw = unfold(total[fold_rows + bs :])
    fac = fac_ref[0]
    bn = fac[:, :bs].astype(bf16).astype(f32)
    pn = (fac[:, bs:] * keep).astype(bf16).astype(f32)
    mm = functools.partial(dot, precision=highest)
    t1 = mm(own_raw, bn) + mm(cross_raw, pn, tn)
    t0 = mm(cross_raw, bn) + mm(lead_raw, pn)
    own = (mm(bn, t1, tn) + mm(pn, t0, tn)) * sc_ref[0]
    h_ref[:fold_rows] = fold(own).astype(bf16)
    h_ref[fold_rows:] = (t0 * sc_ref[0]).astype(bf16)
    row = lax.broadcasted_iota(jnp.int32, (bs, bs), 0)
    col = lax.broadcasted_iota(jnp.int32, (bs, bs), 1)
    tr_ref[...] = jnp.zeros_like(tr_ref) + jnp.sum(jnp.where(row == col, own, 0.0))


def image_stats(ids, scalars, parts, factor):
    _, bs, wide = factor.shape
    whole = lambda shape: pl.BlockSpec(shape, lambda i, ids: (0,) * len(shape))
    return pl.pallas_call(
        functools.partial(image_stats_body, len(parts)),
        grid_spec=pltpu.PrefetchScalarGridSpec(
            num_scalar_prefetch=1,
            grid=(1,),
            in_specs=[pl.BlockSpec(memory_space=pltpu.SMEM)]
            + [whole(part.shape) for part in parts]
            + [pl.BlockSpec((1, bs, wide), lambda i, ids: (0, 0, 0))],
            out_specs=[whole((7 * bs // 4, bs)), whole((8, 128))],
        ),
        out_shape=[
            jax.ShapeDtypeStruct((7 * bs // 4, bs), bf16),
            jax.ShapeDtypeStruct((8, 128), f32),
        ],
        cost_estimate=light,
        compiler_params=params("arbitrary"),
        name="image_stats",
    )(ids, scalars, *parts, factor)


def stats_body(x_ref, l_ref, f_ref, o_ref, t_ref):
    groups, _, count, bs = x_ref.shape
    k = pl.program_id(0)
    cols = x_ref[:, 0].reshape(groups * count, bs)
    lead = l_ref[:, 0].reshape(groups * count, bs)

    @pl.when(k == 0)
    def _():
        t_ref[...] = jnp.zeros_like(t_ref)

    image = (dot(cols, f_ref[0, :, :bs]) + dot(lead, f_ref[0, :, bs:])).astype(bf16)
    fold_rows = 3 * bs // 4
    o_ref[0, :fold_rows] = fold(dot(image, image, tn)).astype(bf16)
    o_ref[0, fold_rows:] = dot(lead, image, tn).astype(bf16)
    wide = image.astype(f32)
    t_ref[...] = t_ref[...] + jnp.sum(wide * wide)


def stats(ids, owned, blocks):
    groups, slots, count, bs = owned.shape
    zs = slots - 1

    def body(ids_ref, *refs):
        stats_body(*refs)

    return pl.pallas_call(
        body,
        grid_spec=pltpu.PrefetchScalarGridSpec(
            num_scalar_prefetch=1,
            grid=(zs,),
            in_specs=[
                pl.BlockSpec((groups, 1, count, bs), lambda k, ids: (0, ids[0] ^ k, 0, 0)),
                pl.BlockSpec((groups, 1, count, bs), lambda k, ids: (0, zs, 0, 0)),
                pl.BlockSpec((1, bs, 2 * bs), lambda k, ids: (k, 0, 0)),
            ],
            out_specs=[
                pl.BlockSpec((1, 7 * bs // 4, bs), lambda k, ids: (k, 0, 0)),
                pl.BlockSpec((8, 128), lambda k, ids: (0, 0)),
            ],
        ),
        out_shape=[
            jax.ShapeDtypeStruct((zs, 7 * bs // 4, bs), bf16),
            jax.ShapeDtypeStruct((8, 128), f32),
        ],
        cost_estimate=light,
        compiler_params=params("arbitrary"),
        name="plane_stats",
    )(ids, owned, owned, blocks)


def advance_block(width, own, cross, fac, mom, b0, other_h, other_g, keep):
    bs = fac.shape[0]
    diag = fac[:, :bs]
    side = fac[:, bs:] * keep
    db = diag.astype(bf16)
    sb = side.astype(bf16)
    gram_d = dot(db, db, tn) + dot(sb, sb, tn)
    gram_s = dot(b0, sb, tn)
    row = lax.broadcasted_iota(jnp.int32, (bs, bs), 0)
    col = lax.broadcasted_iota(jnp.int32, (bs, bs), 1)
    ident = jnp.where(row == col, width, 0.0)
    scale = 1.0 / (2.0 * width)
    md = momentum_rate * mom[:, :bs] + (other_h * own + damping * other_g * gram_d - ident) * scale
    ms = momentum_rate * mom[:, bs:] + (other_h * cross + damping * other_g * gram_s) * scale
    ms = ms * keep
    mdb = md.astype(bf16)
    new_d = diag - step_rate * dot(db, mdb)
    new_s = side - step_rate * (dot(b0, ms.astype(bf16)) + dot(sb, mdb)) * keep
    return md, ms, new_d, new_s


def order_of(ids, m):
    return ids[1] ^ ((m & 1) * 2 + (m >> 1))


def advance_body(width, ids_ref, sc_ref, h_ref, fac_ref, mom_ref, lead_ref, fn_ref, mn_ref, fb_ref):
    bs = lead_ref.shape[0]
    j = order_of(ids_ref, pl.program_id(0))
    keep = jnp.where(ids_ref[2] + j > 0, 1.0, 0.0)
    md, ms, new_d, new_s = advance_block(
        width,
        unfold(h_ref[0, : 3 * bs // 4].astype(f32)),
        dot(lead_ref[...], h_ref[0, 3 * bs // 4 :], tn),
        fac_ref[0],
        mom_ref[0],
        lead_ref[...],
        sc_ref[0],
        sc_ref[1],
        keep,
    )
    fn_ref[0, :, :bs] = new_d
    fn_ref[0, :, bs:] = new_s
    mn_ref[0, :, :bs] = md
    mn_ref[0, :, bs:] = ms
    fb_ref[0, :, :bs] = new_d.astype(bf16)
    fb_ref[0, :, bs:] = new_s.astype(bf16)


def advance_all(width, ids, scalars, stats, factor, moment, lead):
    blocks, bs, wide = factor.shape
    spec = pl.BlockSpec((1, bs, wide), lambda m, ids: (order_of(ids, m), 0, 0))
    return pl.pallas_call(
        functools.partial(advance_body, width),
        grid_spec=pltpu.PrefetchScalarGridSpec(
            num_scalar_prefetch=1,
            grid=(blocks,),
            in_specs=[
                pl.BlockSpec(memory_space=pltpu.SMEM),
                pl.BlockSpec((1, 7 * bs // 4, bs), lambda m, ids: (m, 0, 0)),
                spec,
                spec,
                pl.BlockSpec((bs, bs), lambda m, ids: (0, 0)),
            ],
            out_specs=[spec, spec, spec],
        ),
        out_shape=[
            jax.ShapeDtypeStruct(factor.shape, f32),
            jax.ShapeDtypeStruct(factor.shape, f32),
            jax.ShapeDtypeStruct(factor.shape, bf16),
        ],
        cost_estimate=light,
        compiler_params=params("arbitrary"),
        name="advance_all",
    )(ids, scalars, stats, factor, moment, lead)


def columns_body(ids_ref, g_ref, l_ref, k_ref, s_ref, t_ref):
    blocks, bs, _ = k_ref.shape
    lead = l_ref[...]
    term = None
    for n in range(blocks):
        kd = k_ref[n, :, :bs]
        ks = k_ref[n, :, bs:]
        first = (dot(g_ref[:, n * bs : (n + 1) * bs], kd) + dot(lead, ks)).astype(bf16)
        second = dot(first, kd, nt)
        s_ref[:, n * bs : (n + 1) * bs] = second.astype(bf16)
        part = dot(first, ks, nt)
        if n == 0:
            part = part + second * jnp.where(ids_ref[2] == 0, 1.0, 0.0)
        term = part if term is None else term + part
    t_ref[...] = term.astype(bf16)


def columns(ids, grad, lead, kb):
    rows, wide = grad.shape
    blocks, bs, _ = kb.shape
    tile = 512
    return pl.pallas_call(
        columns_body,
        grid_spec=pltpu.PrefetchScalarGridSpec(
            num_scalar_prefetch=1,
            grid=(rows // tile,),
            in_specs=[
                pl.BlockSpec((tile, wide), lambda i, ids: (i, 0)),
                pl.BlockSpec((tile, bs), lambda i, ids: (i, 0)),
                pl.BlockSpec(kb.shape, lambda i, ids: (0, 0, 0)),
            ],
            out_specs=[
                pl.BlockSpec((tile, wide), lambda i, ids: (i, 0)),
                pl.BlockSpec((tile, bs), lambda i, ids: (i, 0)),
            ],
        ),
        out_shape=[
            jax.ShapeDtypeStruct((rows, wide), bf16),
            jax.ShapeDtypeStruct((rows, bs), bf16),
        ],
        cost_estimate=light,
        compiler_params=params("arbitrary"),
        name="column_products",
    )(ids, grad, lead, kb)


def row_of(ids, k):
    per = ids[4]
    return ((ids[3] & 1) ^ (k // per)) * per + k % per


def gathered_at(ids, k):
    i = row_of(ids, k)
    return (i % ids[4]) * 2 + i // ids[4]


def rows_body(ids_ref, s_ref, l_ref, c_ref, p_ref, u_ref, acc_ref):
    k = pl.program_id(0)
    bs = c_ref.shape[1]
    cd = c_ref[0, :, :bs]
    cs = c_ref[0, :, bs:]
    third = (dot(cd, s_ref[:, bs:], tn) + dot(cs, l_ref[...], tn)).astype(bf16)
    pair = dot(jnp.concatenate([cd, cs], axis=0), third)
    fourth = pair[:bs]
    p_ref[:, bs:] = fourth.astype(bf16)
    is_first = (ids_ref[1] == 0) & (row_of(ids_ref, k) == 0)
    term = pair[bs:] + fourth * jnp.where(is_first, 1.0, 0.0)

    @pl.when(k == 0)
    def _():
        acc_ref[...] = term

    @pl.when(k > 0)
    def _():
        acc_ref[...] = acc_ref[...] + term

    @pl.when(k == pl.num_programs(0) - 1)
    def _():
        u_ref[...] = acc_ref[...].astype(bf16)


def rows(ids, second, lead, cb):
    count, wide = second.shape
    blocks, bs, _ = cb.shape
    rest = wide - bs
    spec = pl.BlockSpec((bs, wide), lambda k, ids: (row_of(ids, k), 0))
    whole = pl.BlockSpec((bs, rest), lambda k, ids: (0, 0))
    return pl.pallas_call(
        rows_body,
        grid_spec=pltpu.PrefetchScalarGridSpec(
            num_scalar_prefetch=1,
            grid=(blocks,),
            in_specs=[
                spec,
                whole,
                pl.BlockSpec((1, bs, 2 * bs), lambda k, ids: (k, 0, 0)),
            ],
            out_specs=[spec, whole],
            scratch_shapes=[pltpu.VMEM((bs, rest), f32)],
        ),
        out_shape=[
            jax.ShapeDtypeStruct((count, wide), bf16),
            jax.ShapeDtypeStruct((bs, rest), bf16),
        ],
        cost_estimate=light,
        compiler_params=params("arbitrary"),
        name="row_products",
    )(ids, second, lead, cb)


def lead_rows_body(ids_ref, s_ref, g_ref, l_ref, c_ref, _, p_ref, u_ref):
    blocks, bs, _ = c_ref.shape
    total = jnp.zeros((bs, bs), f32)
    for k in range(blocks):
        i = row_of(ids_ref, k)
        own = s_ref[pl.ds(pl.multiple_of(i * bs, bs), bs), :]
        whole = g_ref[pl.ds(pl.multiple_of(gathered_at(ids_ref, k) * bs, bs), bs), :]
        second = jnp.where(ids_ref[3] == 0, whole, own)
        cd = c_ref[k, :, :bs]
        cs = c_ref[k, :, bs:]
        third = (dot(cd, second, tn) + dot(cs, l_ref[...], tn)).astype(bf16)
        pair = dot(jnp.concatenate([cd, cs], axis=0), third)
        fourth = pair[:bs]
        p_ref[pl.ds(pl.multiple_of(i * bs, bs), bs), :] = fourth.astype(bf16)
        is_first = (ids_ref[1] == 0) & (i == 0)
        total = total + pair[bs:] + fourth * jnp.where(is_first, 1.0, 0.0)
    u_ref[...] = total.astype(bf16)


def lead_rows_products(ids, second, gathered, lead, cb, tile):
    count, _ = second.shape
    blocks, bs, _ = cb.shape
    column = pl.BlockSpec((count, bs), lambda i, ids: (0, 0))
    square = pl.BlockSpec((bs, bs), lambda i, ids: (0, 0))
    return pl.pallas_call(
        lead_rows_body,
        grid_spec=pltpu.PrefetchScalarGridSpec(
            num_scalar_prefetch=1,
            grid=(1,),
            in_specs=[
                column,
                column,
                square,
                pl.BlockSpec(cb.shape, lambda i, ids: (0, 0, 0)),
                pl.BlockSpec(memory_space=pl.ANY),
            ],
            out_specs=[column, square],
        ),
        out_shape=[
            jax.ShapeDtypeStruct(tile.shape, bf16),
            jax.ShapeDtypeStruct((bs, bs), bf16),
        ],
        input_output_aliases={5: 0},
        cost_estimate=light,
        compiler_params=params("arbitrary"),
        name="lead_row_products",
    )(ids, second, gathered, lead, cb, tile)


def put_top_body(ids_ref, p_ref, lead_ref, rest_ref, o_ref):
    bs = lead_ref.shape[1]
    first = ids_ref[1] == 0

    @pl.when(first)
    def _():
        o_ref[:, :bs] = lead_ref[...]
        o_ref[:, bs:] = rest_ref[...]

    @pl.when(jnp.logical_not(first))
    def _():
        o_ref[...] = p_ref[...]


def put_top(ids, tile, lead, rest):
    bs = lead.shape[0]
    spec = lambda width: pl.BlockSpec((bs, width), lambda i, ids: (0, 0))
    top = spec(tile.shape[1])
    return pl.pallas_call(
        put_top_body,
        grid_spec=pltpu.PrefetchScalarGridSpec(
            num_scalar_prefetch=1,
            grid=(1,),
            in_specs=[top, spec(bs), spec(rest.shape[1])],
            out_specs=top,
        ),
        out_shape=jax.ShapeDtypeStruct(tile.shape, tile.dtype),
        input_output_aliases={1: 0},
        cost_estimate=light,
        compiler_params=params("arbitrary"),
        name="put_top",
    )(ids, tile, lead, rest)


def after(value, *earlier):
    return lax.optimization_barrier((value,) + earlier)[0]


def planned(acts, out_grads, token_counts, k_factor, c_factor, k_moment, c_moment, grad_weight):
    tok_dev, width = acts.shape
    ds, bs, _ = k_factor.shape
    shards = lax.axis_size("fsdp")
    xs = 2
    zs = shards // xs
    d = lax.axis_index("dp")
    s = lax.axis_index("fsdp")
    x = s % xs
    z = s // xs
    flat = lambda dd, ss: dd * shards + ss
    plane = [[flat(dd, zz * xs + xx) for dd in range(ds) for xx in range(xs)] for zz in range(zs)]
    flip_x = [(i, i ^ 1) for i in range(shards)]
    ids = jnp.stack([z, d, s * ds, s, jnp.int32(ds)]).astype(jnp.int32)
    token_total = jnp.sum(token_counts).astype(f32)
    stat_scalars = (1.0 / token_total).reshape(1)

    def along_z(value, k):
        pairs = [(zz * xs + xx, (zz ^ k) * xs + xx) for zz in range(zs) for xx in range(xs)]
        return lax.ppermute(value, "fsdp", pairs)

    def from_group_0(value):
        value = jnp.where(d == 0, value, lax.ppermute(value, "dp", [(0, 2)]))
        return jnp.where(d % 2 == 0, value, lax.ppermute(value, "dp", [(0, 1), (2, 3)]))

    def block_along_z(factor, *earlier):
        own = lax.dynamic_index_in_dim(factor, d, 0, keepdims=False)
        side_keep = jnp.where(s * ds + d > 0, 1.0, 0.0)
        own = jnp.concatenate([own[:, :bs], own[:, bs:] * side_keep], axis=1).astype(bf16)
        own = after(own, *earlier)
        return jnp.stack([own] + [along_z(own, k) for k in range(1, zs)])

    def mean_of(parts):
        total = parts[0].astype(f32)
        for part in parts[1:]:
            total = total + part.astype(f32)
        return (total / token_total).astype(bf16)

    def each_along_z(partial):
        return [partial[0]] + [along_z(partial[k], k) for k in range(1, zs)]

    def over_dp(value):
        pair = jnp.stack([value, lax.ppermute(value, "dp", [(i, i ^ 2) for i in range(ds)])])
        other = lax.ppermute(pair, "dp", [(i, i ^ 1) for i in range(ds)])
        return jnp.concatenate([pair, other], axis=0)

    def gram_part(factor):
        block_ids = s * ds + lax.iota(jnp.int32, ds)
        keep = (block_ids > 0).astype(f32)[:, None, None]
        side = factor[:, :, bs:] * keep
        return (jnp.sum(factor[:, :, :bs] ** 2) + jnp.sum(side * side)) / ds

    def exchange(packed):
        return lax.all_to_all(packed, both, 0, 0, tiled=True, axis_index_groups=plane)

    load = jnp.concatenate(
        [k_factor[0, :, :bs].astype(bf16), c_factor[0, :, :bs].astype(bf16), grad_weight[:, :bs]]
    )
    load_half = load.shape[0] // xs
    load_x = lax.ppermute(load[load_half:], "fsdp", [(0, 1)])

    def down_z(value, stride):
        pairs = [
            (zz * xs + xx, (zz + stride) * xs + xx)
            for zz in range(0, zs, 2 * stride)
            for xx in range(xs)
        ]
        return lax.ppermute(value, "fsdp", pairs)

    owned_k = exchange(pack(token_counts, acts, zs, xs, ds, bs))
    blocks_c = block_along_z(c_factor)
    own_k = lax.dynamic_slice_in_dim(k_factor, d, 1, 0)
    packed_c = pack(token_counts, out_grads, zs, xs, ds, bs)
    gram_k = gram_part(k_factor)
    gram_c = gram_part(c_factor)
    packed_c, owned_k, blocks_c, own_k, gram_k, gram_c = lax.optimization_barrier(
        (packed_c, owned_k, blocks_c, own_k, gram_k, gram_c)
    )
    owned_c = exchange(packed_c)

    raw_k = raw_moments(ids, owned_k)
    sent_k = each_along_z(raw_k)
    stride = zs // 2
    mine = jnp.where(s == 0, load[:load_half], after(load_x, *sent_k))
    while stride > 1:
        got = down_z(mine, stride)
        mine = jnp.where(z % (2 * stride) == 0, mine, got)
        stride //= 2
    last_z = down_z(mine, 1)

    stat_k, trace_k = image_stats(ids, stat_scalars, sent_k, own_k)
    partial_c, square_c = stats(ids, after(owned_c, trace_k), blocks_c)
    rows8 = lax.broadcasted_iota(jnp.int32, (8, 128), 0)
    sums = jnp.where(
        rows8 == 0,
        trace_k,
        jnp.where(rows8 == 1, square_c, jnp.where(rows8 == 2, gram_k, gram_c)),
    )
    sent_c = each_along_z(partial_c)
    sums = jnp.broadcast_to(sums[None], (ds * shards, 8, 128))
    totals = jnp.sum(lax.all_to_all(sums, both, 0, 0, tiled=True), axis=0)[:, 0]
    for_k = jnp.stack([totals[1] / token_total, totals[3]])
    for_c = jnp.stack([totals[0], totals[2]])
    all_k = over_dp(after(stat_k, partial_c))
    mine = jnp.where(z % 2 == 0, mine, after(last_z, partial_c))
    other = lax.ppermute(mine, "fsdp", flip_x)
    load = jnp.concatenate([jnp.where(x == 0, mine, other), jnp.where(x == 0, other, mine)])
    lead_k, lead_c, grad_lead = load[:bs], load[bs : 2 * bs], load[2 * bs :]

    scale_width = float(width)
    k_factor_new, k_moment_new, kb = advance_all(
        scale_width, ids, for_k, all_k, k_factor, k_moment, lead_k
    )
    second, term = columns(ids, grad_weight, grad_lead, kb)
    count = grad_weight.shape[0]
    kept = lax.dynamic_slice_in_dim(term, x * (count // xs), count // xs, 0)
    passed = lax.dynamic_slice_in_dim(term, (1 - x) * (count // xs), count // xs, 0)
    passed = lax.ppermute(passed, "fsdp", flip_x)

    stat_c = mean_of([after(part, term) for part in sent_c])
    all_c = over_dp(stat_c)

    c_factor_new, c_moment_new, cb = advance_all(
        scale_width, ids, for_c, all_c, c_factor, c_moment, lead_c
    )
    halves = []
    for h in range(2):
        turn = 2 * h
        pairs = [
            (flat(r ^ turn, zz * xs + xx), flat(zz, r * xs + xx))
            for r in range(ds)
            for zz in range(zs)
            for xx in range(xs)
        ]
        halves.append(lax.ppermute(cb[h * (ds // 2) : (h + 1) * (ds // 2)], both, pairs))
    others = [lax.ppermute(h, "fsdp", flip_x) for h in halves]

    halved = (kept.astype(f32) + passed.astype(f32)).astype(bf16).reshape(zs, bs, bs)
    turned = [lax.dynamic_index_in_dim(halved, z ^ k, 0, keepdims=False) for k in range(zs)]
    got = [after(g, cb) for g in each_along_z(turned)]

    c_rows = jnp.concatenate(halves + others, axis=0)

    top_rest = from_group_0(second[:bs, bs:])

    block_sum = got[0].astype(f32)
    for g in got[1:]:
        block_sum = block_sum + g.astype(f32)
    block_sum = block_sum.astype(bf16)
    pair = jnp.stack([block_sum, lax.ppermute(block_sum, "fsdp", [(2 * k + 1, 2 * k) for k in range(zs)])])
    pair = after(pair, halves[0])
    gathered = [pair] + [lax.ppermute(pair, "fsdp", [(xs * k, 0)]) for k in range(1, zs)]
    top_lead = jnp.where(s == 0, block_sum, second[:bs, :bs])
    top_lead = from_group_0(top_lead)
    def sum_to_group_0(value):
        total = value.astype(f32) + lax.ppermute(value, "dp", [(2, 0), (3, 1)]).astype(f32)
        other = lax.ppermute(total.astype(bf16), "dp", [(1, 0)])
        return (total + other.astype(f32)).astype(bf16)

    precond, up_rest = rows(ids, second, top_rest, c_rows)
    gathered = [after(g, up_rest) for g in gathered]
    gathered = jnp.concatenate(gathered, axis=0).reshape(count, bs)
    up_rest = sum_to_group_0(up_rest)
    precond, up_lead = lead_rows_products(ids, second, gathered, top_lead, c_rows, precond)
    precond = put_top(ids, precond, sum_to_group_0(up_lead), up_rest)
    return (k_factor_new, c_factor_new, k_moment_new, c_moment_new, precond)


def spread(value, axis, source):
    kept = jnp.where(lax.axis_index(axis) == source, value, 0).astype(value.dtype)
    return lax.psum(kept, axis)


def owner_image(columns, lead_columns, diag_half, side_half):
    row_count = columns.shape[0]
    block_count = diag_half.shape[0]
    block_size = diag_half.shape[1]
    blocked = columns.reshape(row_count, block_count, block_size)
    image_sum = jnp.einsum("tnk,nkj->tnj", blocked, diag_half, preferred_element_type=jnp.float32)
    image_sum = image_sum + jnp.einsum(
        "tk,nkj->tnj", lead_columns, side_half, preferred_element_type=jnp.float32
    )
    return image_sum.astype(jnp.bfloat16).reshape(row_count, block_count * block_size)


def to_owners(pair):
    return (
        lax.all_to_all(pair[0], "fsdp", split_axis=1, concat_axis=0, tiled=True),
        lax.all_to_all(pair[1], "fsdp", split_axis=1, concat_axis=0, tiled=True),
    )


def fetch_lead(before):
    return (
        lax.all_gather(before[0], "fsdp", axis=0, tiled=True),
        lax.all_gather(before[1], "fsdp", axis=0, tiled=True),
    )


def block_stats(owned, lead_image, block_count, block_size):
    blocked = owned.reshape(owned.shape[0], block_count, block_size)
    own_sum = jnp.einsum("tni,tnj->nij", blocked, blocked, preferred_element_type=jnp.float32)
    cross_sum = jnp.einsum("ti,tnj->nij", lead_image, blocked, preferred_element_type=jnp.float32)
    return (own_sum, cross_sum)


def gram_trace(factor, border_keep):
    block_size = factor.shape[1]
    diag_part = factor[:, :, :block_size]
    side_part = factor[:, :, block_size:] * border_keep
    return jnp.sum(diag_part * diag_part) + jnp.sum(side_part * side_part)


def advance(factor, moment, own_sum, cross_sum, lead_block, border_keep, other_h, other_g, width):
    block_size = factor.shape[1]
    diag_part = factor[:, :, :block_size]
    side_part = factor[:, :, block_size:] * border_keep
    gram_diag = jnp.einsum("nki,nkj->nij", diag_part, diag_part, precision=highest)
    gram_diag = gram_diag + jnp.einsum("nki,nkj->nij", side_part, side_part, precision=highest)
    gram_side = jnp.einsum("ki,nkj->nij", lead_block, side_part, precision=highest)
    identity = jnp.eye(block_size, dtype=jnp.float32)
    fresh_diag = (other_h * own_sum + damping * other_g * gram_diag - width * identity) / (
        2.0 * width
    )
    fresh_side = (other_h * cross_sum + damping * other_g * gram_side) * border_keep / (2.0 * width)
    moment_diag = momentum_rate * moment[:, :, :block_size] + fresh_diag
    moment_side = (momentum_rate * moment[:, :, block_size:] + fresh_side) * border_keep
    new_diag = diag_part - step_rate * jnp.einsum(
        "nik,nkj->nij", diag_part, moment_diag, precision=highest
    )
    side_change = jnp.einsum("ik,nkj->nij", lead_block, moment_side, precision=highest)
    side_change = side_change + jnp.einsum(
        "nik,nkj->nij", side_part, moment_diag, precision=highest
    )
    new_side = (side_part - step_rate * side_change) * border_keep
    return (
        jnp.concatenate([new_diag, new_side], axis=-1),
        jnp.concatenate([moment_diag, moment_side], axis=-1),
    )


def general(acts, out_grads, token_counts, k_factor, c_factor, k_moment, c_moment, grad_weight):
    tok_dev, width = acts.shape
    blocks_dev = k_factor.shape[0]
    block_size = k_factor.shape[1]
    group_count = lax.axis_size("dp")
    shard_count = lax.axis_size("fsdp")
    group_id = lax.axis_index("dp")
    shard_id = lax.axis_index("fsdp")
    token_total = jnp.sum(token_counts).astype(jnp.float32)
    valid_limit = jnp.sum(jnp.where(lax.iota(jnp.int32, group_count) == group_id, token_counts, 0))
    positions = shard_id * tok_dev + lax.iota(jnp.int32, tok_dev)
    row_keep = (positions < valid_limit).astype(jnp.bfloat16)[:, None]
    masked_acts = acts * row_keep
    masked_grads = out_grads * row_keep
    block_ids = shard_id * blocks_dev + lax.iota(jnp.int32, blocks_dev)
    border_keep = (block_ids > 0).astype(jnp.float32)[:, None, None]
    lead_k, lead_c = (
        spread(k_factor[0, :, :block_size], "fsdp", 0),
        spread(c_factor[0, :, :block_size], "fsdp", 0),
    )
    raw_acts, raw_grads = to_owners((masked_acts, masked_grads))
    lead_raw_acts, lead_raw_grads = fetch_lead(
        (masked_acts[:, :block_size], masked_grads[:, :block_size])
    )
    k_diag_half = k_factor[:, :, :block_size].astype(jnp.bfloat16)
    k_side_half = (k_factor[:, :, block_size:] * border_keep).astype(jnp.bfloat16)
    c_diag_half = c_factor[:, :, :block_size].astype(jnp.bfloat16)
    c_side_half = (c_factor[:, :, block_size:] * border_keep).astype(jnp.bfloat16)
    owned_acts = owner_image(raw_acts, lead_raw_acts, k_diag_half, k_side_half)
    owned_grads = owner_image(raw_grads, lead_raw_grads, c_diag_half, c_side_half)
    lead_acts = jnp.dot(
        lead_raw_acts, lead_k.astype(jnp.bfloat16), preferred_element_type=jnp.float32
    ).astype(jnp.bfloat16)
    lead_grads = jnp.dot(
        lead_raw_grads, lead_c.astype(jnp.bfloat16), preferred_element_type=jnp.float32
    ).astype(jnp.bfloat16)
    own_k, cross_k = block_stats(owned_acts, lead_acts, blocks_dev, block_size)
    own_c, cross_c = block_stats(owned_grads, lead_grads, blocks_dev, block_size)
    summed = lax.psum((own_k, cross_k, own_c, cross_c), "dp")
    gram_k = gram_trace(k_factor, border_keep)
    gram_c = gram_trace(c_factor, border_keep)
    local_traces = jnp.stack(
        [
            jnp.sum(jnp.trace(summed[0], axis1=1, axis2=2)),
            jnp.sum(jnp.trace(summed[2], axis1=1, axis2=2)),
            gram_k,
            gram_c,
        ]
    )
    totals = lax.psum(local_traces, "fsdp")
    trace_hk = totals[0] / token_total
    trace_hc = totals[1] / token_total
    scale_width = float(width)
    k_factor_new, k_moment_new = advance(
        k_factor,
        k_moment,
        summed[0] / token_total,
        summed[1] / token_total,
        lead_k,
        border_keep,
        trace_hc,
        totals[3],
        scale_width,
    )
    c_factor_new, c_moment_new = advance(
        c_factor,
        c_moment,
        summed[2] / token_total,
        summed[3] / token_total,
        lead_c,
        border_keep,
        trace_hk,
        totals[2],
        scale_width,
    )
    grad_rows = grad_weight.shape[0]
    grad_lead = spread(grad_weight[:, :block_size], "fsdp", 0)
    k_diag = k_factor_new[:, :, :block_size].astype(jnp.bfloat16)
    k_side = k_factor_new[:, :, block_size:].astype(jnp.bfloat16)
    grad_blocked = grad_weight.reshape(grad_rows, blocks_dev, block_size)
    first_sum = jnp.einsum("rnk,nkj->rnj", grad_blocked, k_diag, preferred_element_type=jnp.float32)
    first_sum = first_sum + jnp.einsum(
        "rk,nkj->rnj", grad_lead, k_side, preferred_element_type=jnp.float32
    )
    first_product = first_sum.astype(jnp.bfloat16)
    own_second = jnp.einsum(
        "rnk,njk->rnj", first_product, k_diag, preferred_element_type=jnp.float32
    )
    lead_term = jnp.einsum("rnk,njk->rj", first_product, k_side, preferred_element_type=jnp.float32)
    lead_sum = lax.psum(lead_term, "fsdp")
    lead_mask = (block_ids == 0).astype(jnp.float32)[None, :, None]
    second_product = (own_second + lead_mask * lead_sum[:, None, :]).astype(jnp.bfloat16)
    row_blocks = grad_rows // block_size
    owner_count = shard_count // group_count
    c_half = c_factor_new.astype(jnp.bfloat16)
    fetched = []
    for owner_step in range(owner_count):
        fetched.append(spread(c_half, "fsdp", group_id * owner_count + owner_step))
    row_factor = jnp.concatenate(fetched, axis=0)
    c_diag = row_factor[:, :, :block_size]
    c_side = row_factor[:, :, block_size:]
    by_rows = second_product.reshape(row_blocks, block_size, blocks_dev * block_size)
    lead_rows = spread(by_rows[0], "dp", 0)
    third_sum = jnp.einsum("nki,nkc->nic", c_diag, by_rows, preferred_element_type=jnp.float32)
    third_sum = third_sum + jnp.einsum(
        "nki,kc->nic", c_side, lead_rows, preferred_element_type=jnp.float32
    )
    third_product = third_sum.astype(jnp.bfloat16)
    own_fourth = jnp.einsum(
        "nik,nkc->nic", c_diag, third_product, preferred_element_type=jnp.float32
    )
    row_term = jnp.einsum("nik,nkc->ic", c_side, third_product, preferred_element_type=jnp.float32)
    row_sum = lax.psum(row_term, "dp")
    row_ids = group_id * row_blocks + lax.iota(jnp.int32, row_blocks)
    row_mask = (row_ids == 0).astype(jnp.float32)[:, None, None]
    precond = (
        (own_fourth + row_mask * row_sum[None, :, :])
        .astype(jnp.bfloat16)
        .reshape(grad_rows, blocks_dev * block_size)
    )
    return (k_factor_new, c_factor_new, k_moment_new, c_moment_new, precond)


def per_device(*args):
    blocks = args[3].shape[0]
    groups, shards = lax.axis_size("dp"), lax.axis_size("fsdp")
    fits = blocks == 4 and groups == 4 and shards == 8
    return (planned if fits else general)(*args)


def solution(mesh):
    in_specs = (
        P(("dp", "fsdp"), None),
        P(("dp", "fsdp"), None),
        P(),
        P("fsdp", None, None),
        P("fsdp", None, None),
        P("fsdp", None, None),
        P("fsdp", None, None),
        P("dp", "fsdp"),
    )
    out_specs = (
        P("fsdp", None, None),
        P("fsdp", None, None),
        P("fsdp", None, None),
        P("fsdp", None, None),
        P("dp", "fsdp"),
    )
    return jax.shard_map(
        per_device, mesh=mesh, in_specs=in_specs, out_specs=out_specs, check_vma=False
    )
```
